32 devices in a mesh: sub: 16 (over z, y, core), row: 2 (over x).
Axes of the slice: x: 2, y: 2, z: 4, core: 2. Of those that a mesh axis runs over, the one named last changes fastest.
Arguments:
- compliance: bfloat16 [16, 36, 18, 128, 128], P('sub', 'row'), may hold values from -0.0625 to 0.0625
- block_columns: int32 [16, 36, 18], P('sub', 'row'), may hold values from 0 to 35, as said below
- load_response: bfloat16 [16, 32, 4608], P('sub', None, 'row'), may hold values from -6 to 6
- starting_motion: bfloat16 [16, 32, 4608], P('sub', None, 'row'), may hold values from -6 to 6
- start_traction: bfloat16 [16, 32, 4608], P('sub', None, 'row'), may hold values from -6 to 6
- stiffness: float32 [16, 4608], P('sub', 'row'), may hold values from 1 to 10
- history: float32 [16, 4608], P('sub', 'row'), may hold values from 0 to 0.6
- face_partner: int32 [16, 36], P('sub', 'row'), may hold values from -1 to 8, as said below
- orientation: int32 [16, 36, 128], P('sub', 'row'), may hold values from 0 to 127, as said below
Outputs:
- displacement: bfloat16 [16, 32, 4608], P('sub', None, 'row')
- traction: bfloat16 [16, 32, 4608], P('sub', None, 'row')
The draws below stay inside these ranges and needn't reach their ends.
Inputs may be any that keep to these rules, and one draw needn't show every extreme that they name: `block_columns`: each block row names 18 distinct face columns. `face_partner`: an entry is -1 for a free face, else the position, within the facing group of the same run of the neighbouring substructure, of the matched face. Matches are mutual. Faces facing s+1 on the last substructure and faces facing s-1 on the first are free. In some run of some substructure all 9 faces facing s+1 are matched. `orientation`: each face's row is a permutation of 0 to 127; matched faces carry mutually inverse permutations.
All inputs are finite; a program needn't handle non-finite values.
Results may differ from the reference program's by a relative error of at most 0.0045.
The reference program's roundings to bfloat16 on the way count: a program that leaves them out, or rounds other values in their place, can miss the bound.
Values may be sent and summed in bfloat16 or wider, within the bound.
No kernel may reach another device: no remote copies, remote signals or barrier semaphores. Data moves between devices by JAX's collectives and lax.ppermute only.
A program may use at most 64 MiB of HBM per device.

```python
import math
import jax
import jax.numpy as jnp
from jax import lax

ORDER = 4608
SURFACE_EXTENT = 128
NNZB = 18
TIMES = 32
ITERS = 3
SUBS = 16
FACES = 36
GROUP = 9
N_ROW = 2


def shuffled(subkey, length):
    return jax.random.permutation(subkey, length).astype(jnp.int32)


def matching(key):
    halves = FACES // (2 * GROUP)
    keys = jax.random.split(key, 6)
    pairs = SUBS * halves
    choose = jax.random.randint(keys[0], (SUBS, halves), 0, 4)
    sparse = jax.random.randint(keys[1], (SUBS, halves), 0, GROUP // 3 + 1)
    counts = jnp.where(choose == 0, GROUP, sparse)
    busiest = jax.random.randint(keys[2], (), 0, max(SUBS - 1, 1))
    sub_ids = jnp.arange(SUBS)[:, None]
    counts = jnp.where(sub_ids == busiest, GROUP, counts)
    counts = jnp.where(sub_ids == SUBS - 1, 0, counts)
    perm_top = jax.vmap(lambda subkey: shuffled(subkey, GROUP))(jax.random.split(keys[3], pairs)).reshape(SUBS, halves, GROUP)
    perm_bottom = jax.vmap(lambda subkey: shuffled(subkey, GROUP))(jax.random.split(keys[4], pairs)).reshape(SUBS, halves, GROUP)
    inverse_top = jnp.argsort(perm_top, axis=-1).astype(jnp.int32)
    inverse_bottom = jnp.argsort(perm_bottom, axis=-1).astype(jnp.int32)
    top_entry = jnp.where(inverse_top < counts[..., None], jnp.take_along_axis(perm_bottom, inverse_top, axis=-1), -1)
    bottom_next = jnp.where(inverse_bottom < counts[..., None], jnp.take_along_axis(perm_top, inverse_bottom, axis=-1), -1)
    bottom_entry = jnp.concatenate([jnp.full((1, halves, GROUP), -1, jnp.int32), bottom_next[:-1]], axis=0)
    partner_table = jnp.concatenate([top_entry, bottom_entry], axis=2).reshape(SUBS, FACES)
    turns = jax.vmap(lambda subkey: shuffled(subkey, SURFACE_EXTENT))(jax.random.split(keys[5], pairs * GROUP)).reshape(SUBS, halves, GROUP, SURFACE_EXTENT)
    top_turn = jnp.take_along_axis(turns, jnp.broadcast_to(inverse_top[..., None], turns.shape), axis=2)
    bottom_pair = jnp.take_along_axis(turns, jnp.broadcast_to(inverse_bottom[..., None], turns.shape), axis=2)
    bottom_next_turn = jnp.argsort(bottom_pair, axis=-1).astype(jnp.int32)
    bottom_turn = jnp.concatenate([turns[:1], bottom_next_turn[:-1]], axis=0)
    turning = jnp.concatenate([top_turn, bottom_turn], axis=2).reshape(SUBS, FACES, SURFACE_EXTENT)
    return (partner_table.astype(jnp.int32), turning.astype(jnp.int32))


def draw_face_partner(key, part):
    return matching(jax.random.fold_in(key, 11))[0]


def draw_orientation(key, part):
    return matching(jax.random.fold_in(key, 11))[1]


def draw_block_columns(key, part):
    keys = jax.random.split(jax.random.fold_in(key, 5), SUBS * FACES)
    picked = jax.vmap(lambda subkey: shuffled(subkey, FACES)[:NNZB])(keys)
    return picked.reshape(SUBS, FACES, NNZB).astype(jnp.int32)


def levels(key, shape, pieces, least, largest):
    def one(dim, parts):
        steps = jax.random.uniform(jax.random.fold_in(jax.random.fold_in(key, 6), dim), (parts,), jnp.float32, least / len(pieces), largest / len(pieces))
        return jnp.repeat(jnp.exp(steps), shape[dim] // parts).reshape((-1,) + (1,) * (len(shape) - dim - 1))

    gain = one(*pieces[0])
    for cut in pieces[1:]:
        gain = gain * one(*cut)
    return gain


def bell_draw(rng, dims, spread, most, shards=(), kind=jnp.bfloat16):
    array = spread * jax.random.normal(rng, dims, jnp.float32)
    if shards:
        array = array * levels(rng, dims, shards, -0.22, 0.18)
    return jnp.clip(array, -most, most).astype(kind)


def setup_inputs(seed: int = 0) -> dict:
    arg_keys = jax.random.split(jax.random.key(seed), 10)
    return {
        "compliance": bell_draw(arg_keys[0], (SUBS, FACES, NNZB, SURFACE_EXTENT, SURFACE_EXTENT), (4 * SURFACE_EXTENT * NNZB) ** -0.5, 0.0625, ((0, 16), (1, 2))),
        "block_columns": draw_block_columns(jax.random.fold_in(arg_keys[9], 71), 0),
        "load_response": bell_draw(arg_keys[2], (SUBS, TIMES, ORDER), 1.0, 6.0, ((0, 16), (2, 2))),
        "starting_motion": bell_draw(arg_keys[3], (SUBS, TIMES, ORDER), 1.0, 6.0, ((0, 16), (2, 2))),
        "start_traction": bell_draw(arg_keys[4], (SUBS, TIMES, ORDER), 1.0, 6.0, ((0, 16), (2, 2))),
        "stiffness": jnp.clip(jnp.exp(math.log(10.0) - 2.3025851 * jax.random.uniform(arg_keys[5], (SUBS, ORDER), jnp.float32) ** levels(arg_keys[5], (SUBS, ORDER), ((0, 16), (1, 2)), -0.2, 0.2)), 1.0, 10.0),
        "history": jnp.clip(0.6 * jax.random.uniform(arg_keys[6], (SUBS, ORDER), jnp.float32) ** levels(arg_keys[6], (SUBS, ORDER), ((0, 16), (1, 2)), -0.2, 0.2), 0.0, 0.6),
        "face_partner": draw_face_partner(jax.random.fold_in(arg_keys[9], 71), 0),
        "orientation": draw_orientation(jax.random.fold_in(arg_keys[9], 71), 0),
    }


search_stiffness = 1.0
onset_jump = 0.15
failure_jump = 1.5


def cohesive(upward_marker, constitutive_parameters, opposing_surface, live_mask):
    temporal_points = upward_marker.shape[0]
    mate_upward_marker = opposing_surface[:temporal_points]
    joint_rigidity = 0.5 * (constitutive_parameters[0] + opposing_surface[temporal_points])
    joint_record = jnp.maximum(constitutive_parameters[1], opposing_surface[temporal_points + 1])
    difference = upward_marker - mate_upward_marker
    jump_size = difference / (search_stiffness + 2.0 * joint_rigidity)
    peak_jump = jnp.maximum(joint_record, lax.cummax(jnp.abs(jump_size), axis=0))
    damage = jnp.clip((peak_jump - onset_jump) / (failure_jump - onset_jump), 0.0, 1.0)
    effective = joint_rigidity * (1.0 - damage)
    traction = jnp.where(live_mask, effective * difference / (search_stiffness + 2.0 * effective), 0.0)
    displacement = (traction - upward_marker) / search_stiffness
    return displacement, traction


def reference(compliance, block_columns, load_response, starting_motion, start_traction, stiffness, history, face_partner, orientation):
    constitutive_parameters = jnp.stack([stiffness, history], axis=1).reshape(SUBS, 2, FACES, SURFACE_EXTENT)
    face_ids = jnp.arange(FACES, dtype=jnp.int32)
    within = face_ids % (FACES // N_ROW)
    run_start = face_ids - within
    facing_up = within < GROUP
    present_motion = starting_motion.astype(jnp.float32)
    present_stress = start_traction.astype(jnp.float32)

    def linear_section(operands):
        compliance_sub, columns, load_sub, disp_sub, trac_sub = operands
        robin_sum = trac_sub + search_stiffness * disp_sub
        flexibility_tiles = robin_sum.astype(jnp.bfloat16).reshape(TIMES, FACES, SURFACE_EXTENT)
        picked = jnp.take(flexibility_tiles, columns.astype(jnp.int32), axis=1).astype(jnp.float32)
        operator_multiply = jnp.einsum("tijb,ijab->tia", picked, compliance_sub.astype(jnp.float32))
        proportional_reaction = operator_multiply.reshape(TIMES, ORDER) + load_sub.astype(jnp.float32)
        return robin_sum - 2.0 * search_stiffness * proportional_reaction

    for iteration in range(ITERS):
        ascent_all = lax.map(linear_section, (compliance, block_columns, load_response, present_motion, present_stress))
        payload_all = jnp.concatenate([ascent_all.reshape(SUBS, TIMES, FACES, SURFACE_EXTENT), constitutive_parameters], axis=1)

        def local_section(sub_index):
            upper_payload = lax.dynamic_index_in_dim(payload_all, jnp.minimum(sub_index + 1, SUBS - 1), 0, keepdims=False)
            lower_payload = lax.dynamic_index_in_dim(payload_all, jnp.maximum(sub_index - 1, 0), 0, keepdims=False)
            own_payload = lax.dynamic_index_in_dim(payload_all, sub_index, 0, keepdims=False)
            partner_table = lax.dynamic_index_in_dim(face_partner, sub_index, 0, keepdims=False)
            turning = lax.dynamic_index_in_dim(orientation, sub_index, 0, keepdims=False)
            live_mask = (partner_table >= 0)[:, None]
            safe_index = jnp.maximum(partner_table, 0)
            source = jnp.where(facing_up, run_start + GROUP + safe_index, run_start + safe_index).astype(jnp.int32)
            chosen = jnp.where(facing_up[None, :, None], jnp.take(upper_payload, source, axis=1), jnp.take(lower_payload, source, axis=1))
            opposing_surface = jnp.take_along_axis(chosen, jnp.broadcast_to(turning[None], chosen.shape).astype(jnp.int32), axis=2)
            motion_distribution, stress_distribution = cohesive(own_payload[:TIMES], own_payload[TIMES:], opposing_surface, live_mask)
            return motion_distribution.reshape(TIMES, ORDER), stress_distribution.reshape(TIMES, ORDER)

        present_motion, present_stress = lax.map(local_section, jnp.arange(SUBS, dtype=jnp.int32))
    return present_motion.astype(jnp.bfloat16), present_stress.astype(jnp.bfloat16)
```

```python
import functools

import jax
import jax.numpy as jnp
from jax import lax
from jax.experimental import pallas as pl
from jax.experimental.pallas import tpu as pltpu
from jax.sharding import PartitionSpec as P

ITERS = 3
SUBLANES = 8
VMEM_BYTES = 24 * 2**20

ONSET_JUMP = 0.15
FAILURE_JUMP = 1.5

VMEM = pl.BlockSpec(memory_space=pltpu.VMEM)
SMEM = pl.BlockSpec(memory_space=pltpu.SMEM)


def first_robin(motion_ref, stress_ref, load_ref, turn_ref, stiff_ref, record_ref,
                robin_ref, half_ref, load_faces_ref, turn_out_ref, stiff_out_ref, record_out_ref):
    faces, _, extent = robin_ref.shape
    for face in range(faces):
        lanes = slice(face * extent, (face + 1) * extent)
        robin = stress_ref[:, lanes].astype(jnp.float32) + motion_ref[:, lanes].astype(jnp.float32)
        robin_ref[face] = robin
        half_ref[face] = robin.astype(jnp.bfloat16)
        load_faces_ref[face] = load_ref[:, lanes]
    turn_out_ref[...] = turn_ref[...]
    stiff_out_ref[...] = stiff_ref[...]
    record_out_ref[...] = record_ref[...]


def linear_section(side, columns_ref, place_ref, compliance_ref, own_ref, other_ref, robin_ref, load_ref,
                   stiff_ref, record_ref, out_ref, half_ref):
    group, rows, _ = out_ref.shape
    faces, times, _ = own_ref.shape
    stored = compliance_ref.shape[1]
    first, mine = place_ref[side], place_ref[2]
    half_ref[pl.ds(mine * faces, faces)] = own_ref[...]
    half_ref[pl.ds((1 - mine) * faces, faces)] = other_ref[...]
    for index in range(group):
        face = first + index
        picked = jnp.concatenate([half_ref[columns_ref[face, j]] for j in range(stored)], axis=1)
        blocks = jnp.concatenate([compliance_ref[face, j] for j in range(stored)], axis=1)
        response = lax.dot_general(
            picked, blocks, (((1,), (1,)), ((), ())), preferred_element_type=jnp.float32
        ) + load_ref[face].astype(jnp.float32)
        out_ref[index, :times] = robin_ref[face] - 2.0 * response
        if rows > times:
            out_ref[index, times : times + 1] = stiff_ref[pl.ds(face, 1), :]
            out_ref[index, times + 1 : times + 2] = record_ref[pl.ds(face, 1), :]
            out_ref[index, times + 2 :] = jnp.zeros_like(out_ref[index, times + 2 :])


def running_peak(sizes):
    row = lax.broadcasted_iota(jnp.int32, sizes.shape, 0)
    step = 1
    while step < sizes.shape[0]:
        earlier = pltpu.roll(sizes, step, 0)
        sizes = jnp.maximum(sizes, jnp.where(row >= step, earlier, 0.0))
        step *= 2
    return sizes


def local_section(begin, last, place_ref, partner_ref, turn_ref, own0_ref, own1_ref, mate0_ref, mate1_ref,
                  stiff_ref, record_ref, first_ref, second_ref, *pair_refs):
    group = own0_ref.shape[0]
    times, extent = first_ref.shape[0] if last else first_ref.shape[1], turn_ref.shape[1]
    gather = functools.partial(jnp.take_along_axis, axis=1, mode="promise_in_bounds")
    for side, (own_ref, mate_ref) in enumerate(((own0_ref, mate0_ref), (own1_ref, mate1_ref))):
        for index in range(group):
            face = place_ref[side] + index
            partner = partner_ref[face]
            mate = jnp.maximum(partner, 0)
            turn = turn_ref[pl.ds(face, 1), :]
            ascent = own_ref[index, :times]
            mate_ascent = gather(mate_ref[mate, :times], jnp.broadcast_to(turn, (times, extent)))
            stiffness = stiff_ref[pl.ds(face, 1), :]
            record = record_ref[pl.ds(face, 1), :]
            if begin:
                constants = gather(mate_ref[mate, times:], jnp.broadcast_to(turn, (SUBLANES, extent)))
                stiffness = 0.5 * (stiffness + constants[:1])
                record = jnp.maximum(record, constants[1:2])
                pair_refs[0][pl.ds(face, 1), :] = stiffness
                pair_refs[1][pl.ds(face, 1), :] = record
            difference = ascent - mate_ascent
            jump = difference / (1.0 + 2.0 * stiffness)
            peak = jnp.maximum(record, running_peak(jnp.abs(jump)))
            damage = jnp.clip((peak - ONSET_JUMP) / (FAILURE_JUMP - ONSET_JUMP), 0.0, 1.0)
            effective = stiffness * (1.0 - damage)
            traction = jnp.where(partner >= 0, effective * difference / (1.0 + 2.0 * effective), 0.0)
            motion = traction - ascent
            if last:
                lanes = pl.ds(pl.multiple_of(face * extent, extent), extent)
                first_ref[:, lanes] = motion.astype(jnp.bfloat16)
                second_ref[:, lanes] = traction.astype(jnp.bfloat16)
            else:
                robin = traction + motion
                first_ref[face] = robin
                second_ref[face] = robin.astype(jnp.bfloat16)


def shards(
    compliance,
    block_columns,
    load_response,
    starting_motion,
    start_traction,
    stiffness,
    history,
    face_partner,
    orientation,
):
    _, faces, stored, extent, _ = compliance.shape
    times = starting_motion.shape[1]
    group = faces // 2
    subs = lax.axis_size("sub")
    rows = lax.axis_size("row")
    near = group * (lax.axis_index("sub") % 2)
    place = jnp.stack([near, group - near, lax.axis_index("row")]).astype(jnp.int32)
    near_pairs = [(s, s ^ 1) for s in range(subs) if s ^ 1 < subs]
    far_pairs = [(s, t) for s in range(subs) for t in [s - 1 if s % 2 == 0 else s + 1] if 0 <= t < subs]
    swap = [(r, rows - 1 - r) for r in range(rows)]
    params = pltpu.CompilerParams(vmem_limit_bytes=VMEM_BYTES)

    compliance = pltpu.with_memory_space_constraint(compliance[0], pltpu.VMEM)
    columns = block_columns[0]
    partner = face_partner[0]

    def f32(*shape):
        return jax.ShapeDtypeStruct(shape, jnp.float32)

    def bf16(*shape):
        return jax.ShapeDtypeStruct(shape, jnp.bfloat16)

    tall = (faces, times, extent)
    robin, half, load, turn, stiff, record = pl.pallas_call(
        first_robin,
        out_shape=(
            f32(*tall), bf16(*tall), bf16(*tall),
            jax.ShapeDtypeStruct((faces, extent), jnp.int32), f32(faces, extent), f32(faces, extent),
        ),
        in_specs=[VMEM] * 6,
        out_specs=(VMEM,) * 6,
        compiler_params=params,
    )(
        starting_motion[0], start_traction[0], load_response[0], orientation[0],
        stiffness.reshape(faces, extent), history.reshape(faces, extent),
    )

    def ascent_of(side, begin, other):
        return pl.pallas_call(
            functools.partial(linear_section, side),
            out_shape=f32(group, times + SUBLANES if begin else times, extent),
            in_specs=[SMEM, SMEM] + [VMEM] * 7,
            out_specs=VMEM,
            scratch_shapes=[pltpu.VMEM((rows * faces, times, extent), jnp.bfloat16)],
            compiler_params=params,
        )(columns, place, compliance, half, other, robin, load, stiff, record)

    for iteration in range(ITERS):
        begin, last = iteration == 0, iteration == ITERS - 1
        other = lax.ppermute(half, "row", swap)
        ascent_far = ascent_of(1, begin, other)
        mates_far = lax.ppermute(ascent_far, "sub", far_pairs)
        ascent_near = ascent_of(0, begin, other)
        mates_near = lax.ppermute(ascent_near, "sub", near_pairs)
        outs = (bf16(times, faces * extent),) * 2 if last else (f32(*tall), bf16(*tall))
        if begin:
            outs += (f32(faces, extent),) * 2
        robin, half, *pair = pl.pallas_call(
            functools.partial(local_section, begin, last),
            out_shape=outs,
            in_specs=[SMEM, SMEM] + [VMEM] * 7,
            out_specs=(VMEM,) * len(outs),
            compiler_params=params,
        )(place, partner, turn, ascent_near, ascent_far, mates_near, mates_far, stiff, record)
        if begin:
            stiff, record = pair
    return robin[None], half[None]


def solution(mesh):
    in_specs = (
        P("sub", "row", None, None, None),
        P("sub", "row", None),
        P("sub", None, "row"),
        P("sub", None, "row"),
        P("sub", None, "row"),
        P("sub", "row"),
        P("sub", "row"),
        P("sub", "row"),
        P("sub", "row", None),
    )
    out_specs = (P("sub", None, "row"), P("sub", None, "row"))
    return jax.shard_map(shards, mesh=mesh, in_specs=in_specs, out_specs=out_specs, check_vma=False)
```

```python
import functools

import jax
import jax.numpy as jnp
from jax import lax
from jax.experimental import pallas as pl
from jax.experimental.pallas import tpu as pltpu
from jax.sharding import PartitionSpec as P

ITERS = 3
SUBLANES = 8
VMEM_BYTES = 24 * 2**20

ONSET_JUMP = 0.15
FAILURE_JUMP = 1.5

VMEM = pl.BlockSpec(memory_space=pltpu.VMEM)
SMEM = pl.BlockSpec(memory_space=pltpu.SMEM)
ANY = pl.BlockSpec(memory_space=pl.ANY)


def position(group):
    near = group * (lax.axis_index("sub") % 2)
    return near, group - near, lax.axis_index("row")


def first_robin(motion_hbm, stress_hbm, robin_ref, half_ref, motion_ref, stress_ref, sems):
    copies = [
        pltpu.make_async_copy(motion_hbm, motion_ref, sems.at[0]),
        pltpu.make_async_copy(stress_hbm, stress_ref, sems.at[1]),
    ]
    for copy in copies:
        copy.start()
    for copy in copies:
        copy.wait()
    faces, _, extent = robin_ref.shape
    for face in range(faces):
        lanes = slice(face * extent, (face + 1) * extent)
        robin = stress_ref[:, lanes].astype(jnp.float32) + motion_ref[:, lanes].astype(jnp.float32)
        robin_ref[face] = robin
        half_ref[face] = robin.astype(jnp.bfloat16)


def block_products(parts):
    times, extent = parts[0][0][0].shape
    zero = jnp.zeros_like(parts[0][0][1])
    depth = max(len(part) for part in parts)
    parts = [part + [(part[0][0], zero)] * (depth - len(part)) for part in parts]
    values = jnp.concatenate([jnp.concatenate([v for v, _ in part], axis=1) for part in parts], axis=0)
    blocks = jnp.concatenate([jnp.concatenate([c for _, c in part], axis=1) for part in parts], axis=0)
    product = lax.dot_general(values, blocks, (((1,), (1,)), ((), ())), preferred_element_type=jnp.float32)
    return [
        product[p * times : (p + 1) * times, p * extent : (p + 1) * extent] for p in range(len(parts))
    ]


def linear_section(side, columns_ref, compliance_ref, own_ref, other_ref, robin_ref, load_ref,
                   stiff_ref, record_ref, *refs):
    out_ref, half_ref = refs[-2:]
    group, rows, extent = out_ref.shape
    faces, times, _ = own_ref.shape
    stored = compliance_ref.shape[1]
    *starts, mine = position(group)
    first = starts[side]
    half_ref[pl.ds(mine * faces, faces)] = own_ref[...]
    half_ref[pl.ds((1 - mine) * faces, faces)] = other_ref[...]

    def entries(face, begin, end):
        return [(half_ref[columns_ref[face, 0, j]], compliance_ref[face, j]) for j in range(begin, end)]

    def finish(index, product):
        face = first + index
        lanes = pl.ds(pl.multiple_of(face * extent, extent), extent)
        response = product + load_ref[:, lanes].astype(jnp.float32)
        out_ref[index, :times] = robin_ref[face] - 2.0 * response
        if rows > times:
            out_ref[index, times : times + 1] = stiff_ref[:, lanes]
            out_ref[index, times + 1 : times + 2] = record_ref[:, lanes]
            out_ref[index, times + 2 :] = jnp.zeros_like(out_ref[index, times + 2 :])

    for index in range(0, group - 1, 2):
        pair = block_products([entries(first + index + k, 0, stored) for k in range(2)])
        for k in range(2):
            finish(index + k, pair[k])
    if group % 2:
        face = first + group - 1
        cut = (stored + 3) // 4 * 2
        finish(group - 1, sum(block_products([entries(face, 0, cut), entries(face, cut, stored)])))


def running_peak(sizes):
    row = lax.broadcasted_iota(jnp.int32, sizes.shape, 0)
    step = 1
    while step < sizes.shape[0]:
        earlier = pltpu.roll(sizes, step, 0)
        sizes = jnp.maximum(sizes, jnp.where(row >= step, earlier, 0.0))
        step *= 2
    return sizes


def local_section(begin, last, partner_ref, turn_ref, own0_ref, own1_ref, mate0_ref, mate1_ref,
                  stiff_ref, record_ref, first_ref, second_ref, *pair_refs):
    group = own0_ref.shape[0]
    extent = own0_ref.shape[2]
    times = first_ref.shape[0] if last else first_ref.shape[1]
    starts = position(group)
    gather = functools.partial(jnp.take_along_axis, axis=1, mode="promise_in_bounds")
    for side, (own_ref, mate_ref) in enumerate(((own0_ref, mate0_ref), (own1_ref, mate1_ref))):
        for index in range(group):
            face = starts[side] + index
            lanes = pl.ds(pl.multiple_of(face * extent, extent), extent)
            partner = partner_ref[0, face]
            mate = jnp.maximum(partner, 0)
            turn = turn_ref[:, lanes]
            ascent = own_ref[index, :times]
            mate_ascent = gather(mate_ref[mate, :times], jnp.broadcast_to(turn, (times, extent)))
            stiffness = stiff_ref[:, lanes]
            record = record_ref[:, lanes]
            if begin:
                constants = gather(mate_ref[mate, times:], jnp.broadcast_to(turn, (SUBLANES, extent)))
                stiffness = 0.5 * (stiffness + constants[:1])
                record = jnp.maximum(record, constants[1:2])
                pair_refs[0][:, lanes] = stiffness
                pair_refs[1][:, lanes] = record
            difference = ascent - mate_ascent
            jump = difference / (1.0 + 2.0 * stiffness)
            peak = jnp.maximum(record, running_peak(jnp.abs(jump)))
            damage = jnp.clip((peak - ONSET_JUMP) / (FAILURE_JUMP - ONSET_JUMP), 0.0, 1.0)
            effective = stiffness * (1.0 - damage)
            traction = jnp.where(partner >= 0, effective * difference / (1.0 + 2.0 * effective), 0.0)
            motion = traction - ascent
            if last:
                first_ref[:, lanes] = motion.astype(jnp.bfloat16)
                second_ref[:, lanes] = traction.astype(jnp.bfloat16)
            else:
                robin = traction + motion
                first_ref[face] = robin
                second_ref[face] = robin.astype(jnp.bfloat16)


def shards(
    compliance,
    block_columns,
    load_response,
    starting_motion,
    start_traction,
    stiffness,
    history,
    face_partner,
    orientation,
):
    _, faces, stored, extent, _ = compliance.shape
    times = starting_motion.shape[1]
    group = faces // 2
    subs = lax.axis_size("sub")
    rows = lax.axis_size("row")
    near_pairs = [(s, s ^ 1) for s in range(subs) if s ^ 1 < subs]
    far_pairs = [(s, t) for s in range(subs) for t in [s - 1 if s % 2 == 0 else s + 1] if 0 <= t < subs]
    swap = [(r, rows - 1 - r) for r in range(rows)]
    params = pltpu.CompilerParams(vmem_limit_bytes=VMEM_BYTES)

    compliance = pltpu.with_memory_space_constraint(compliance[0], pltpu.VMEM)
    columns = jnp.transpose(block_columns, (1, 0, 2))
    turn = orientation.reshape(1, -1)
    load = load_response[0]

    def f32(*shape):
        return jax.ShapeDtypeStruct(shape, jnp.float32)

    def bf16(*shape):
        return jax.ShapeDtypeStruct(shape, jnp.bfloat16)

    tall = (faces, times, extent)
    flat = (times, faces * extent)
    robin, half = pl.pallas_call(
        first_robin,
        out_shape=(f32(*tall), bf16(*tall)),
        in_specs=[ANY] * 2,
        out_specs=(VMEM,) * 2,
        scratch_shapes=[
            pltpu.VMEM(flat, jnp.bfloat16), pltpu.VMEM(flat, jnp.bfloat16), pltpu.SemaphoreType.DMA((2,)),
        ],
        compiler_params=params,
    )(starting_motion[0], start_traction[0])

    def ascent_of(side, begin, other, after=()):
        return pl.pallas_call(
            functools.partial(linear_section, side),
            out_shape=f32(group, times + SUBLANES if begin else times, extent),
            in_specs=[SMEM] + [VMEM] * 7 + [ANY] * len(after),
            out_specs=VMEM,
            scratch_shapes=[pltpu.VMEM((rows * faces, times, extent), jnp.bfloat16)],
            compiler_params=params,
        )(columns, compliance, half, other, robin, load, stiffness, history, *after)

    stiff, record = stiffness, history
    for iteration in range(ITERS):
        begin, last = iteration == 0, iteration == ITERS - 1
        other = lax.ppermute(half, "row", swap)
        ascent_far = ascent_of(1, begin, other)
        mates_far = lax.ppermute(ascent_far, "sub", far_pairs)
        ascent_near = ascent_of(0, begin, other, (ascent_far,))
        mates_near = lax.ppermute(ascent_near, "sub", near_pairs)
        outs = (bf16(*flat),) * 2 if last else (f32(*tall), bf16(*tall))
        if begin:
            outs += (f32(1, faces * extent),) * 2
        robin, half, *pair = pl.pallas_call(
            functools.partial(local_section, begin, last),
            out_shape=outs,
            in_specs=[SMEM] + [VMEM] * 7,
            out_specs=(VMEM,) * len(outs),
            compiler_params=params,
        )(face_partner, turn, ascent_near, ascent_far, mates_near, mates_far, stiff, record)
        if begin:
            stiff, record = pair
    return robin[None], half[None]


def solution(mesh):
    in_specs = (
        P("sub", "row", None, None, None),
        P("sub", "row", None),
        P("sub", None, "row"),
        P("sub", None, "row"),
        P("sub", None, "row"),
        P("sub", "row"),
        P("sub", "row"),
        P("sub", "row"),
        P("sub", "row", None),
    )
    out_specs = (P("sub", None, "row"), P("sub", None, "row"))
    return jax.shard_map(shards, mesh=mesh, in_specs=in_specs, out_specs=out_specs, check_vma=False)
```

```python
import functools

import jax
import jax.numpy as jnp
from jax import lax
from jax.experimental import pallas as pl
from jax.experimental.pallas import tpu as pltpu
from jax.sharding import PartitionSpec as P

ITERS = 3
SUBLANES = 8
VMEM_BYTES = 24 * 2**20

ONSET_JUMP = 0.15
FAILURE_JUMP = 1.5

VMEM = pl.BlockSpec(memory_space=pltpu.VMEM)
SMEM = pl.BlockSpec(memory_space=pltpu.SMEM)
ANY = pl.BlockSpec(memory_space=pl.ANY)


def position(group):
    near = group * (lax.axis_index("sub") % 2)
    return near, group - near, lax.axis_index("row")


def lanes_of(face, extent):
    return pl.ds(pl.multiple_of(face * extent, extent), extent)


def prepare(motion_hbm, stress_hbm, load_hbm, stiff_hbm, record_hbm, turn_hbm, columns_hbm, partner_hbm,
            robin0_ref, robin1_ref, half0_ref, half1_ref, load_ref, stiff_ref, record_ref, turn_ref, columns_ref, partner_ref,
            motion_ref, stress_ref, sems):
    pairs = (
        (motion_hbm, motion_ref), (stress_hbm, stress_ref), (load_hbm, load_ref), (stiff_hbm, stiff_ref),
        (record_hbm, record_ref), (turn_hbm, turn_ref), (columns_hbm, columns_ref), (partner_hbm, partner_ref),
    )
    copies = [pltpu.make_async_copy(source, target, sems.at[n]) for n, (source, target) in enumerate(pairs)]
    for copy in copies:
        copy.start()
    for copy in copies[:2]:
        copy.wait()
    group, _, extent = robin0_ref.shape
    starts = position(group)
    for side, (robin_ref, half_ref) in enumerate(((robin0_ref, half0_ref), (robin1_ref, half1_ref))):
        for index in range(group):
            lanes = lanes_of(starts[side] + index, extent)
            robin = stress_ref[:, lanes].astype(jnp.float32) + motion_ref[:, lanes].astype(jnp.float32)
            robin_ref[index] = robin
            half_ref[index] = robin.astype(jnp.bfloat16)
    for copy in copies[2:]:
        copy.wait()


def fetch(blocks_hbm, blocks_ref, sems):
    copies = [
        pltpu.make_async_copy(blocks_hbm.at[face], blocks_ref.at[face], sems.at[face])
        for face in range(blocks_hbm.shape[0])
    ]
    for copy in copies:
        copy.start()
    for copy in copies:
        copy.wait()


def block_products(parts):
    times, extent = parts[0][0][0].shape
    zero = jnp.zeros_like(parts[0][0][1])
    depth = max(len(part) for part in parts)
    parts = [part + [(part[0][0], zero)] * (depth - len(part)) for part in parts]
    values = jnp.concatenate([jnp.concatenate([v for v, _ in part], axis=1) for part in parts], axis=0)
    blocks = jnp.concatenate([jnp.concatenate([c for _, c in part], axis=1) for part in parts], axis=0)
    product = lax.dot_general(values, blocks, (((1,), (1,)), ((), ())), preferred_element_type=jnp.float32)
    return [
        product[p * times : (p + 1) * times, p * extent : (p + 1) * extent] for p in range(len(parts))
    ]


def linear_section(side, columns_ref, compliance_ref, own0_ref, own1_ref, other0_ref, other1_ref, robin_ref, load_ref,
                   stiff_ref, record_ref, *refs):
    out_ref, half_ref = refs[-2:]
    group, rows, extent = out_ref.shape
    times = own0_ref.shape[1]
    faces, stored = compliance_ref.shape[:2]
    *starts, mine = position(group)
    first = starts[side]
    for run, refs in ((mine, (own0_ref, own1_ref)), (1 - mine, (other0_ref, other1_ref))):
        for start, ref in zip(starts, refs):
            half_ref[pl.ds(run * faces + start, group)] = ref[...]

    def entries(face, begin, end):
        return [(half_ref[columns_ref[face, 0, j]], compliance_ref[face, j]) for j in range(begin, end)]

    def finish(index, product):
        lanes = lanes_of(first + index, extent)
        response = product + load_ref[:, lanes].astype(jnp.float32)
        out_ref[index, :times] = robin_ref[index] - 2.0 * response
        if rows > times:
            out_ref[index, times : times + 1] = stiff_ref[:, lanes]
            out_ref[index, times + 1 : times + 2] = record_ref[:, lanes]
            out_ref[index, times + 2 :] = jnp.zeros_like(out_ref[index, times + 2 :])

    for index in range(0, group - 1, 2):
        pair = block_products([entries(first + index + k, 0, stored) for k in range(2)])
        for k in range(2):
            finish(index + k, pair[k])
    if group % 2:
        face = first + group - 1
        cut = (stored + 3) // 4 * 2
        finish(group - 1, sum(block_products([entries(face, 0, cut), entries(face, cut, stored)])))


def running_peak(sizes):
    row = lax.broadcasted_iota(jnp.int32, sizes.shape, 0)
    step = 1
    while step < sizes.shape[0]:
        earlier = pltpu.roll(sizes, step, 0)
        sizes = jnp.maximum(sizes, jnp.where(row >= step, earlier, 0.0))
        step *= 2
    return sizes


def local_face(times, ascent, mate, turn, stiffness, record, live, begin):
    extent = ascent.shape[1]
    gather = functools.partial(jnp.take_along_axis, axis=1, mode="promise_in_bounds")
    mate_ascent = gather(mate[:times], jnp.broadcast_to(turn, (times, extent)))
    if begin:
        constants = gather(mate[times:], jnp.broadcast_to(turn, (SUBLANES, extent)))
        stiffness = 0.5 * (stiffness + constants[:1])
        record = jnp.maximum(record, constants[1:2])
    difference = ascent - mate_ascent
    jump = difference / (1.0 + 2.0 * stiffness)
    peak = jnp.maximum(record, running_peak(jnp.abs(jump)))
    damage = jnp.clip((peak - ONSET_JUMP) / (FAILURE_JUMP - ONSET_JUMP), 0.0, 1.0)
    effective = stiffness * (1.0 - damage)
    traction = jnp.where(live, effective * difference / (1.0 + 2.0 * effective), 0.0)
    return traction, traction - ascent, stiffness, record


def local_group(side, begin, partner_ref, turn_ref, own_ref, mate_ref, stiff_ref, record_ref, robin_ref, half_ref, *pair_refs):
    group, times, extent = robin_ref.shape
    first = position(group)[side]
    for index in range(group):
        face = first + index
        partner = partner_ref[0, face]
        constants = lanes_of(face if begin else index, extent)
        traction, motion, stiffness, record = local_face(
            times, own_ref[index, :times], mate_ref[jnp.maximum(partner, 0)], turn_ref[:, lanes_of(face, extent)],
            stiff_ref[:, constants], record_ref[:, constants], partner >= 0, begin,
        )
        robin = traction + motion
        robin_ref[index] = robin
        half_ref[index] = robin.astype(jnp.bfloat16)
        if begin:
            pair_refs[0][:, lanes_of(index, extent)] = stiffness
            pair_refs[1][:, lanes_of(index, extent)] = record


def local_last(partner_ref, turn_ref, own0_ref, own1_ref, mate0_ref, mate1_ref, stiff0_ref, stiff1_ref,
               record0_ref, record1_ref, motion_ref, traction_ref):
    group, times, extent = own0_ref.shape
    starts = position(group)
    for side, (own_ref, mate_ref, stiff_ref, record_ref) in enumerate((
        (own0_ref, mate0_ref, stiff0_ref, record0_ref), (own1_ref, mate1_ref, stiff1_ref, record1_ref),
    )):
        for index in range(group):
            face = starts[side] + index
            lanes, constants = lanes_of(face, extent), lanes_of(index, extent)
            partner = partner_ref[0, face]
            traction, motion, _, _ = local_face(
                times, own_ref[index], mate_ref[jnp.maximum(partner, 0)], turn_ref[:, lanes],
                stiff_ref[:, constants], record_ref[:, constants], partner >= 0, False,
            )
            motion_ref[:, lanes] = motion.astype(jnp.bfloat16)
            traction_ref[:, lanes] = traction.astype(jnp.bfloat16)


def shards(
    compliance,
    block_columns,
    load_response,
    starting_motion,
    start_traction,
    stiffness,
    history,
    face_partner,
    orientation,
):
    _, faces, stored, extent, _ = compliance.shape
    times = starting_motion.shape[1]
    group = faces // 2
    subs = lax.axis_size("sub")
    rows = lax.axis_size("row")
    near_pairs = [(s, s ^ 1 if s ^ 1 < subs else s) for s in range(subs)]
    far_mate = [s - 1 if s % 2 == 0 else s + 1 for s in range(subs)]
    far_pairs = [(s, t if 0 <= t < subs else s) for s, t in enumerate(far_mate)]
    swap = [(r, rows - 1 - r) for r in range(rows)]

    def f32(*shape):
        return jax.ShapeDtypeStruct(shape, jnp.float32)

    def bf16(*shape):
        return jax.ShapeDtypeStruct(shape, jnp.bfloat16)

    def s32(*shape):
        return jax.ShapeDtypeStruct(shape, jnp.int32)

    def call(kernel, in_specs, out_shape, scratch=(), moved=0):
        outs = out_shape if isinstance(out_shape, tuple) else (out_shape,)
        return pl.pallas_call(
            kernel,
            out_shape=out_shape,
            in_specs=in_specs,
            out_specs=(VMEM,) * len(outs) if isinstance(out_shape, tuple) else VMEM,
            scratch_shapes=scratch,
            compiler_params=pltpu.CompilerParams(vmem_limit_bytes=VMEM_BYTES),
            cost_estimate=pl.CostEstimate(flops=0, bytes_accessed=moved, transcendentals=0),
        )

    part = (group, times, extent)
    flat = (times, faces * extent)
    block_bytes = faces * stored * extent * extent * 2
    part_bytes = group * times * extent * 4
    robin0, robin1, half0, half1, load, stiff, record, turn, columns, partner = call(
        prepare, [ANY] * 8,
        (f32(*part), f32(*part), bf16(*part), bf16(*part), bf16(*flat), f32(1, faces * extent), f32(1, faces * extent),
         s32(1, faces * extent), s32(faces, 1, stored), s32(1, faces)),
        [pltpu.VMEM(flat, jnp.bfloat16), pltpu.VMEM(flat, jnp.bfloat16), pltpu.SemaphoreType.DMA((8,))],
        8 * part_bytes,
    )(
        starting_motion[0], start_traction[0], load_response[0], stiffness, history,
        orientation.reshape(1, -1), jnp.transpose(block_columns, (1, 0, 2)), face_partner,
    )
    blocks = call(
        fetch, [ANY], pltpu.VMEM((faces, stored, extent, extent), jnp.bfloat16),
        [pltpu.SemaphoreType.DMA((faces,))], block_bytes,
    )(compliance[0])

    robin, half = [robin0, robin1], [half0, half1]
    stiffs, records = [stiff, stiff], [record, record]
    for iteration in range(ITERS):
        begin, last = iteration == 0, iteration == ITERS - 1
        other = [lax.ppermute(half[side], "row", swap) for side in range(2)]
        ascent, mates = [None, None], [None, None]
        for side, pairs in ((1, far_pairs), (0, near_pairs)):
            after = () if side else (ascent[1],)
            ascent[side] = call(
                functools.partial(linear_section, side),
                [SMEM] + [VMEM] * 9 + [ANY] * len(after),
                f32(group, times + SUBLANES if begin else times, extent),
                [pltpu.VMEM((rows * faces, times, extent), jnp.bfloat16)],
                2 * block_bytes,
            )(columns, blocks, *half, *other, robin[side], load, stiff, record, *after)
            mates[side] = lax.ppermute(ascent[side], "sub", pairs)
        if last:
            return tuple(out[None] for out in call(
                local_last, [SMEM] + [VMEM] * 9, (bf16(*flat),) * 2, (), 8 * part_bytes,
            )(partner, turn, *ascent, *mates, *stiffs, *records))
        for side in range(2):
            outs = (f32(*part), bf16(*part))
            if begin:
                outs += (f32(1, group * extent),) * 2
            robin[side], half[side], *pair = call(
                functools.partial(local_group, side, begin), [SMEM] + [VMEM] * 5, outs, (), 8 * part_bytes,
            )(partner, turn, ascent[side], mates[side], stiffs[side], records[side])
            if begin:
                stiffs[side], records[side] = pair


def solution(mesh):
    in_specs = (
        P("sub", "row", None, None, None),
        P("sub", "row", None),
        P("sub", None, "row"),
        P("sub", None, "row"),
        P("sub", None, "row"),
        P("sub", "row"),
        P("sub", "row"),
        P("sub", "row"),
        P("sub", "row", None),
    )
    out_specs = (P("sub", None, "row"), P("sub", None, "row"))
    return jax.shard_map(shards, mesh=mesh, in_specs=in_specs, out_specs=out_specs, check_vma=False)
```

```python
import functools

import jax
import jax.numpy as jnp
from jax import lax
from jax.experimental import pallas as pl
from jax.experimental.pallas import tpu as pltpu
from jax.sharding import PartitionSpec as P

ITERS = 3
SUBLANES = 8
VMEM_BYTES = 24 * 2**20

ONSET_JUMP = 0.15
FAILURE_JUMP = 1.5

VMEM = pl.BlockSpec(memory_space=pltpu.VMEM)
SMEM = pl.BlockSpec(memory_space=pltpu.SMEM)
HBM = pl.BlockSpec(memory_space=pltpu.HBM)


def position(group):
    near = group * (lax.axis_index("sub") % 2)
    return group - near, near, lax.axis_index("row")


def lanes_of(face, extent):
    return pl.ds(pl.multiple_of(face * extent, extent), extent)


def prepare(motion_hbm, stress_hbm, load_hbm, stiff_hbm, record_hbm, turn_hbm, columns_hbm, partner_hbm,
            robin0_ref, robin1_ref, half0_ref, half1_ref, load_ref, stiff_ref, record_ref, turn_ref, columns_ref, partner_ref,
            motion_ref, stress_ref, sems):
    pairs = (
        (motion_hbm, motion_ref), (stress_hbm, stress_ref), (load_hbm, load_ref), (stiff_hbm, stiff_ref),
        (record_hbm, record_ref), (turn_hbm, turn_ref), (columns_hbm, columns_ref), (partner_hbm, partner_ref),
    )
    copies = [pltpu.make_async_copy(source, target, sems.at[n]) for n, (source, target) in enumerate(pairs)]
    for copy in copies:
        copy.start()
    for copy in copies[:2]:
        copy.wait()
    group, _, extent = robin0_ref.shape
    starts = position(group)
    for side, (robin_ref, half_ref) in enumerate(((robin0_ref, half0_ref), (robin1_ref, half1_ref))):
        for index in range(group):
            lanes = lanes_of(starts[side] + index, extent)
            robin = stress_ref[:, lanes].astype(jnp.float32) + motion_ref[:, lanes].astype(jnp.float32)
            robin_ref[index] = robin
            half_ref[index] = robin.astype(jnp.bfloat16)
    for copy in copies[2:]:
        copy.wait()


def fetch(blocks_hbm, blocks_ref, sems):
    copies = [
        pltpu.make_async_copy(blocks_hbm.at[face], blocks_ref.at[face], sems.at[face])
        for face in range(blocks_hbm.shape[0])
    ]
    for copy in copies:
        copy.start()
    for copy in copies:
        copy.wait()


def block_products(parts):
    times, extent = parts[0][0][0].shape
    zero = jnp.zeros_like(parts[0][0][1])
    depth = max(len(part) for part in parts)
    parts = [part + [(part[0][0], zero)] * (depth - len(part)) for part in parts]
    values = jnp.concatenate([jnp.concatenate([v for v, _ in part], axis=1) for part in parts], axis=0)
    blocks = jnp.concatenate([jnp.concatenate([c for _, c in part], axis=1) for part in parts], axis=0)
    product = lax.dot_general(values, blocks, (((1,), (1,)), ((), ())), preferred_element_type=jnp.float32)
    return [
        product[p * times : (p + 1) * times, p * extent : (p + 1) * extent] for p in range(len(parts))
    ]


def linear_section(side, columns_ref, compliance_ref, own0_ref, own1_ref, other0_ref, other1_ref, robin_ref, load_ref,
                   stiff_ref, record_ref, out_ref, half_ref):
    group, rows, extent = out_ref.shape
    times = own0_ref.shape[1]
    faces, stored = compliance_ref.shape[:2]
    *starts, mine = position(group)
    first = starts[side]
    for run, refs in ((mine, (own0_ref, own1_ref)), (1 - mine, (other0_ref, other1_ref))):
        for start, ref in zip(starts, refs):
            half_ref[pl.ds(run * faces + start, group)] = ref[...]

    def entries(face, begin, end):
        return [(half_ref[columns_ref[face, 0, j]], compliance_ref[face, j]) for j in range(begin, end)]

    def finish(index, product):
        lanes = lanes_of(first + index, extent)
        response = product + load_ref[:, lanes].astype(jnp.float32)
        out_ref[index, :times] = robin_ref[index] - 2.0 * response
        if rows > times:
            out_ref[index, times : times + 1] = stiff_ref[:, lanes]
            out_ref[index, times + 1 : times + 2] = record_ref[:, lanes]
            out_ref[index, times + 2 :] = jnp.zeros_like(out_ref[index, times + 2 :])

    for index in range(0, group - 1, 2):
        pair = block_products([entries(first + index + k, 0, stored) for k in range(2)])
        for k in range(2):
            finish(index + k, pair[k])
    if group % 2:
        face = first + group - 1
        cut = (stored + 3) // 4 * 2
        finish(group - 1, sum(block_products([entries(face, 0, cut), entries(face, cut, stored)])))


def running_peak(sizes):
    row = lax.broadcasted_iota(jnp.int32, sizes.shape, 0)
    step = 1
    while step < sizes.shape[0]:
        earlier = pltpu.roll(sizes, step, 0)
        sizes = jnp.maximum(sizes, jnp.where(row >= step, earlier, 0.0))
        step *= 2
    return sizes


def local_face(times, ascent, mate, turn, stiffness, record, live, begin):
    extent = ascent.shape[1]
    gather = functools.partial(jnp.take_along_axis, axis=1, mode="promise_in_bounds")
    mate_ascent = gather(mate[:times], jnp.broadcast_to(turn, (times, extent)))
    if begin:
        constants = gather(mate[times:], jnp.broadcast_to(turn, (SUBLANES, extent)))
        stiffness = 0.5 * (stiffness + constants[:1])
        record = jnp.maximum(record, constants[1:2])
    difference = ascent - mate_ascent
    jump = difference / (1.0 + 2.0 * stiffness)
    peak = jnp.maximum(record, running_peak(jnp.abs(jump)))
    damage = jnp.clip((peak - ONSET_JUMP) / (FAILURE_JUMP - ONSET_JUMP), 0.0, 1.0)
    effective = stiffness * (1.0 - damage)
    traction = jnp.where(live, effective * difference / (1.0 + 2.0 * effective), 0.0)
    return traction, traction - ascent, stiffness, record


def local_group(side, begin, partner_ref, turn_ref, own_ref, mate_ref, stiff_ref, record_ref, robin_ref, half_ref, *pair_refs):
    group, times, extent = robin_ref.shape
    first = position(group)[side]
    for index in range(group):
        face = first + index
        partner = partner_ref[0, face]
        constants = lanes_of(face if begin else index, extent)
        traction, motion, stiffness, record = local_face(
            times, own_ref[index, :times], mate_ref[jnp.maximum(partner, 0)], turn_ref[:, lanes_of(face, extent)],
            stiff_ref[:, constants], record_ref[:, constants], partner >= 0, begin,
        )
        robin = traction + motion
        robin_ref[index] = robin
        half_ref[index] = robin.astype(jnp.bfloat16)
        if begin:
            pair_refs[0][:, lanes_of(index, extent)] = stiffness
            pair_refs[1][:, lanes_of(index, extent)] = record


def local_last(partner_ref, turn_ref, own0_ref, own1_ref, mate0_ref, mate1_ref, stiff0_ref, stiff1_ref,
               record0_ref, record1_ref, motion_ref, traction_ref):
    group, times, extent = own0_ref.shape
    starts = position(group)
    for side, (own_ref, mate_ref, stiff_ref, record_ref) in enumerate((
        (own0_ref, mate0_ref, stiff0_ref, record0_ref), (own1_ref, mate1_ref, stiff1_ref, record1_ref),
    )):
        for index in range(group):
            face = starts[side] + index
            lanes, constants = lanes_of(face, extent), lanes_of(index, extent)
            partner = partner_ref[0, face]
            traction, motion, _, _ = local_face(
                times, own_ref[index], mate_ref[jnp.maximum(partner, 0)], turn_ref[:, lanes],
                stiff_ref[:, constants], record_ref[:, constants], partner >= 0, False,
            )
            motion_ref[:, lanes] = motion.astype(jnp.bfloat16)
            traction_ref[:, lanes] = traction.astype(jnp.bfloat16)


def shards(
    compliance,
    block_columns,
    load_response,
    starting_motion,
    start_traction,
    stiffness,
    history,
    face_partner,
    orientation,
):
    _, faces, stored, extent, _ = compliance.shape
    times = starting_motion.shape[1]
    group = faces // 2
    subs = lax.axis_size("sub")
    rows = lax.axis_size("row")
    near_pairs = [(s, s ^ 1) for s in range(subs) if s ^ 1 < subs]
    far_pairs = [(s, t) for s in range(subs) for t in [s - 1 if s % 2 == 0 else s + 1] if 0 <= t < subs]
    swap = [(r, rows - 1 - r) for r in range(rows)]

    def f32(*shape):
        return jax.ShapeDtypeStruct(shape, jnp.float32)

    def bf16(*shape):
        return jax.ShapeDtypeStruct(shape, jnp.bfloat16)

    def s32(*shape):
        return jax.ShapeDtypeStruct(shape, jnp.int32)

    def call(kernel, in_specs, out_shape, scratch=(), moved=0):
        outs = out_shape if isinstance(out_shape, tuple) else (out_shape,)
        return pl.pallas_call(
            kernel,
            out_shape=out_shape,
            in_specs=in_specs,
            out_specs=(VMEM,) * len(outs) if isinstance(out_shape, tuple) else VMEM,
            scratch_shapes=scratch,
            compiler_params=pltpu.CompilerParams(vmem_limit_bytes=VMEM_BYTES),
            cost_estimate=pl.CostEstimate(flops=moved, bytes_accessed=moved, transcendentals=0) if moved else None,
        )

    part = (group, times, extent)
    flat = (times, faces * extent)
    block_bytes = faces * stored * extent * extent * 2
    part_bytes = group * times * extent * 4
    robin0, robin1, half0, half1, load, stiff, record, turn, columns, partner = call(
        prepare, [HBM] * 8,
        (f32(*part), f32(*part), bf16(*part), bf16(*part), bf16(*flat), f32(1, faces * extent), f32(1, faces * extent),
         s32(1, faces * extent), s32(faces, 1, stored), s32(1, faces)),
        [pltpu.VMEM(flat, jnp.bfloat16), pltpu.VMEM(flat, jnp.bfloat16), pltpu.SemaphoreType.DMA((8,))],
        8 * part_bytes,
    )(*(pltpu.with_memory_space_constraint(value, pltpu.HBM) for value in (
        starting_motion[0], start_traction[0], load_response[0], stiffness, history,
        orientation.reshape(1, -1), jnp.transpose(block_columns, (1, 0, 2)), face_partner,
    )))
    blocks = call(
        fetch, [HBM], pltpu.VMEM((faces, stored, extent, extent), jnp.bfloat16),
        [pltpu.SemaphoreType.DMA((faces,))], block_bytes,
    )(pltpu.with_memory_space_constraint(compliance[0], pltpu.HBM))

    robin, half = [robin0, robin1], [half0, half1]
    stiffs, records = [stiff, stiff], [record, record]
    for iteration in range(ITERS):
        begin, last = iteration == 0, iteration == ITERS - 1
        other = [lax.ppermute(half[side], "row", swap) for side in range(2)]
        ascent, mates = [None, None], [None, None]
        for side, pairs in enumerate((far_pairs, near_pairs)):
            ascent[side] = call(
                functools.partial(linear_section, side),
                [SMEM] + [VMEM] * 9,
                f32(group, times + SUBLANES if begin else times, extent),
                [pltpu.VMEM((rows * faces, times, extent), jnp.bfloat16)],
                2 * block_bytes,
            )(columns, blocks, *half, *other, robin[side], load, stiff, record)
            mates[side] = lax.ppermute(ascent[side], "sub", pairs)
        if last:
            return tuple(out[None] for out in call(
                local_last, [SMEM] + [VMEM] * 9, (bf16(*flat),) * 2,
            )(partner, turn, *ascent, *mates, *stiffs, *records))
        for side in range(2):
            outs = (f32(*part), bf16(*part))
            if begin:
                outs += (f32(1, group * extent),) * 2
            robin[side], half[side], *pair = call(
                functools.partial(local_group, side, begin), [SMEM] + [VMEM] * 5, outs,
            )(partner, turn, ascent[side], mates[side], stiffs[side], records[side])
            if begin:
                stiffs[side], records[side] = pair


def solution(mesh):
    in_specs = (
        P("sub", "row", None, None, None),
        P("sub", "row", None),
        P("sub", None, "row"),
        P("sub", None, "row"),
        P("sub", None, "row"),
        P("sub", "row"),
        P("sub", "row"),
        P("sub", "row"),
        P("sub", "row", None),
    )
    out_specs = (P("sub", None, "row"), P("sub", None, "row"))
    return jax.shard_map(shards, mesh=mesh, in_specs=in_specs, out_specs=out_specs, check_vma=False)
```

```python
import functools

import jax
import jax.numpy as jnp
from jax import lax
from jax.experimental import pallas as pl
from jax.experimental.pallas import tpu as pltpu
from jax.sharding import PartitionSpec as P

ITERS = 3
SUBLANES = 8
VMEM_BYTES = 24 * 2**20

ONSET_JUMP = 0.15
FAILURE_JUMP = 1.5

VMEM = pl.BlockSpec(memory_space=pltpu.VMEM)
SMEM = pl.BlockSpec(memory_space=pltpu.SMEM)
HBM = pl.BlockSpec(memory_space=pltpu.HBM)


def position(group):
    near = group * (lax.axis_index("sub") % 2)
    return group - near, near, lax.axis_index("row")


def lanes_of(face, extent):
    return pl.ds(pl.multiple_of(face * extent, extent), extent)


def prepare(motion_hbm, stress_hbm, load_hbm, stiff_hbm, record_hbm, turn_hbm, columns_hbm, partner_hbm,
            robin0_ref, robin1_ref, half0_ref, half1_ref, load_ref, stiff_ref, record_ref, turn_ref, columns_ref, partner_ref,
            motion_ref, stress_ref, sems):
    pairs = (
        (motion_hbm, motion_ref), (stress_hbm, stress_ref), (load_hbm, load_ref), (stiff_hbm, stiff_ref),
        (record_hbm, record_ref), (turn_hbm, turn_ref), (columns_hbm, columns_ref), (partner_hbm, partner_ref),
    )
    copies = [pltpu.make_async_copy(source, target, sems.at[n]) for n, (source, target) in enumerate(pairs)]
    for copy in copies:
        copy.start()
    for copy in copies[:2]:
        copy.wait()
    group, _, extent = robin0_ref.shape
    starts = position(group)
    for side, (robin_ref, half_ref) in enumerate(((robin0_ref, half0_ref), (robin1_ref, half1_ref))):
        for index in range(group):
            lanes = lanes_of(starts[side] + index, extent)
            robin = stress_ref[:, lanes].astype(jnp.float32) + motion_ref[:, lanes].astype(jnp.float32)
            robin_ref[index] = robin
            half_ref[index] = robin.astype(jnp.bfloat16)
    for copy in copies[2:]:
        copy.wait()


def fetch(blocks_hbm, blocks_ref, sems):
    copies = [
        pltpu.make_async_copy(blocks_hbm.at[face], blocks_ref.at[face], sems.at[face])
        for face in range(blocks_hbm.shape[0])
    ]
    for copy in copies:
        copy.start()
    for copy in copies:
        copy.wait()


def block_products(parts):
    times, extent = parts[0][0][0].shape
    zero = jnp.zeros_like(parts[0][0][1])
    depth = max(len(part) for part in parts)
    parts = [part + [(part[0][0], zero)] * (depth - len(part)) for part in parts]
    values = jnp.concatenate([jnp.concatenate([v for v, _ in part], axis=1) for part in parts], axis=0)
    blocks = jnp.concatenate([jnp.concatenate([c for _, c in part], axis=1) for part in parts], axis=0)
    product = lax.dot_general(values, blocks, (((1,), (1,)), ((), ())), preferred_element_type=jnp.float32)
    return [
        product[p * times : (p + 1) * times, p * extent : (p + 1) * extent] for p in range(len(parts))
    ]


def linear_section(side, columns_ref, compliance_ref, own0_ref, own1_ref, other0_ref, other1_ref, robin_ref, load_ref,
                   stiff_ref, record_ref, out_ref, half_ref):
    group, rows, extent = out_ref.shape
    times = own0_ref.shape[1]
    faces, stored = compliance_ref.shape[:2]
    *starts, mine = position(group)
    first = starts[side]
    for run, refs in ((mine, (own0_ref, own1_ref)), (1 - mine, (other0_ref, other1_ref))):
        for start, ref in zip(starts, refs):
            half_ref[pl.ds(run * faces + start, group)] = ref[...]

    def entries(face, begin, end):
        return [(half_ref[columns_ref[face, 0, j]], compliance_ref[face, j]) for j in range(begin, end)]

    def finish(index, product):
        lanes = lanes_of(first + index, extent)
        response = product + load_ref[:, lanes].astype(jnp.float32)
        out_ref[index, :times] = robin_ref[index] - 2.0 * response
        if rows > times:
            out_ref[index, times : times + 1] = stiff_ref[:, lanes]
            out_ref[index, times + 1 : times + 2] = record_ref[:, lanes]
            out_ref[index, times + 2 :] = jnp.zeros_like(out_ref[index, times + 2 :])

    for index in range(0, group - 1, 2):
        pair = block_products([entries(first + index + k, 0, stored) for k in range(2)])
        for k in range(2):
            finish(index + k, pair[k])
    if group % 2:
        face = first + group - 1
        cut = (stored + 3) // 4 * 2
        finish(group - 1, sum(block_products([entries(face, 0, cut), entries(face, cut, stored)])))


def running_peak(sizes):
    row = lax.broadcasted_iota(jnp.int32, sizes.shape, 0)
    step = 1
    while step < sizes.shape[0]:
        earlier = pltpu.roll(sizes, step, 0)
        sizes = jnp.maximum(sizes, jnp.where(row >= step, earlier, 0.0))
        step *= 2
    return sizes


def local_face(times, ascent, mate, turn, stiffness, record, live, begin):
    extent = ascent.shape[1]
    gather = functools.partial(jnp.take_along_axis, axis=1, mode="promise_in_bounds")
    mate_ascent = gather(mate[:times], jnp.broadcast_to(turn, (times, extent)))
    if begin:
        constants = gather(mate[times:], jnp.broadcast_to(turn, (SUBLANES, extent)))
        stiffness = 0.5 * (stiffness + constants[:1])
        record = jnp.maximum(record, constants[1:2])
    difference = ascent - mate_ascent
    jump = difference / (1.0 + 2.0 * stiffness)
    peak = jnp.maximum(record, running_peak(jnp.abs(jump)))
    damage = jnp.clip((peak - ONSET_JUMP) / (FAILURE_JUMP - ONSET_JUMP), 0.0, 1.0)
    effective = stiffness * (1.0 - damage)
    traction = jnp.where(live, effective * difference / (1.0 + 2.0 * effective), 0.0)
    return traction, traction - ascent, stiffness, record


def local_group(side, begin, partner_ref, turn_ref, own_ref, mate_ref, stiff_ref, record_ref, robin_ref, half_ref, *pair_refs):
    group, times, extent = robin_ref.shape
    first = position(group)[side]
    for index in range(group):
        face = first + index
        partner = partner_ref[0, face]
        constants = lanes_of(face if begin else index, extent)
        traction, motion, stiffness, record = local_face(
            times, own_ref[index, :times], mate_ref[jnp.maximum(partner, 0)], turn_ref[:, lanes_of(face, extent)],
            stiff_ref[:, constants], record_ref[:, constants], partner >= 0, begin,
        )
        robin = traction + motion
        robin_ref[index] = robin
        half_ref[index] = robin.astype(jnp.bfloat16)
        if begin:
            pair_refs[0][:, lanes_of(index, extent)] = stiffness
            pair_refs[1][:, lanes_of(index, extent)] = record


def local_last(partner_ref, turn_ref, own0_ref, own1_ref, mate0_ref, mate1_ref, stiff0_ref, stiff1_ref,
               record0_ref, record1_ref, motion_ref, traction_ref):
    group, times, extent = own0_ref.shape
    starts = position(group)
    for side, (own_ref, mate_ref, stiff_ref, record_ref) in enumerate((
        (own0_ref, mate0_ref, stiff0_ref, record0_ref), (own1_ref, mate1_ref, stiff1_ref, record1_ref),
    )):
        for index in range(group):
            face = starts[side] + index
            lanes, constants = lanes_of(face, extent), lanes_of(index, extent)
            partner = partner_ref[0, face]
            traction, motion, _, _ = local_face(
                times, own_ref[index], mate_ref[jnp.maximum(partner, 0)], turn_ref[:, lanes],
                stiff_ref[:, constants], record_ref[:, constants], partner >= 0, False,
            )
            motion_ref[:, lanes] = motion.astype(jnp.bfloat16)
            traction_ref[:, lanes] = traction.astype(jnp.bfloat16)


def shards(
    compliance,
    block_columns,
    load_response,
    starting_motion,
    start_traction,
    stiffness,
    history,
    face_partner,
    orientation,
):
    _, faces, stored, extent, _ = compliance.shape
    times = starting_motion.shape[1]
    group = faces // 2
    subs = lax.axis_size("sub")
    rows = lax.axis_size("row")
    near_pairs = [(s, s ^ 1) for s in range(subs) if s ^ 1 < subs]
    far_pairs = [(s, t) for s in range(subs) for t in [s - 1 if s % 2 == 0 else s + 1] if 0 <= t < subs]
    swap = [(r, rows - 1 - r) for r in range(rows)]

    def f32(*shape):
        return jax.ShapeDtypeStruct(shape, jnp.float32)

    def bf16(*shape):
        return jax.ShapeDtypeStruct(shape, jnp.bfloat16)

    def s32(*shape):
        return jax.ShapeDtypeStruct(shape, jnp.int32)

    def call(kernel, in_specs, out_shape, scratch=(), moved=0, out_specs=()):
        outs = out_shape if isinstance(out_shape, tuple) else (out_shape,)
        out_specs = out_specs or (VMEM,) * len(outs)
        return pl.pallas_call(
            kernel,
            out_shape=out_shape,
            in_specs=in_specs,
            out_specs=out_specs if isinstance(out_shape, tuple) else out_specs[0],
            scratch_shapes=scratch,
            compiler_params=pltpu.CompilerParams(vmem_limit_bytes=VMEM_BYTES),
            cost_estimate=pl.CostEstimate(flops=moved, bytes_accessed=moved, transcendentals=0) if moved else None,
        )

    part = (group, times, extent)
    flat = (times, faces * extent)
    block_bytes = faces * stored * extent * extent * 2
    part_bytes = group * times * extent * 4
    robin0, robin1, half0, half1, load, stiff, record, turn, columns, partner = call(
        prepare, [HBM] * 8,
        (f32(*part), f32(*part), bf16(*part), bf16(*part), bf16(*flat), f32(1, faces * extent), f32(1, faces * extent),
         s32(1, faces * extent), pltpu.SMEM((faces, 1, stored), jnp.int32), pltpu.SMEM((1, faces), jnp.int32)),
        [pltpu.VMEM(flat, jnp.bfloat16), pltpu.VMEM(flat, jnp.bfloat16), pltpu.SemaphoreType.DMA((8,))],
        8 * part_bytes, (VMEM,) * 8 + (SMEM,) * 2,
    )(*(pltpu.with_memory_space_constraint(value, pltpu.HBM) for value in (
        starting_motion[0], start_traction[0], load_response[0], stiffness, history,
        orientation.reshape(1, -1), jnp.transpose(block_columns, (1, 0, 2)), face_partner,
    )))
    columns, partner = (pltpu.with_memory_space_constraint(table, pltpu.SMEM) for table in (columns, partner))
    blocks = call(
        fetch, [HBM], pltpu.VMEM((faces, stored, extent, extent), jnp.bfloat16),
        [pltpu.SemaphoreType.DMA((faces,))], block_bytes,
    )(pltpu.with_memory_space_constraint(compliance[0], pltpu.HBM))

    robin, half = [robin0, robin1], [half0, half1]
    stiffs, records = [stiff, stiff], [record, record]
    for iteration in range(ITERS):
        begin, last = iteration == 0, iteration == ITERS - 1
        other = [lax.ppermute(half[side], "row", swap) for side in range(2)]
        ascent, mates = [None, None], [None, None]
        for side, pairs in enumerate((far_pairs, near_pairs)):
            ascent[side] = call(
                functools.partial(linear_section, side),
                [SMEM] + [VMEM] * 9,
                f32(group, times + SUBLANES if begin else times, extent),
                [pltpu.VMEM((rows * faces, times, extent), jnp.bfloat16)],
                2 * block_bytes,
            )(columns, blocks, *half, *other, robin[side], load, stiff, record)
            mates[side] = lax.ppermute(ascent[side], "sub", pairs)
        if last:
            return tuple(out[None] for out in call(
                local_last, [SMEM] + [VMEM] * 9, (bf16(*flat),) * 2,
            )(partner, turn, *ascent, *mates, *stiffs, *records))
        for side in range(2):
            outs = (f32(*part), bf16(*part))
            if begin:
                outs += (f32(1, group * extent),) * 2
            robin[side], half[side], *pair = call(
                functools.partial(local_group, side, begin), [SMEM] + [VMEM] * 5, outs,
            )(partner, turn, ascent[side], mates[side], stiffs[side], records[side])
            if begin:
                stiffs[side], records[side] = pair


def solution(mesh):
    in_specs = (
        P("sub", "row", None, None, None),
        P("sub", "row", None),
        P("sub", None, "row"),
        P("sub", None, "row"),
        P("sub", None, "row"),
        P("sub", "row"),
        P("sub", "row"),
        P("sub", "row"),
        P("sub", "row", None),
    )
    out_specs = (P("sub", None, "row"), P("sub", None, "row"))
    return jax.shard_map(shards, mesh=mesh, in_specs=in_specs, out_specs=out_specs, check_vma=False)
```

```python
import functools

import jax
import jax.numpy as jnp
from jax import lax
from jax.experimental import pallas as pl
from jax.experimental.pallas import tpu as pltpu
from jax.sharding import PartitionSpec as P

ITERS = 3
SUBLANES = 8
VMEM_BYTES = 24 * 2**20

ONSET_JUMP = 0.15
FAILURE_JUMP = 1.5

VMEM = pl.BlockSpec(memory_space=pltpu.VMEM)
SMEM = pl.BlockSpec(memory_space=pltpu.SMEM)
HBM = pl.BlockSpec(memory_space=pltpu.HBM)


def position(group):
    near = group * (lax.axis_index("sub") % 2)
    return near, group - near, lax.axis_index("row")


def lanes_of(face, extent):
    return pl.ds(pl.multiple_of(face * extent, extent), extent)


def prepare(motion_hbm, stress_hbm, load_hbm, stiff_hbm, record_hbm, turn_hbm, columns_hbm, partner_hbm,
            robin0_ref, robin1_ref, half0_ref, half1_ref, load_ref, stiff_ref, record_ref, turn_ref, columns_ref, partner_ref,
            motion_ref, stress_ref, sems):
    pairs = (
        (motion_hbm, motion_ref), (stress_hbm, stress_ref), (load_hbm, load_ref), (stiff_hbm, stiff_ref),
        (record_hbm, record_ref), (turn_hbm, turn_ref), (columns_hbm, columns_ref), (partner_hbm, partner_ref),
    )
    copies = [pltpu.make_async_copy(source, target, sems.at[n]) for n, (source, target) in enumerate(pairs)]
    for copy in copies:
        copy.start()
    for copy in copies[:2]:
        copy.wait()
    group, _, extent = robin0_ref.shape
    starts = position(group)
    for side, (robin_ref, half_ref) in enumerate(((robin0_ref, half0_ref), (robin1_ref, half1_ref))):
        for index in range(group):
            lanes = lanes_of(starts[side] + index, extent)
            robin = stress_ref[:, lanes].astype(jnp.float32) + motion_ref[:, lanes].astype(jnp.float32)
            robin_ref[index] = robin
            half_ref[index] = robin.astype(jnp.bfloat16)
    for copy in copies[2:]:
        copy.wait()


def fetch(blocks_hbm, blocks_ref, sems):
    copies = [
        pltpu.make_async_copy(blocks_hbm.at[face], blocks_ref.at[face], sems.at[face])
        for face in range(blocks_hbm.shape[0])
    ]
    for copy in copies:
        copy.start()
    for copy in copies:
        copy.wait()


def block_products(parts):
    times, extent = parts[0][0][0].shape
    zero = jnp.zeros_like(parts[0][0][1])
    depth = max(len(part) for part in parts)
    parts = [part + [(part[0][0], zero)] * (depth - len(part)) for part in parts]
    values = jnp.concatenate([jnp.concatenate([v for v, _ in part], axis=1) for part in parts], axis=0)
    blocks = jnp.concatenate([jnp.concatenate([c for _, c in part], axis=1) for part in parts], axis=0)
    product = lax.dot_general(values, blocks, (((1,), (1,)), ((), ())), preferred_element_type=jnp.float32)
    return [
        product[p * times : (p + 1) * times, p * extent : (p + 1) * extent] for p in range(len(parts))
    ]


def linear_section(side, columns_ref, compliance_ref, own0_ref, own1_ref, other0_ref, other1_ref, robin_ref, load_ref,
                   stiff_ref, record_ref, out_ref, half_ref):
    group, times, extent = own0_ref.shape
    rows = out_ref.shape[1]
    faces, stored = compliance_ref.shape[:2]
    *starts, mine = position(group)
    first = starts[side]
    for run, refs in ((mine, (own0_ref, own1_ref)), (1 - mine, (other0_ref, other1_ref))):
        for start, ref in zip(starts, refs):
            half_ref[pl.ds(run * faces + start, group)] = ref[...]

    def entries(face, begin, end):
        return [(half_ref[columns_ref[face, 0, j]], compliance_ref[face, j]) for j in range(begin, end)]

    def finish(index, product):
        lanes = lanes_of(first + index, extent)
        response = product + load_ref[:, lanes].astype(jnp.float32)
        out_ref[index, :times] = robin_ref[index] - 2.0 * response
        if rows > times:
            out_ref[index, times : times + 1] = stiff_ref[:, lanes]
            out_ref[index, times + 1 : times + 2] = record_ref[:, lanes]
            out_ref[index, times + 2 :] = jnp.zeros_like(out_ref[index, times + 2 :])

    for index in range(0, group - 1, 2):
        pair = block_products([entries(first + index + k, 0, stored) for k in range(2)])
        for k in range(2):
            finish(index + k, pair[k])
    for spare in range(group, out_ref.shape[0]):
        out_ref[spare] = jnp.zeros_like(out_ref[spare])
    if group % 2:
        face = first + group - 1
        cut = (stored + 3) // 4 * 2
        finish(group - 1, sum(block_products([entries(face, 0, cut), entries(face, cut, stored)])))


def running_peak(sizes):
    row = lax.broadcasted_iota(jnp.int32, sizes.shape, 0)
    step = 1
    while step < sizes.shape[0]:
        earlier = pltpu.roll(sizes, step, 0)
        sizes = jnp.maximum(sizes, jnp.where(row >= step, earlier, 0.0))
        step *= 2
    return sizes


def local_face(times, ascent, mate, turn, stiffness, record, live, begin):
    extent = ascent.shape[1]
    gather = functools.partial(jnp.take_along_axis, axis=1, mode="promise_in_bounds")
    mate_ascent = gather(mate[:times], jnp.broadcast_to(turn, (times, extent)))
    if begin:
        constants = gather(mate[times:], jnp.broadcast_to(turn, (SUBLANES, extent)))
        stiffness = 0.5 * (stiffness + constants[:1])
        record = jnp.maximum(record, constants[1:2])
    difference = ascent - mate_ascent
    jump = difference / (1.0 + 2.0 * stiffness)
    peak = jnp.maximum(record, running_peak(jnp.abs(jump)))
    damage = jnp.clip((peak - ONSET_JUMP) / (FAILURE_JUMP - ONSET_JUMP), 0.0, 1.0)
    effective = stiffness * (1.0 - damage)
    traction = jnp.where(live, effective * difference / (1.0 + 2.0 * effective), 0.0)
    return traction, traction - ascent, stiffness, record


def local_group(side, begin, partner_ref, turn_ref, own_ref, mate_ref, stiff_ref, record_ref, robin_ref, half_ref, *pair_refs):
    group, times, extent = robin_ref.shape
    first = position(group)[side]
    for index in range(group):
        face = first + index
        partner = partner_ref[0, face]
        constants = lanes_of(face if begin else index, extent)
        traction, motion, stiffness, record = local_face(
            times, own_ref[index, :times], mate_ref[jnp.maximum(partner, 0)], turn_ref[:, lanes_of(face, extent)],
            stiff_ref[:, constants], record_ref[:, constants], partner >= 0, begin,
        )
        robin = traction + motion
        robin_ref[index] = robin
        half_ref[index] = robin.astype(jnp.bfloat16)
        if begin:
            pair_refs[0][:, lanes_of(index, extent)] = stiffness
            pair_refs[1][:, lanes_of(index, extent)] = record


def local_last(partner_ref, turn_ref, own0_ref, own1_ref, mate0_ref, mate1_ref, stiff0_ref, stiff1_ref,
               record0_ref, record1_ref, motion_ref, traction_ref):
    group, times, extent = own0_ref.shape
    starts = position(group)
    for side, (own_ref, mate_ref, stiff_ref, record_ref) in enumerate((
        (own0_ref, mate0_ref, stiff0_ref, record0_ref), (own1_ref, mate1_ref, stiff1_ref, record1_ref),
    )):
        for index in range(group):
            face = starts[side] + index
            lanes, constants = lanes_of(face, extent), lanes_of(index, extent)
            partner = partner_ref[0, face]
            traction, motion, _, _ = local_face(
                times, own_ref[index], mate_ref[jnp.maximum(partner, 0)], turn_ref[:, lanes],
                stiff_ref[:, constants], record_ref[:, constants], partner >= 0, False,
            )
            motion_ref[:, lanes] = motion.astype(jnp.bfloat16)
            traction_ref[:, lanes] = traction.astype(jnp.bfloat16)


def shards(
    compliance,
    block_columns,
    load_response,
    starting_motion,
    start_traction,
    stiffness,
    history,
    face_partner,
    orientation,
):
    _, faces, stored, extent, _ = compliance.shape
    times = starting_motion.shape[1]
    group = faces // 2
    subs = lax.axis_size("sub")
    rows = lax.axis_size("row")
    near_pairs = [(s, s ^ 1) for s in range(subs) if s ^ 1 < subs]
    far_pairs = [(s, t) for s in range(subs) for t in [s - 1 if s % 2 == 0 else s + 1] if 0 <= t < subs]
    swap = [(r, rows - 1 - r) for r in range(rows)]

    def f32(*shape):
        return jax.ShapeDtypeStruct(shape, jnp.float32)

    def bf16(*shape):
        return jax.ShapeDtypeStruct(shape, jnp.bfloat16)

    def s32(*shape):
        return jax.ShapeDtypeStruct(shape, jnp.int32)

    def call(kernel, in_specs, out_shape, scratch=(), moved=0, out_specs=()):
        outs = out_shape if isinstance(out_shape, tuple) else (out_shape,)
        out_specs = out_specs or (VMEM,) * len(outs)
        return pl.pallas_call(
            kernel,
            out_shape=out_shape,
            in_specs=in_specs,
            out_specs=out_specs if isinstance(out_shape, tuple) else out_specs[0],
            scratch_shapes=scratch,
            compiler_params=pltpu.CompilerParams(vmem_limit_bytes=VMEM_BYTES),
            cost_estimate=pl.CostEstimate(flops=moved, bytes_accessed=moved, transcendentals=0) if moved else None,
        )

    part = (group, times, extent)
    flat = (times, faces * extent)
    block_bytes = faces * stored * extent * extent * 2
    part_bytes = group * times * extent * 4
    robin0, robin1, half0, half1, load, stiff, record, turn, columns, partner = call(
        prepare, [HBM] * 8,
        (f32(*part), f32(*part), bf16(*part), bf16(*part), bf16(*flat), f32(1, faces * extent), f32(1, faces * extent),
         s32(1, faces * extent), pltpu.SMEM((faces, 1, stored), jnp.int32), pltpu.SMEM((1, faces), jnp.int32)),
        [pltpu.VMEM(flat, jnp.bfloat16), pltpu.VMEM(flat, jnp.bfloat16), pltpu.SemaphoreType.DMA((8,))],
        8 * part_bytes, (VMEM,) * 8 + (SMEM,) * 2,
    )(*(pltpu.with_memory_space_constraint(value, pltpu.HBM) for value in (
        starting_motion[0], start_traction[0], load_response[0], stiffness, history,
        orientation.reshape(1, -1), jnp.transpose(block_columns, (1, 0, 2)), face_partner,
    )))
    columns, partner = (pltpu.with_memory_space_constraint(table, pltpu.SMEM) for table in (columns, partner))
    blocks = call(
        fetch, [HBM], pltpu.VMEM((faces, stored, extent, extent), jnp.bfloat16),
        [pltpu.SemaphoreType.DMA((faces,))], block_bytes,
    )(pltpu.with_memory_space_constraint(compliance[0], pltpu.HBM))

    robin, half = [robin0, robin1], [half0, half1]
    stiffs, records = [stiff, stiff], [record, record]
    for iteration in range(ITERS):
        begin, last = iteration == 0, iteration == ITERS - 1
        other = [lax.ppermute(half[side], "row", swap) for side in range(2)]
        ascent, mates = [None, None], [None, None]
        for side, pairs in enumerate((near_pairs, far_pairs)):
            ascent[side] = call(
                functools.partial(linear_section, side),
                [SMEM] + [VMEM] * 9,
                f32(group + side, times + SUBLANES if begin else times, extent),
                [pltpu.VMEM((rows * faces, times, extent), jnp.bfloat16)],
                2 * block_bytes,
            )(columns, blocks, *half, *other, robin[side], load, stiff, record)
            mates[side] = lax.ppermute(ascent[side], "sub", pairs)
        if last:
            return tuple(out[None] for out in call(
                local_last, [SMEM] + [VMEM] * 9, (bf16(*flat),) * 2,
            )(partner, turn, *ascent, *mates, *stiffs, *records))
        for side in range(2):
            outs = (f32(*part), bf16(*part))
            if begin:
                outs += (f32(1, group * extent),) * 2
            robin[side], half[side], *pair = call(
                functools.partial(local_group, side, begin), [SMEM] + [VMEM] * 5, outs,
            )(partner, turn, ascent[side], mates[side], stiffs[side], records[side])
            if begin:
                stiffs[side], records[side] = pair


def solution(mesh):
    in_specs = (
        P("sub", "row", None, None, None),
        P("sub", "row", None),
        P("sub", None, "row"),
        P("sub", None, "row"),
        P("sub", None, "row"),
        P("sub", "row"),
        P("sub", "row"),
        P("sub", "row"),
        P("sub", "row", None),
    )
    out_specs = (P("sub", None, "row"), P("sub", None, "row"))
    return jax.shard_map(shards, mesh=mesh, in_specs=in_specs, out_specs=out_specs, check_vma=False)
```

```python
import functools

import jax
import jax.numpy as jnp
from jax import lax
from jax.experimental import pallas as pl
from jax.experimental.pallas import tpu as pltpu
from jax.sharding import PartitionSpec as P

ITERS = 3
SUBLANES = 8
VMEM_BYTES = 24 * 2**20

ONSET_JUMP = 0.15
FAILURE_JUMP = 1.5

VMEM = pl.BlockSpec(memory_space=pltpu.VMEM)
SMEM = pl.BlockSpec(memory_space=pltpu.SMEM)
HBM = pl.BlockSpec(memory_space=pltpu.HBM)


def first_face(side, group):
    return side * group


def lanes_of(face, extent):
    return slice(face * extent, (face + 1) * extent)


def prepare(motion_hbm, stress_hbm, load_hbm, stiff_hbm, record_hbm, turn_hbm, columns_hbm, partner_hbm,
            robin0_ref, robin1_ref, half0_ref, half1_ref, load_ref, stiff_ref, record_ref, turn_ref, columns_ref, partner_ref,
            motion_ref, stress_ref, sems):
    pairs = (
        (motion_hbm, motion_ref), (stress_hbm, stress_ref), (load_hbm, load_ref), (stiff_hbm, stiff_ref),
        (record_hbm, record_ref), (turn_hbm, turn_ref), (columns_hbm, columns_ref), (partner_hbm, partner_ref),
    )
    copies = [pltpu.make_async_copy(source, target, sems.at[n]) for n, (source, target) in enumerate(pairs)]
    for copy in copies:
        copy.start()
    for copy in copies[:2]:
        copy.wait()
    group, _, extent = robin0_ref.shape
    for side, (robin_ref, half_ref) in enumerate(((robin0_ref, half0_ref), (robin1_ref, half1_ref))):
        for index in range(group):
            lanes = lanes_of(first_face(side, group) + index, extent)
            robin = stress_ref[:, lanes].astype(jnp.float32) + motion_ref[:, lanes].astype(jnp.float32)
            robin_ref[index] = robin
            half_ref[index] = robin.astype(jnp.bfloat16)
    for copy in copies[2:]:
        copy.wait()


def fetch(blocks_hbm, blocks_ref, sems):
    copies = [
        pltpu.make_async_copy(blocks_hbm.at[face], blocks_ref.at[face], sems.at[face])
        for face in range(blocks_hbm.shape[0])
    ]
    for copy in copies:
        copy.start()
    for copy in copies:
        copy.wait()


def block_products(parts):
    times, extent = parts[0][0][0].shape
    zero = jnp.zeros_like(parts[0][0][1])
    depth = max(len(part) for part in parts)
    parts = [part + [(part[0][0], zero)] * (depth - len(part)) for part in parts]
    values = jnp.concatenate([jnp.concatenate([v for v, _ in part], axis=1) for part in parts], axis=0)
    blocks = jnp.concatenate([jnp.concatenate([c for _, c in part], axis=1) for part in parts], axis=0)
    product = lax.dot_general(values, blocks, (((1,), (1,)), ((), ())), preferred_element_type=jnp.float32)
    return [
        product[p * times : (p + 1) * times, p * extent : (p + 1) * extent] for p in range(len(parts))
    ]


def linear_section(side, columns_ref, compliance_ref, own0_ref, own1_ref, other0_ref, other1_ref, robin_ref, load_ref,
                   stiff_ref, record_ref, out_ref, half_ref):
    group, times, extent = own0_ref.shape
    rows = out_ref.shape[1]
    faces, stored = compliance_ref.shape[:2]
    first = first_face(side, group)
    mine = lax.axis_index("row")
    for run, refs in ((mine, (own0_ref, own1_ref)), (1 - mine, (other0_ref, other1_ref))):
        for part, ref in enumerate(refs):
            half_ref[pl.ds(run * faces + first_face(part, group), group)] = ref[...]

    def entries(face, begin, end):
        return [(half_ref[columns_ref[face, 0, j]], compliance_ref[face, j]) for j in range(begin, end)]

    def finish(index, product):
        lanes = lanes_of(first + index, extent)
        response = product + load_ref[:, lanes].astype(jnp.float32)
        out_ref[index, :times] = robin_ref[index] - 2.0 * response
        if rows > times:
            out_ref[index, times : times + 1] = stiff_ref[:, lanes]
            out_ref[index, times + 1 : times + 2] = record_ref[:, lanes]
            out_ref[index, times + 2 :] = jnp.zeros_like(out_ref[index, times + 2 :])

    for index in range(0, group - 1, 2):
        pair = block_products([entries(first + index + k, 0, stored) for k in range(2)])
        for k in range(2):
            finish(index + k, pair[k])
    if group % 2:
        face = first + group - 1
        cut = (stored + 3) // 4 * 2
        finish(group - 1, sum(block_products([entries(face, 0, cut), entries(face, cut, stored)])))


def running_peak(sizes):
    row = lax.broadcasted_iota(jnp.int32, sizes.shape, 0)
    step = 1
    while step < sizes.shape[0]:
        earlier = pltpu.roll(sizes, step, 0)
        sizes = jnp.maximum(sizes, jnp.where(row >= step, earlier, 0.0))
        step *= 2
    return sizes


def local_face(times, ascent, mate, turn, stiffness, record, live, begin):
    extent = ascent.shape[1]
    gather = functools.partial(jnp.take_along_axis, axis=1, mode="promise_in_bounds")
    mate_ascent = gather(mate[:times], jnp.broadcast_to(turn, (times, extent)))
    if begin:
        constants = gather(mate[times:], jnp.broadcast_to(turn, (SUBLANES, extent)))
        stiffness = 0.5 * (stiffness + constants[:1])
        record = jnp.maximum(record, constants[1:2])
    difference = ascent - mate_ascent
    jump = difference / (1.0 + 2.0 * stiffness)
    peak = jnp.maximum(record, running_peak(jnp.abs(jump)))
    damage = jnp.clip((peak - ONSET_JUMP) / (FAILURE_JUMP - ONSET_JUMP), 0.0, 1.0)
    effective = stiffness * (1.0 - damage)
    traction = jnp.where(live, effective * difference / (1.0 + 2.0 * effective), 0.0)
    return traction, traction - ascent, stiffness, record


def local_group(side, begin, partner_ref, turn_ref, own_ref, mate_ref, stiff_ref, record_ref, robin_ref, half_ref, *pair_refs):
    group, times, extent = robin_ref.shape
    first = first_face(side, group)
    for index in range(group):
        face = first + index
        partner = partner_ref[0, face]
        constants = lanes_of(face if begin else index, extent)
        traction, motion, stiffness, record = local_face(
            times, own_ref[index, :times], mate_ref[jnp.maximum(partner, 0)], turn_ref[:, lanes_of(face, extent)],
            stiff_ref[:, constants], record_ref[:, constants], partner >= 0, begin,
        )
        robin = traction + motion
        robin_ref[index] = robin
        half_ref[index] = robin.astype(jnp.bfloat16)
        if begin:
            pair_refs[0][:, lanes_of(index, extent)] = stiffness
            pair_refs[1][:, lanes_of(index, extent)] = record


def local_last(partner_ref, turn_ref, own0_ref, own1_ref, mate0_ref, mate1_ref, stiff0_ref, stiff1_ref,
               record0_ref, record1_ref, motion_ref, traction_ref):
    group, times, extent = own0_ref.shape
    for side, (own_ref, mate_ref, stiff_ref, record_ref) in enumerate((
        (own0_ref, mate0_ref, stiff0_ref, record0_ref), (own1_ref, mate1_ref, stiff1_ref, record1_ref),
    )):
        for index in range(group):
            face = first_face(side, group) + index
            lanes, constants = lanes_of(face, extent), lanes_of(index, extent)
            partner = partner_ref[0, face]
            traction, motion, _, _ = local_face(
                times, own_ref[index], mate_ref[jnp.maximum(partner, 0)], turn_ref[:, lanes],
                stiff_ref[:, constants], record_ref[:, constants], partner >= 0, False,
            )
            motion_ref[:, lanes] = motion.astype(jnp.bfloat16)
            traction_ref[:, lanes] = traction.astype(jnp.bfloat16)


def shards(
    compliance,
    block_columns,
    load_response,
    starting_motion,
    start_traction,
    stiffness,
    history,
    face_partner,
    orientation,
):
    _, faces, stored, extent, _ = compliance.shape
    times = starting_motion.shape[1]
    group = faces // 2
    subs = lax.axis_size("sub")
    rows = lax.axis_size("row")
    shifts = [[(s, (s + step) % subs) for s in range(subs)] for step in (1, -1)]
    swap = [(r, rows - 1 - r) for r in range(rows)]

    def f32(*shape):
        return jax.ShapeDtypeStruct(shape, jnp.float32)

    def bf16(*shape):
        return jax.ShapeDtypeStruct(shape, jnp.bfloat16)

    def s32(*shape):
        return jax.ShapeDtypeStruct(shape, jnp.int32)

    def call(kernel, in_specs, out_shape, scratch=(), moved=0, out_specs=()):
        outs = out_shape if isinstance(out_shape, tuple) else (out_shape,)
        out_specs = out_specs or (VMEM,) * len(outs)
        return pl.pallas_call(
            kernel,
            out_shape=out_shape,
            in_specs=in_specs,
            out_specs=out_specs if isinstance(out_shape, tuple) else out_specs[0],
            scratch_shapes=scratch,
            compiler_params=pltpu.CompilerParams(vmem_limit_bytes=VMEM_BYTES),
            cost_estimate=pl.CostEstimate(flops=moved, bytes_accessed=moved, transcendentals=0) if moved else None,
        )

    part = (group, times, extent)
    flat = (times, faces * extent)
    block_bytes = faces * stored * extent * extent * 2
    part_bytes = group * times * extent * 4
    robin0, robin1, half0, half1, load, stiff, record, turn, columns, partner = call(
        prepare, [HBM] * 8,
        (f32(*part), f32(*part), bf16(*part), bf16(*part), bf16(*flat), f32(1, faces * extent), f32(1, faces * extent),
         s32(1, faces * extent), pltpu.SMEM((faces, 1, stored), jnp.int32), pltpu.SMEM((1, faces), jnp.int32)),
        [pltpu.VMEM(flat, jnp.bfloat16), pltpu.VMEM(flat, jnp.bfloat16), pltpu.SemaphoreType.DMA((8,))],
        8 * part_bytes, (VMEM,) * 8 + (SMEM,) * 2,
    )(*(pltpu.with_memory_space_constraint(value, pltpu.HBM) for value in (
        starting_motion[0], start_traction[0], load_response[0], stiffness, history,
        orientation.reshape(1, -1), jnp.transpose(block_columns, (1, 0, 2)), face_partner,
    )))
    columns, partner = (pltpu.with_memory_space_constraint(table, pltpu.SMEM) for table in (columns, partner))
    blocks = call(
        fetch, [HBM], pltpu.VMEM((faces, stored, extent, extent), jnp.bfloat16),
        [pltpu.SemaphoreType.DMA((faces,))], block_bytes,
    )(pltpu.with_memory_space_constraint(compliance[0], pltpu.HBM))

    robin, half = [robin0, robin1], [half0, half1]
    stiffs, records = [stiff, stiff], [record, record]
    for iteration in range(ITERS):
        begin, last = iteration == 0, iteration == ITERS - 1
        other = [lax.ppermute(half[side], "row", swap) for side in range(2)]
        ascent, mates = [None, None], [None, None]
        for side in range(2):
            ascent[side] = call(
                functools.partial(linear_section, side),
                [SMEM] + [VMEM] * 9,
                f32(group, times + SUBLANES if begin else times, extent),
                [pltpu.VMEM((rows * faces, times, extent), jnp.bfloat16)],
                2 * block_bytes,
            )(columns, blocks, *half, *other, robin[side], load, stiff, record)
            mates[1 - side] = lax.ppermute(ascent[side], "sub", shifts[side])
        if last:
            return tuple(out[None] for out in call(
                local_last, [SMEM] + [VMEM] * 9, (bf16(*flat),) * 2,
            )(partner, turn, *ascent, *mates, *stiffs, *records))
        for side in (1, 0):
            outs = (f32(*part), bf16(*part))
            if begin:
                outs += (f32(1, group * extent),) * 2
            robin[side], half[side], *pair = call(
                functools.partial(local_group, side, begin), [SMEM] + [VMEM] * 5, outs,
            )(partner, turn, ascent[side], mates[side], stiffs[side], records[side])
            if begin:
                stiffs[side], records[side] = pair


def solution(mesh):
    in_specs = (
        P("sub", "row", None, None, None),
        P("sub", "row", None),
        P("sub", None, "row"),
        P("sub", None, "row"),
        P("sub", None, "row"),
        P("sub", "row"),
        P("sub", "row"),
        P("sub", "row"),
        P("sub", "row", None),
    )
    out_specs = (P("sub", None, "row"), P("sub", None, "row"))
    return jax.shard_map(shards, mesh=mesh, in_specs=in_specs, out_specs=out_specs, check_vma=False)
```

```python
import functools

import jax
import jax.numpy as jnp
from jax import lax
from jax.experimental import pallas as pl
from jax.experimental.pallas import tpu as pltpu
from jax.sharding import PartitionSpec as P

ITERS = 3
SUBLANES = 8
VMEM_BYTES = 24 * 2**20

ONSET_JUMP = 0.15
FAILURE_JUMP = 1.5

VMEM = pl.BlockSpec(memory_space=pltpu.VMEM)
SMEM = pl.BlockSpec(memory_space=pltpu.SMEM)
HBM = pl.BlockSpec(memory_space=pltpu.HBM)


def position(group):
    near = group * (lax.axis_index("sub") % 2)
    return near, group - near, lax.axis_index("row")


def lanes_of(face, extent):
    return pl.ds(pl.multiple_of(face * extent, extent), extent)


def prepare(motion_hbm, stress_hbm, load_hbm, stiff_hbm, record_hbm, turn_hbm, columns_hbm, partner_hbm,
            robin0_ref, robin1_ref, half0_ref, half1_ref, load_ref, stiff_ref, record_ref, turn_ref, columns_ref, partner_ref,
            motion_ref, stress_ref, sems):
    pairs = (
        (motion_hbm, motion_ref), (stress_hbm, stress_ref), (load_hbm, load_ref), (stiff_hbm, stiff_ref),
        (record_hbm, record_ref), (turn_hbm, turn_ref), (columns_hbm, columns_ref), (partner_hbm, partner_ref),
    )
    copies = [pltpu.make_async_copy(source, target, sems.at[n]) for n, (source, target) in enumerate(pairs)]
    for copy in copies:
        copy.start()
    for copy in copies[:2]:
        copy.wait()
    group, _, extent = robin0_ref.shape
    starts = position(group)
    for side, (robin_ref, half_ref) in enumerate(((robin0_ref, half0_ref), (robin1_ref, half1_ref))):
        for index in range(group):
            lanes = lanes_of(starts[side] + index, extent)
            robin = stress_ref[:, lanes].astype(jnp.float32) + motion_ref[:, lanes].astype(jnp.float32)
            robin_ref[index] = robin
            half_ref[index] = robin.astype(jnp.bfloat16)
    for copy in copies[2:]:
        copy.wait()


def fetch(blocks_hbm, blocks_ref, sems):
    copies = [
        pltpu.make_async_copy(blocks_hbm.at[face], blocks_ref.at[face], sems.at[face])
        for face in range(blocks_hbm.shape[0])
    ]
    for copy in copies:
        copy.start()
    for copy in copies:
        copy.wait()


def block_products(parts):
    times, extent = parts[0][0][0].shape
    zero = jnp.zeros_like(parts[0][0][1])
    depth = max(len(part) for part in parts)
    parts = [part + [(part[0][0], zero)] * (depth - len(part)) for part in parts]
    values = jnp.concatenate([jnp.concatenate([v for v, _ in part], axis=1) for part in parts], axis=0)
    blocks = jnp.concatenate([jnp.concatenate([c for _, c in part], axis=1) for part in parts], axis=0)
    product = lax.dot_general(values, blocks, (((1,), (1,)), ((), ())), preferred_element_type=jnp.float32)
    return [
        product[p * times : (p + 1) * times, p * extent : (p + 1) * extent] for p in range(len(parts))
    ]


def linear_section(side, columns_ref, compliance_ref, own0_ref, own1_ref, other0_ref, other1_ref, robin_ref, load_ref,
                   stiff_ref, record_ref, out_ref, half_ref):
    group, times, extent = own0_ref.shape
    rows = out_ref.shape[1]
    faces, stored = compliance_ref.shape[:2]
    *starts, mine = position(group)
    first = starts[side]
    for run, refs in ((mine, (own0_ref, own1_ref)), (1 - mine, (other0_ref, other1_ref))):
        for start, ref in zip(starts, refs):
            half_ref[pl.ds(run * faces + start, group)] = ref[...]

    def entries(face, begin, end):
        return [(half_ref[columns_ref[face, 0, j]], compliance_ref[face, j]) for j in range(begin, end)]

    def finish(index, product):
        lanes = lanes_of(first + index, extent)
        response = product + load_ref[:, lanes].astype(jnp.float32)
        out_ref[index, :times] = robin_ref[index] - 2.0 * response
        if rows > times:
            out_ref[index, times : times + 1] = stiff_ref[:, lanes]
            out_ref[index, times + 1 : times + 2] = record_ref[:, lanes]
            out_ref[index, times + 2 :] = jnp.zeros_like(out_ref[index, times + 2 :])

    for index in range(0, group - 1, 2):
        pair = block_products([entries(first + index + k, 0, stored) for k in range(2)])
        for k in range(2):
            finish(index + k, pair[k])
    for spare in range(group, out_ref.shape[0]):
        out_ref[spare] = jnp.zeros_like(out_ref[spare])
    if group % 2:
        face = first + group - 1
        cut = (stored + 3) // 4 * 2
        finish(group - 1, sum(block_products([entries(face, 0, cut), entries(face, cut, stored)])))


def running_peak(sizes):
    row = lax.broadcasted_iota(jnp.int32, sizes.shape, 0)
    step = 1
    while step < sizes.shape[0]:
        earlier = pltpu.roll(sizes, step, 0)
        sizes = jnp.maximum(sizes, jnp.where(row >= step, earlier, 0.0))
        step *= 2
    return sizes


def local_face(times, ascent, mate, turn, stiffness, record, live, begin):
    extent = ascent.shape[1]
    gather = functools.partial(jnp.take_along_axis, axis=1, mode="promise_in_bounds")
    mate_ascent = gather(mate[:times], jnp.broadcast_to(turn, (times, extent)))
    if begin:
        constants = gather(mate[times:], jnp.broadcast_to(turn, (SUBLANES, extent)))
        stiffness = 0.5 * (stiffness + constants[:1])
        record = jnp.maximum(record, constants[1:2])
    difference = ascent - mate_ascent
    jump = difference / (1.0 + 2.0 * stiffness)
    peak = jnp.maximum(record, running_peak(jnp.abs(jump)))
    damage = jnp.clip((peak - ONSET_JUMP) / (FAILURE_JUMP - ONSET_JUMP), 0.0, 1.0)
    effective = stiffness * (1.0 - damage)
    traction = jnp.where(live, effective * difference / (1.0 + 2.0 * effective), 0.0)
    return traction, traction - ascent, stiffness, record


def local_group(side, begin, partner_ref, turn_ref, own_ref, mate_ref, stiff_ref, record_ref, robin_ref, half_ref, *pair_refs):
    group, times, extent = robin_ref.shape
    first = position(group)[side]
    for index in range(group):
        face = first + index
        partner = partner_ref[0, face]
        constants = lanes_of(face if begin else index, extent)
        traction, motion, stiffness, record = local_face(
            times, own_ref[index, :times], mate_ref[jnp.maximum(partner, 0)], turn_ref[:, lanes_of(face, extent)],
            stiff_ref[:, constants], record_ref[:, constants], partner >= 0, begin,
        )
        robin = traction + motion
        robin_ref[index] = robin
        half_ref[index] = robin.astype(jnp.bfloat16)
        if begin:
            pair_refs[0][:, lanes_of(index, extent)] = stiffness
            pair_refs[1][:, lanes_of(index, extent)] = record


def local_last(partner_ref, turn_ref, own0_ref, own1_ref, mate0_ref, mate1_ref, stiff0_ref, stiff1_ref,
               record0_ref, record1_ref, motion_ref, traction_ref):
    group, times, extent = own0_ref.shape
    starts = position(group)
    for side, (own_ref, mate_ref, stiff_ref, record_ref) in enumerate((
        (own0_ref, mate0_ref, stiff0_ref, record0_ref), (own1_ref, mate1_ref, stiff1_ref, record1_ref),
    )):
        for index in range(group):
            face = starts[side] + index
            lanes, constants = lanes_of(face, extent), lanes_of(index, extent)
            partner = partner_ref[0, face]
            traction, motion, _, _ = local_face(
                times, own_ref[index], mate_ref[jnp.maximum(partner, 0)], turn_ref[:, lanes],
                stiff_ref[:, constants], record_ref[:, constants], partner >= 0, False,
            )
            motion_ref[:, lanes] = motion.astype(jnp.bfloat16)
            traction_ref[:, lanes] = traction.astype(jnp.bfloat16)


def shards(
    compliance,
    block_columns,
    load_response,
    starting_motion,
    start_traction,
    stiffness,
    history,
    face_partner,
    orientation,
):
    _, faces, stored, extent, _ = compliance.shape
    times = starting_motion.shape[1]
    group = faces // 2
    subs = lax.axis_size("sub")
    rows = lax.axis_size("row")
    near_pairs = [(s, s ^ 1) for s in range(subs)]
    far_pairs = []
    for s in range(subs):
        mate = s - 1 if s % 2 == 0 else s + 1
        for r in range(rows):
            there = mate * rows + r if 0 <= mate < subs else s * rows + rows - 1 - r
            far_pairs.append((s * rows + r, there))
    swap = [(r, rows - 1 - r) for r in range(rows)]

    def f32(*shape):
        return jax.ShapeDtypeStruct(shape, jnp.float32)

    def bf16(*shape):
        return jax.ShapeDtypeStruct(shape, jnp.bfloat16)

    def s32(*shape):
        return jax.ShapeDtypeStruct(shape, jnp.int32)

    def call(kernel, in_specs, out_shape, scratch=(), moved=0, out_specs=()):
        outs = out_shape if isinstance(out_shape, tuple) else (out_shape,)
        out_specs = out_specs or (VMEM,) * len(outs)
        return pl.pallas_call(
            kernel,
            out_shape=out_shape,
            in_specs=in_specs,
            out_specs=out_specs if isinstance(out_shape, tuple) else out_specs[0],
            scratch_shapes=scratch,
            compiler_params=pltpu.CompilerParams(vmem_limit_bytes=VMEM_BYTES),
            cost_estimate=pl.CostEstimate(flops=moved, bytes_accessed=moved, transcendentals=0) if moved else None,
        )

    part = (group, times, extent)
    flat = (times, faces * extent)
    block_bytes = faces * stored * extent * extent * 2
    part_bytes = group * times * extent * 4
    robin0, robin1, half0, half1, load, stiff, record, turn, columns, partner = call(
        prepare, [HBM] * 8,
        (f32(*part), f32(*part), bf16(*part), bf16(*part), bf16(*flat), f32(1, faces * extent), f32(1, faces * extent),
         s32(1, faces * extent), pltpu.SMEM((faces, 1, stored), jnp.int32), pltpu.SMEM((1, faces), jnp.int32)),
        [pltpu.VMEM(flat, jnp.bfloat16), pltpu.VMEM(flat, jnp.bfloat16), pltpu.SemaphoreType.DMA((8,))],
        8 * part_bytes, (VMEM,) * 8 + (SMEM,) * 2,
    )(*(pltpu.with_memory_space_constraint(value, pltpu.HBM) for value in (
        starting_motion[0], start_traction[0], load_response[0], stiffness, history,
        orientation.reshape(1, -1), jnp.transpose(block_columns, (1, 0, 2)), face_partner,
    )))
    columns, partner = (pltpu.with_memory_space_constraint(table, pltpu.SMEM) for table in (columns, partner))
    blocks = call(
        fetch, [HBM], pltpu.VMEM((faces, stored, extent, extent), jnp.bfloat16),
        [pltpu.SemaphoreType.DMA((faces,))], block_bytes,
    )(pltpu.with_memory_space_constraint(compliance[0], pltpu.HBM))

    robin, half = [robin0, robin1], [half0, half1]
    stiffs, records = [stiff, stiff], [record, record]
    for iteration in range(ITERS):
        begin, last = iteration == 0, iteration == ITERS - 1
        other = [lax.ppermute(half[side], "row", swap) for side in range(2)]
        ascent, mates = [None, None], [None, None]
        for side, (axes, pairs) in enumerate((("sub", near_pairs), (("sub", "row"), far_pairs))):
            ascent[side] = call(
                functools.partial(linear_section, side),
                [SMEM] + [VMEM] * 9,
                f32(group + side, times + SUBLANES if begin else times, extent),
                [pltpu.VMEM((rows * faces, times, extent), jnp.bfloat16)],
                2 * block_bytes,
            )(columns, blocks, *half, *other, robin[side], load, stiff, record)
            mates[side] = lax.ppermute(ascent[side], axes, pairs)
        if last:
            return tuple(out[None] for out in call(
                local_last, [SMEM] + [VMEM] * 9, (bf16(*flat),) * 2,
            )(partner, turn, *ascent, *mates, *stiffs, *records))
        for side in range(2):
            outs = (f32(*part), bf16(*part))
            if begin:
                outs += (f32(1, group * extent),) * 2
            robin[side], half[side], *pair = call(
                functools.partial(local_group, side, begin), [SMEM] + [VMEM] * 5, outs,
            )(partner, turn, ascent[side], mates[side], stiffs[side], records[side])
            if begin:
                stiffs[side], records[side] = pair


def solution(mesh):
    in_specs = (
        P("sub", "row", None, None, None),
        P("sub", "row", None),
        P("sub", None, "row"),
        P("sub", None, "row"),
        P("sub", None, "row"),
        P("sub", "row"),
        P("sub", "row"),
        P("sub", "row"),
        P("sub", "row", None),
    )
    out_specs = (P("sub", None, "row"), P("sub", None, "row"))
    return jax.shard_map(shards, mesh=mesh, in_specs=in_specs, out_specs=out_specs, check_vma=False)
```

```python
import functools

import jax
import jax.numpy as jnp
from jax import lax
from jax.experimental import pallas as pl
from jax.experimental.pallas import tpu as pltpu
from jax.sharding import PartitionSpec as P

ITERS = 3
SUBLANES = 8
VMEM_BYTES = 24 * 2**20

ONSET_JUMP = 0.15
FAILURE_JUMP = 1.5

VMEM = pl.BlockSpec(memory_space=pltpu.VMEM)
SMEM = pl.BlockSpec(memory_space=pltpu.SMEM)
HBM = pl.BlockSpec(memory_space=pltpu.HBM)


def position(group):
    near = group * (lax.axis_index("sub") % 2)
    return near, group - near, lax.axis_index("row")


def lanes_of(face, extent):
    return pl.ds(pl.multiple_of(face * extent, extent), extent)


def prepare(early, motion_hbm, stress_hbm, blocks_hbm, robin0_ref, robin1_ref, half_ref, blocks_ref,
            motion_ref, stress_ref, sems):
    copies = [
        pltpu.make_async_copy(motion_hbm, motion_ref, sems.at[0]),
        pltpu.make_async_copy(stress_hbm, stress_ref, sems.at[1]),
        pltpu.make_async_copy(blocks_hbm.at[:early], blocks_ref.at[:early], sems.at[2]),
    ]
    for copy in copies:
        copy.start()
    for copy in copies[:2]:
        copy.wait()
    group, _, extent = robin0_ref.shape
    starts = position(group)
    for side, robin_ref in enumerate((robin0_ref, robin1_ref)):
        for index in range(group):
            lanes = lanes_of(starts[side] + index, extent)
            robin = stress_ref[:, lanes].astype(jnp.float32) + motion_ref[:, lanes].astype(jnp.float32)
            robin_ref[index] = robin
            half_ref[side * group + index] = robin.astype(jnp.bfloat16)
    copies[2].wait()


def fetch(early, blocks_in_ref, blocks_hbm, load_hbm, stiff_hbm, record_hbm, turn_hbm, columns_hbm, partner_hbm,
          blocks_ref, load_ref, stiff_ref, record_ref, turn_ref, columns_ref, partner_ref, sems):
    pairs = [
        (load_hbm, load_ref), (stiff_hbm, stiff_ref), (record_hbm, record_ref),
        (turn_hbm, turn_ref), (columns_hbm, columns_ref), (partner_hbm, partner_ref),
    ]
    pairs += [(blocks_hbm.at[face], blocks_ref.at[face]) for face in range(early, blocks_hbm.shape[0])]
    copies = [pltpu.make_async_copy(source, target, sems.at[n]) for n, (source, target) in enumerate(pairs)]
    for copy in copies:
        copy.start()
    for copy in copies:
        copy.wait()


def block_products(parts):
    times, extent = parts[0][0][0].shape
    zero = jnp.zeros_like(parts[0][0][1])
    depth = max(len(part) for part in parts)
    parts = [part + [(part[0][0], zero)] * (depth - len(part)) for part in parts]
    values = jnp.concatenate([jnp.concatenate([v for v, _ in part], axis=1) for part in parts], axis=0)
    blocks = jnp.concatenate([jnp.concatenate([c for _, c in part], axis=1) for part in parts], axis=0)
    product = lax.dot_general(values, blocks, (((1,), (1,)), ((), ())), preferred_element_type=jnp.float32)
    return [
        product[p * times : (p + 1) * times, p * extent : (p + 1) * extent] for p in range(len(parts))
    ]


def linear_section(side, columns_ref, compliance_ref, own_ref, other_ref, robin_ref, load_ref,
                   stiff_ref, record_ref, out_ref, half_ref):
    group, times, extent = robin_ref.shape
    rows = out_ref.shape[1]
    faces, stored = compliance_ref.shape[:2]
    *starts, mine = position(group)
    first = starts[side]
    for run, ref in ((mine, own_ref), (1 - mine, other_ref)):
        for part, start in enumerate(starts):
            half_ref[pl.ds(run * faces + start, group)] = ref[part * group : (part + 1) * group]

    def entries(face, begin, end):
        return [(half_ref[columns_ref[face, 0, j]], compliance_ref[face, j]) for j in range(begin, end)]

    def finish(index, product):
        lanes = lanes_of(first + index, extent)
        response = product + load_ref[:, lanes].astype(jnp.float32)
        out_ref[index, :times] = robin_ref[index] - 2.0 * response
        if rows > times:
            out_ref[index, times : times + 1] = stiff_ref[:, lanes]
            out_ref[index, times + 1 : times + 2] = record_ref[:, lanes]
            out_ref[index, times + 2 :] = jnp.zeros_like(out_ref[index, times + 2 :])

    for index in range(0, group - 1, 2):
        pair = block_products([entries(first + index + k, 0, stored) for k in range(2)])
        for k in range(2):
            finish(index + k, pair[k])
    for spare in range(group, out_ref.shape[0]):
        out_ref[spare] = jnp.zeros_like(out_ref[spare])
    if group % 2:
        face = first + group - 1
        cut = (stored + 3) // 4 * 2
        finish(group - 1, sum(block_products([entries(face, 0, cut), entries(face, cut, stored)])))


def running_peak(sizes):
    row = lax.broadcasted_iota(jnp.int32, sizes.shape, 0)
    step = 1
    while step < sizes.shape[0]:
        earlier = pltpu.roll(sizes, step, 0)
        sizes = jnp.maximum(sizes, jnp.where(row >= step, earlier, 0.0))
        step *= 2
    return sizes


def local_face(times, ascent, mate, turn, stiffness, record, live, begin):
    extent = ascent.shape[1]
    gather = functools.partial(jnp.take_along_axis, axis=1, mode="promise_in_bounds")
    mate_ascent = gather(mate[:times], jnp.broadcast_to(turn, (times, extent)))
    if begin:
        constants = gather(mate[times:], jnp.broadcast_to(turn, (SUBLANES, extent)))
        stiffness = 0.5 * (stiffness + constants[:1])
        record = jnp.maximum(record, constants[1:2])
    difference = ascent - mate_ascent
    jump = difference / (1.0 + 2.0 * stiffness)
    peak = jnp.maximum(record, running_peak(jnp.abs(jump)))
    damage = jnp.clip((peak - ONSET_JUMP) / (FAILURE_JUMP - ONSET_JUMP), 0.0, 1.0)
    effective = stiffness * (1.0 - damage)
    traction = jnp.where(live, effective * difference / (1.0 + 2.0 * effective), 0.0)
    return traction, traction - ascent, stiffness, record


def local_group(side, begin, partner_ref, turn_ref, own_ref, mate_ref, stiff_ref, record_ref, *refs):
    if side:
        near_ref, robin_ref, half_ref, *pair_refs = refs
    else:
        robin_ref, half_ref, *pair_refs = refs
    group, times, extent = robin_ref.shape
    first = position(group)[side]
    if side:
        half_ref[:group] = near_ref[...]
    for index in range(group):
        face = first + index
        partner = partner_ref[0, face]
        constants = lanes_of(face if begin else index, extent)
        traction, motion, stiffness, record = local_face(
            times, own_ref[index, :times], mate_ref[jnp.maximum(partner, 0)], turn_ref[:, lanes_of(face, extent)],
            stiff_ref[:, constants], record_ref[:, constants], partner >= 0, begin,
        )
        robin = traction + motion
        robin_ref[index] = robin
        half_ref[side * group + index] = robin.astype(jnp.bfloat16)
        if begin:
            pair_refs[0][:, lanes_of(index, extent)] = stiffness
            pair_refs[1][:, lanes_of(index, extent)] = record


def local_last(partner_ref, turn_ref, own0_ref, own1_ref, mate0_ref, mate1_ref, stiff0_ref, stiff1_ref,
               record0_ref, record1_ref, motion_ref, traction_ref):
    group, times, extent = own0_ref.shape
    starts = position(group)
    for side, (own_ref, mate_ref, stiff_ref, record_ref) in enumerate((
        (own0_ref, mate0_ref, stiff0_ref, record0_ref), (own1_ref, mate1_ref, stiff1_ref, record1_ref),
    )):
        for index in range(group):
            face = starts[side] + index
            lanes, constants = lanes_of(face, extent), lanes_of(index, extent)
            partner = partner_ref[0, face]
            traction, motion, _, _ = local_face(
                times, own_ref[index], mate_ref[jnp.maximum(partner, 0)], turn_ref[:, lanes],
                stiff_ref[:, constants], record_ref[:, constants], partner >= 0, False,
            )
            motion_ref[:, lanes] = motion.astype(jnp.bfloat16)
            traction_ref[:, lanes] = traction.astype(jnp.bfloat16)


def shards(
    compliance,
    block_columns,
    load_response,
    starting_motion,
    start_traction,
    stiffness,
    history,
    face_partner,
    orientation,
):
    _, faces, stored, extent, _ = compliance.shape
    times = starting_motion.shape[1]
    group = faces // 2
    subs = lax.axis_size("sub")
    rows = lax.axis_size("row")
    near_pairs = [(s, s ^ 1) for s in range(subs)]
    far_pairs = []
    for s in range(subs):
        mate = s - 1 if s % 2 == 0 else s + 1
        for r in range(rows):
            there = mate * rows + r if 0 <= mate < subs else s * rows + rows - 1 - r
            far_pairs.append((s * rows + r, there))
    swap = [(r, rows - 1 - r) for r in range(rows)]

    def f32(*shape):
        return jax.ShapeDtypeStruct(shape, jnp.float32)

    def bf16(*shape):
        return jax.ShapeDtypeStruct(shape, jnp.bfloat16)

    def s32(*shape):
        return jax.ShapeDtypeStruct(shape, jnp.int32)

    def call(kernel, in_specs, out_shape, scratch=(), moved=0, out_specs=(), aliases={}):
        outs = out_shape if isinstance(out_shape, tuple) else (out_shape,)
        out_specs = out_specs or (VMEM,) * len(outs)
        return pl.pallas_call(
            kernel,
            out_shape=out_shape,
            in_specs=in_specs,
            out_specs=out_specs if isinstance(out_shape, tuple) else out_specs[0],
            scratch_shapes=scratch,
            input_output_aliases=aliases,
            compiler_params=pltpu.CompilerParams(vmem_limit_bytes=VMEM_BYTES),
            cost_estimate=pl.CostEstimate(flops=moved, bytes_accessed=moved, transcendentals=0) if moved else None,
        )

    part = (group, times, extent)
    flat = (times, faces * extent)
    block_bytes = faces * stored * extent * extent * 2
    part_bytes = group * times * extent * 4
    every = (faces, stored, extent, extent)
    early = faces // 6
    in_hbm = functools.partial(pltpu.with_memory_space_constraint, memory_space=pltpu.HBM)
    robin0, robin1, half, blocks = call(
        functools.partial(prepare, early), [HBM] * 3,
        (f32(*part), f32(*part), bf16(faces, times, extent), pltpu.VMEM(every, jnp.bfloat16)),
        [pltpu.VMEM(flat, jnp.bfloat16), pltpu.VMEM(flat, jnp.bfloat16), pltpu.SemaphoreType.DMA((3,))],
        8 * part_bytes,
    )(in_hbm(starting_motion[0]), in_hbm(start_traction[0]), in_hbm(compliance[0]))
    blocks, load, stiff, record, turn, columns, partner = call(
        functools.partial(fetch, early), [VMEM] + [HBM] * 7,
        (pltpu.VMEM(every, jnp.bfloat16), bf16(*flat), f32(1, faces * extent), f32(1, faces * extent),
         s32(1, faces * extent), pltpu.SMEM((faces, 1, stored), jnp.int32), pltpu.SMEM((1, faces), jnp.int32)),
        [pltpu.SemaphoreType.DMA((6 + faces - early,))],
        block_bytes, (VMEM,) * 5 + (SMEM,) * 2, {0: 0},
    )(
        pltpu.with_memory_space_constraint(blocks, pltpu.VMEM), in_hbm(compliance[0]), in_hbm(load_response[0]),
        in_hbm(stiffness), in_hbm(history), in_hbm(orientation.reshape(1, -1)),
        in_hbm(jnp.transpose(block_columns, (1, 0, 2))), in_hbm(face_partner),
    )
    columns, partner = (pltpu.with_memory_space_constraint(table, pltpu.SMEM) for table in (columns, partner))

    robin = [robin0, robin1]
    stiffs, records = [stiff, stiff], [record, record]
    for iteration in range(ITERS):
        begin, last = iteration == 0, iteration == ITERS - 1
        other = lax.ppermute(half, "row", swap)
        ascent, mates = [None, None], [None, None]
        for side, (axes, pairs) in enumerate((("sub", near_pairs), (("sub", "row"), far_pairs))):
            ascent[side] = call(
                functools.partial(linear_section, side),
                [SMEM] + [VMEM] * 7,
                f32(group + side, times + SUBLANES if begin else times, extent),
                [pltpu.VMEM((rows * faces, times, extent), jnp.bfloat16)],
                2 * block_bytes,
            )(columns, blocks, half, other, robin[side], load, stiff, record)
            mates[side] = lax.ppermute(ascent[side], axes, pairs)
        if last:
            return tuple(out[None] for out in call(
                local_last, [SMEM] + [VMEM] * 9, (bf16(*flat),) * 2,
            )(partner, turn, *ascent, *mates, *stiffs, *records))
        for side in range(2):
            outs = (f32(*part), bf16(faces if side else group, times, extent))
            if begin:
                outs += (f32(1, group * extent),) * 2
            near = (half,) if side else ()
            robin[side], half, *pair = call(
                functools.partial(local_group, side, begin), [SMEM] + [VMEM] * (5 + side), outs,
            )(partner, turn, ascent[side], mates[side], stiffs[side], records[side], *near)
            if begin:
                stiffs[side], records[side] = pair


def solution(mesh):
    in_specs = (
        P("sub", "row", None, None, None),
        P("sub", "row", None),
        P("sub", None, "row"),
        P("sub", None, "row"),
        P("sub", None, "row"),
        P("sub", "row"),
        P("sub", "row"),
        P("sub", "row"),
        P("sub", "row", None),
    )
    out_specs = (P("sub", None, "row"), P("sub", None, "row"))
    return jax.shard_map(shards, mesh=mesh, in_specs=in_specs, out_specs=out_specs, check_vma=False)
```

```python
import functools

import jax
import jax.numpy as jnp
from jax import lax
from jax.experimental import pallas as pl
from jax.experimental.pallas import tpu as pltpu
from jax.sharding import PartitionSpec as P

ITERS = 3
SUBLANES = 8
EARLY = (6, 10)
VMEM_BYTES = 24 * 2**20

ONSET_JUMP = 0.15
FAILURE_JUMP = 1.5

VMEM = pl.BlockSpec(memory_space=pltpu.VMEM)
SMEM = pl.BlockSpec(memory_space=pltpu.SMEM)
ANY = pl.BlockSpec(memory_space=pl.ANY)
HBM = pl.BlockSpec(memory_space=pltpu.HBM)


def position(group):
    near = group * (lax.axis_index("sub") % 2)
    return near, group - near, lax.axis_index("row")


def lanes_of(face, extent):
    return pl.ds(pl.multiple_of(face * extent, extent), extent)


def prepare(motion_hbm, stress_hbm, robin0_ref, robin1_ref, half0_ref, half1_ref, motion_ref, stress_ref, sems):
    copies = [
        pltpu.make_async_copy(motion_hbm, motion_ref, sems.at[0]),
        pltpu.make_async_copy(stress_hbm, stress_ref, sems.at[1]),
    ]
    for copy in copies:
        copy.start()
    for copy in copies:
        copy.wait()
    group, _, extent = robin0_ref.shape
    starts = position(group)
    for side, (robin_ref, half_ref) in enumerate(((robin0_ref, half0_ref), (robin1_ref, half1_ref))):
        for index in range(group):
            lanes = lanes_of(starts[side] + index, extent)
            robin = stress_ref[:, lanes].astype(jnp.float32) + motion_ref[:, lanes].astype(jnp.float32)
            robin_ref[index] = robin
            half_ref[index] = robin.astype(jnp.bfloat16)


def sort_blocks(columns_ref, order_ref, sorted_ref, ready_ref):
    faces, _, stored = columns_ref.shape
    group = faces // 2
    near, far, mine = position(group)
    own = mine * faces
    partner = (1 - mine) * faces + near

    def sort_row(face, _):
        in_far = (face >= far) & (face < far + group)
        width = jnp.where(in_far, group, 0)
        front, back = jnp.int32(0), jnp.int32(stored - 1)
        for j in range(stored):
            column = columns_ref[face, 0, j]
            early = ((column >= own) & (column < own + faces)) | ((column >= partner) & (column < partner + width))
            place = jnp.where(early, front, back)
            order_ref[face, 0, place] = j
            sorted_ref[face, 0, place] = column
            front = jnp.where(early, front + 1, front)
            back = jnp.where(early, back, back - 1)
        ready_ref[0, face] = front
        return 0

    lax.fori_loop(0, faces, sort_row, 0)


def fetch(blocks_hbm, load_hbm, stiff_hbm, record_hbm, turn_hbm, columns_hbm, partner_hbm,
          blocks_ref, load_ref, stiff_ref, record_ref, turn_ref, partner_ref, order_ref, sorted_ref, ready_ref,
          columns_ref, sems):
    pairs = [
        (columns_hbm, columns_ref), (load_hbm, load_ref), (stiff_hbm, stiff_ref), (record_hbm, record_ref),
        (turn_hbm, turn_ref), (partner_hbm, partner_ref),
    ]
    pairs += [(blocks_hbm.at[face], blocks_ref.at[face]) for face in range(blocks_hbm.shape[0])]
    copies = [pltpu.make_async_copy(source, target, sems.at[n]) for n, (source, target) in enumerate(pairs)]
    for copy in copies:
        copy.start()
    copies[0].wait()
    sort_blocks(columns_ref, order_ref, sorted_ref, ready_ref)
    for copy in copies[1:]:
        copy.wait()


def block_products(parts):
    times, extent = parts[0][0][0].shape
    zero = jnp.zeros_like(parts[0][0][1])
    depth = max(len(part) for part in parts)
    parts = [part + [(part[0][0], zero)] * (depth - len(part)) for part in parts]
    values = jnp.concatenate([jnp.concatenate([v for v, _ in part], axis=1) for part in parts], axis=0)
    blocks = jnp.concatenate([jnp.concatenate([c for _, c in part], axis=1) for part in parts], axis=0)
    product = lax.dot_general(values, blocks, (((1,), (1,)), ((), ())), preferred_element_type=jnp.float32)
    return [
        product[p * times : (p + 1) * times, p * extent : (p + 1) * extent] for p in range(len(parts))
    ]


def group_products(first, group, entries, finish):
    for index in range(0, group - 1, 2):
        pair = block_products([entries(first + index + k) for k in range(2)])
        for k in range(2):
            finish(index + k, pair[k])
    if group % 2:
        whole = entries(first + group - 1)
        cut = (len(whole) + 3) // 4 * 2
        finish(group - 1, sum(block_products([whole[:cut], whole[cut:]])))


def early_products(side, order_ref, sorted_ref, ready_ref, compliance_ref, own0_ref, own1_ref, *refs):
    out_ref, half_ref = refs[-2:]
    group, times, _ = out_ref.shape
    faces = compliance_ref.shape[0]
    *starts, mine = position(group)
    none = half_ref.shape[0] - 1
    half_ref[none] = jnp.zeros_like(half_ref[none])
    for start, ref in zip(starts, (own0_ref, own1_ref)):
        half_ref[pl.ds(mine * faces + start, group)] = ref[...]
    for ref in refs[:side]:
        half_ref[pl.ds((1 - mine) * faces + starts[0], group)] = ref[...]

    def entries(face):
        ready = ready_ref[0, face]
        return [
            (half_ref[jnp.where(slot < ready, sorted_ref[face, 0, slot], none)], compliance_ref[face, order_ref[face, 0, slot]])
            for slot in range(EARLY[side])
        ]

    def finish(index, product):
        out_ref[index] = product

    group_products(starts[side], group, entries, finish)


def linear_section(side, begin, order_ref, sorted_ref, ready_ref, compliance_ref, own0_ref, own1_ref, other0_ref, other1_ref,
                   robin_ref, load_ref, *refs):
    out_ref, half_ref = refs[-2:]
    group, times, extent = own0_ref.shape
    rows = out_ref.shape[1]
    faces, stored = compliance_ref.shape[:2]
    *starts, mine = position(group)
    first = starts[side]
    done = 0 if begin else EARLY[side]
    for run, parts in ((mine, (own0_ref, own1_ref)), (1 - mine, (other0_ref, other1_ref))):
        for start, ref in zip(starts, parts):
            half_ref[pl.ds(run * faces + start, group)] = ref[...]

    def entry(face, slot):
        return half_ref[sorted_ref[face, 0, slot]], compliance_ref[face, order_ref[face, 0, slot]]

    def entries(face):
        return [entry(face, slot) for slot in range(done, stored)]

    def finish(index, product):
        lanes = lanes_of(first + index, extent)
        response = product + load_ref[:, lanes].astype(jnp.float32)
        if done:
            response = response + refs[0][index]
        out_ref[index, :times] = robin_ref[index] - 2.0 * response
        if begin:
            out_ref[index, times : times + 1] = refs[0][:, lanes]
            out_ref[index, times + 1 : times + 2] = refs[1][:, lanes]
            out_ref[index, times + 2 :] = jnp.zeros_like(out_ref[index, times + 2 :])

    group_products(first, group, entries, finish)
    for spare in range(group, out_ref.shape[0]):
        out_ref[spare] = jnp.zeros_like(out_ref[spare])
    if done:
        def missed(slot, index):
            values, block = entry(first + index, slot)
            out_ref[index, :times] -= 2.0 * block_products([[(values, block)]])[0]
            return index

        least = ready_ref[0, first]
        for index in range(1, group):
            least = jnp.minimum(least, ready_ref[0, first + index])

        @pl.when(least < done)
        def _():
            for index in range(group):
                lax.fori_loop(ready_ref[0, first + index], done, missed, index)


def running_peak(sizes):
    row = lax.broadcasted_iota(jnp.int32, sizes.shape, 0)
    step = 1
    while step < sizes.shape[0]:
        earlier = pltpu.roll(sizes, step, 0)
        sizes = jnp.maximum(sizes, jnp.where(row >= step, earlier, 0.0))
        step *= 2
    return sizes


def local_face(times, ascent, mate, turn, stiffness, record, live, begin):
    extent = ascent.shape[1]
    gather = functools.partial(jnp.take_along_axis, axis=1, mode="promise_in_bounds")
    mate_ascent = gather(mate[:times], jnp.broadcast_to(turn, (times, extent)))
    if begin:
        constants = gather(mate[times:], jnp.broadcast_to(turn, (SUBLANES, extent)))
        stiffness = 0.5 * (stiffness + constants[:1])
        record = jnp.maximum(record, constants[1:2])
    difference = ascent - mate_ascent
    jump = difference / (1.0 + 2.0 * stiffness)
    peak = jnp.maximum(record, running_peak(jnp.abs(jump)))
    damage = jnp.clip((peak - ONSET_JUMP) / (FAILURE_JUMP - ONSET_JUMP), 0.0, 1.0)
    effective = stiffness * (1.0 - damage)
    traction = jnp.where(live, effective * difference / (1.0 + 2.0 * effective), 0.0)
    return traction, traction - ascent, stiffness, record


def local_group(side, begin, partner_ref, turn_ref, own_ref, mate_ref, stiff_ref, record_ref, robin_ref, half_ref, *pair_refs):
    group, times, extent = robin_ref.shape
    first = position(group)[side]
    for index in range(group):
        face = first + index
        partner = partner_ref[0, face]
        constants = lanes_of(face if begin else index, extent)
        traction, motion, stiffness, record = local_face(
            times, own_ref[index, :times], mate_ref[jnp.maximum(partner, 0)], turn_ref[:, lanes_of(face, extent)],
            stiff_ref[:, constants], record_ref[:, constants], partner >= 0, begin,
        )
        robin = traction + motion
        robin_ref[index] = robin
        half_ref[index] = robin.astype(jnp.bfloat16)
        if begin:
            pair_refs[0][:, lanes_of(index, extent)] = stiffness
            pair_refs[1][:, lanes_of(index, extent)] = record


def local_last(partner_ref, turn_ref, own0_ref, own1_ref, mate0_ref, mate1_ref, stiff0_ref, stiff1_ref,
               record0_ref, record1_ref, motion_ref, traction_ref):
    group, times, extent = own0_ref.shape
    starts = position(group)
    for side, (own_ref, mate_ref, stiff_ref, record_ref) in enumerate((
        (own0_ref, mate0_ref, stiff0_ref, record0_ref), (own1_ref, mate1_ref, stiff1_ref, record1_ref),
    )):
        for index in range(group):
            face = starts[side] + index
            lanes, constants = lanes_of(face, extent), lanes_of(index, extent)
            partner = partner_ref[0, face]
            traction, motion, _, _ = local_face(
                times, own_ref[index], mate_ref[jnp.maximum(partner, 0)], turn_ref[:, lanes],
                stiff_ref[:, constants], record_ref[:, constants], partner >= 0, False,
            )
            motion_ref[:, lanes] = motion.astype(jnp.bfloat16)
            traction_ref[:, lanes] = traction.astype(jnp.bfloat16)


def shards(
    compliance,
    block_columns,
    load_response,
    starting_motion,
    start_traction,
    stiffness,
    history,
    face_partner,
    orientation,
):
    _, faces, stored, extent, _ = compliance.shape
    times = starting_motion.shape[1]
    group = faces // 2
    subs = lax.axis_size("sub")
    rows = lax.axis_size("row")
    near_pairs = [(s, s ^ 1) for s in range(subs)]
    far_pairs = []
    for s in range(subs):
        mate = s - 1 if s % 2 == 0 else s + 1
        for r in range(rows):
            there = mate * rows + r if 0 <= mate < subs else s * rows + rows - 1 - r
            far_pairs.append((s * rows + r, there))
    swap = [(r, rows - 1 - r) for r in range(rows)]

    def f32(*shape):
        return jax.ShapeDtypeStruct(shape, jnp.float32)

    def bf16(*shape):
        return jax.ShapeDtypeStruct(shape, jnp.bfloat16)

    def s32(*shape):
        return jax.ShapeDtypeStruct(shape, jnp.int32)

    def call(kernel, in_specs, out_shape, scratch=(), moved=0, out_specs=()):
        outs = out_shape if isinstance(out_shape, tuple) else (out_shape,)
        out_specs = out_specs or (VMEM,) * len(outs)
        return pl.pallas_call(
            kernel,
            out_shape=out_shape,
            in_specs=in_specs,
            out_specs=out_specs if isinstance(out_shape, tuple) else out_specs[0],
            scratch_shapes=scratch,
            compiler_params=pltpu.CompilerParams(vmem_limit_bytes=VMEM_BYTES),
            cost_estimate=pl.CostEstimate(flops=moved, bytes_accessed=moved, transcendentals=0) if moved else None,
        )

    part = (group, times, extent)
    flat = (times, faces * extent)
    block_bytes = faces * stored * extent * extent * 2
    part_bytes = group * times * extent * 4
    in_hbm = functools.partial(pltpu.with_memory_space_constraint, memory_space=pltpu.HBM)
    robin0, robin1, half0, half1 = call(
        prepare, [HBM] * 2, (f32(*part), f32(*part), bf16(*part), bf16(*part)),
        [pltpu.VMEM(flat, jnp.bfloat16), pltpu.VMEM(flat, jnp.bfloat16), pltpu.SemaphoreType.DMA((2,))],
        8 * part_bytes,
    )(in_hbm(starting_motion[0]), in_hbm(start_traction[0]))
    blocks, load, stiff, record, turn, *tables = call(
        fetch, [HBM] * 7,
        (pltpu.VMEM((faces, stored, extent, extent), jnp.bfloat16), bf16(*flat), f32(1, faces * extent), f32(1, faces * extent),
         s32(1, faces * extent), pltpu.SMEM((1, faces), jnp.int32), pltpu.SMEM((faces, 1, stored), jnp.int32),
         pltpu.SMEM((faces, 1, stored), jnp.int32), pltpu.SMEM((1, faces), jnp.int32)),
        [pltpu.SMEM((faces, 1, stored), jnp.int32), pltpu.SemaphoreType.DMA((6 + faces,))],
        block_bytes, (VMEM,) * 5 + (SMEM,) * 4,
    )(
        in_hbm(compliance[0]), in_hbm(load_response[0]), in_hbm(stiffness), in_hbm(history),
        in_hbm(orientation.reshape(1, -1)), in_hbm(jnp.transpose(block_columns, (1, 0, 2))), in_hbm(face_partner),
    )
    partner, *tables = (pltpu.with_memory_space_constraint(table, pltpu.SMEM) for table in tables)

    robin, half = [robin0, robin1], [half0, half1]
    stiffs, records = [stiff, stiff], [record, record]
    for iteration in range(ITERS):
        begin, last = iteration == 0, iteration == ITERS - 1
        other = [lax.ppermute(half[side], "row", swap) for side in range(2)]
        ascent, mates, early = [None, None], [None, None], []
        for side in range(0 if begin else 2):
            early.append(call(
                functools.partial(early_products, side), [SMEM] * 3 + [VMEM] * (3 + side) + [ANY] * side, f32(*part),
                [pltpu.VMEM((rows * faces + 1, times, extent), jnp.bfloat16)], block_bytes,
            )(*tables, blocks, *half, *other[:side], *early))
        for side, (axes, pairs) in enumerate((("sub", near_pairs), (("sub", "row"), far_pairs))):
            more = (stiff, record) if begin else (early[side],)
            ascent[side] = call(
                functools.partial(linear_section, side, begin),
                [SMEM] * 3 + [VMEM] * (7 + len(more)),
                f32(group + side, times + SUBLANES if begin else times, extent),
                [pltpu.VMEM((rows * faces, times, extent), jnp.bfloat16)],
                2 * block_bytes,
            )(*tables, blocks, *half, *other, robin[side], load, *more)
            mates[side] = lax.ppermute(ascent[side], axes, pairs)
        if last:
            return tuple(out[None] for out in call(
                local_last, [SMEM] + [VMEM] * 9, (bf16(*flat),) * 2,
            )(partner, turn, *ascent, *mates, *stiffs, *records))
        for side in range(2):
            outs = (f32(*part), bf16(*part))
            if begin:
                outs += (f32(1, group * extent),) * 2
            robin[side], half[side], *pair = call(
                functools.partial(local_group, side, begin), [SMEM] + [VMEM] * 5, outs,
            )(partner, turn, ascent[side], mates[side], stiffs[side], records[side])
            if begin:
                stiffs[side], records[side] = pair


def solution(mesh):
    in_specs = (
        P("sub", "row", None, None, None),
        P("sub", "row", None),
        P("sub", None, "row"),
        P("sub", None, "row"),
        P("sub", None, "row"),
        P("sub", "row"),
        P("sub", "row"),
        P("sub", "row"),
        P("sub", "row", None),
    )
    out_specs = (P("sub", None, "row"), P("sub", None, "row"))
    return jax.shard_map(shards, mesh=mesh, in_specs=in_specs, out_specs=out_specs, check_vma=False)
```

```python
import functools

import jax
import jax.numpy as jnp
from jax import lax
from jax.experimental import pallas as pl
from jax.experimental.pallas import tpu as pltpu
from jax.sharding import PartitionSpec as P

ITERS = 3
SUBLANES = 8
EARLY = (6, 10)
VMEM_BYTES = 24 * 2**20

ONSET_JUMP = 0.15
FAILURE_JUMP = 1.5

VMEM = pl.BlockSpec(memory_space=pltpu.VMEM)
SMEM = pl.BlockSpec(memory_space=pltpu.SMEM)
ANY = pl.BlockSpec(memory_space=pl.ANY)
HBM = pl.BlockSpec(memory_space=pltpu.HBM)


def position(group):
    near = group * (lax.axis_index("sub") % 2)
    return near, group - near, lax.axis_index("row")


def lanes_of(face, extent):
    return pl.ds(pl.multiple_of(face * extent, extent), extent)


def sort_blocks(columns_ref, order_ref, sorted_ref, ready_ref):
    faces, _, stored = columns_ref.shape
    group = faces // 2
    near, far, mine = position(group)
    own = mine * faces
    partner = (1 - mine) * faces + near

    def sort_row(face, _):
        in_far = (face >= far) & (face < far + group)
        width = jnp.where(in_far, group, 0)
        front, back = jnp.int32(0), jnp.int32(stored - 1)
        for j in range(stored):
            column = columns_ref[face, 0, j]
            early = ((column >= own) & (column < own + faces)) | ((column >= partner) & (column < partner + width))
            place = jnp.where(early, front, back)
            order_ref[face, 0, place] = j
            sorted_ref[face, 0, place] = column
            front = jnp.where(early, front + 1, front)
            back = jnp.where(early, back, back - 1)
        ready_ref[0, face] = front
        return 0

    lax.fori_loop(0, faces, sort_row, 0)


def fetch(blocks_hbm, load_hbm, motion_hbm, stress_hbm, stiff_hbm, record_hbm, turn_hbm, columns_hbm, partner_hbm,
          blocks_ref, load_ref, motion_ref, stress_ref, stiff_ref, record_ref, turn_ref, partner_ref,
          order_ref, sorted_ref, ready_ref, columns_ref, sems):
    pairs = [
        (columns_hbm, columns_ref), (load_hbm, load_ref), (motion_hbm, motion_ref), (stress_hbm, stress_ref),
        (stiff_hbm, stiff_ref), (record_hbm, record_ref), (turn_hbm, turn_ref), (partner_hbm, partner_ref),
    ]
    pairs += [(blocks_hbm.at[face], blocks_ref.at[face]) for face in range(blocks_hbm.shape[0])]
    copies = [pltpu.make_async_copy(source, target, sems.at[n]) for n, (source, target) in enumerate(pairs)]
    for copy in copies:
        copy.start()
    copies[0].wait()
    sort_blocks(columns_ref, order_ref, sorted_ref, ready_ref)
    for copy in copies[1:]:
        copy.wait()


def block_products(parts):
    times, extent = parts[0][0][0].shape
    zero = jnp.zeros_like(parts[0][0][1])
    depth = max(len(part) for part in parts)
    parts = [part + [(part[0][0], zero)] * (depth - len(part)) for part in parts]
    values = jnp.concatenate([jnp.concatenate([v for v, _ in part], axis=1) for part in parts], axis=0)
    blocks = jnp.concatenate([jnp.concatenate([c for _, c in part], axis=1) for part in parts], axis=0)
    product = lax.dot_general(values, blocks, (((1,), (1,)), ((), ())), preferred_element_type=jnp.float32)
    return [
        product[p * times : (p + 1) * times, p * extent : (p + 1) * extent] for p in range(len(parts))
    ]


def group_products(first, group, entries, finish):
    for index in range(0, group - 1, 2):
        pair = block_products([entries(first + index + k) for k in range(2)])
        for k in range(2):
            finish(index + k, pair[k])
    if group % 2:
        whole = entries(first + group - 1)
        cut = (len(whole) + 3) // 4 * 2
        finish(group - 1, sum(block_products([whole[:cut], whole[cut:]])))


def early_products(side, order_ref, sorted_ref, ready_ref, compliance_ref, own0_ref, own1_ref, *refs):
    out_ref, half_ref = refs[-2:]
    group, times, _ = out_ref.shape
    faces = compliance_ref.shape[0]
    *starts, mine = position(group)
    none = half_ref.shape[0] - 1
    half_ref[none] = jnp.zeros_like(half_ref[none])
    for start, ref in zip(starts, (own0_ref, own1_ref)):
        half_ref[pl.ds(mine * faces + start, group)] = ref[...]
    for ref in refs[:side]:
        half_ref[pl.ds((1 - mine) * faces + starts[0], group)] = ref[...]

    def entries(face):
        ready = ready_ref[0, face]
        return [
            (half_ref[jnp.where(slot < ready, sorted_ref[face, 0, slot], none)], compliance_ref[face, order_ref[face, 0, slot]])
            for slot in range(EARLY[side])
        ]

    def finish(index, product):
        out_ref[index] = product

    group_products(starts[side], group, entries, finish)


def sorted_entry(half_ref, order_ref, sorted_ref, compliance_ref, face, slot):
    return half_ref[sorted_ref[face, 0, slot]], compliance_ref[face, order_ref[face, 0, slot]]


def first_section(side, order_ref, sorted_ref, compliance_ref, own_ref, other_ref, motion_ref, stress_ref, load_ref,
                  stiff_ref, record_ref, out_ref, half_ref):
    times = motion_ref.shape[0]
    faces, stored, extent, _ = compliance_ref.shape
    group = faces // 2
    *starts, mine = position(group)
    first = starts[side]
    for run, ref in ((mine, own_ref), (1 - mine, other_ref)):
        for face in range(faces):
            half_ref[run * faces + face] = ref[:, face * extent : (face + 1) * extent]
    entry = functools.partial(sorted_entry, half_ref, order_ref, sorted_ref, compliance_ref)

    def finish(index, product):
        lanes = lanes_of(first + index, extent)
        robin = stress_ref[:, lanes].astype(jnp.float32) + motion_ref[:, lanes].astype(jnp.float32)
        response = product + load_ref[:, lanes].astype(jnp.float32)
        out_ref[index, :times] = robin - 2.0 * response
        out_ref[index, times : times + 1] = stiff_ref[:, lanes]
        out_ref[index, times + 1 : times + 2] = record_ref[:, lanes]
        out_ref[index, times + 2 :] = jnp.zeros_like(out_ref[index, times + 2 :])

    group_products(first, group, lambda face: [entry(face, slot) for slot in range(stored)], finish)
    for spare in range(group, out_ref.shape[0]):
        out_ref[spare] = jnp.zeros_like(out_ref[spare])


def linear_section(side, order_ref, sorted_ref, ready_ref, compliance_ref, own0_ref, own1_ref, other0_ref, other1_ref,
                   robin_ref, load_ref, early_ref, out_ref, half_ref):
    group, times, extent = own0_ref.shape
    faces, stored = compliance_ref.shape[:2]
    *starts, mine = position(group)
    first, done = starts[side], EARLY[side]
    for run, parts in ((mine, (own0_ref, own1_ref)), (1 - mine, (other0_ref, other1_ref))):
        for start, ref in zip(starts, parts):
            half_ref[pl.ds(run * faces + start, group)] = ref[...]
    entry = functools.partial(sorted_entry, half_ref, order_ref, sorted_ref, compliance_ref)

    def finish(index, product):
        response = early_ref[index] + product + load_ref[:, lanes_of(first + index, extent)].astype(jnp.float32)
        out_ref[index] = robin_ref[index] - 2.0 * response

    group_products(first, group, lambda face: [entry(face, slot) for slot in range(done, stored)], finish)
    for spare in range(group, out_ref.shape[0]):
        out_ref[spare] = jnp.zeros_like(out_ref[spare])

    def missed(slot, index):
        out_ref[index] -= 2.0 * block_products([[entry(first + index, slot)]])[0]
        return index

    least = ready_ref[0, first]
    for index in range(1, group):
        least = jnp.minimum(least, ready_ref[0, first + index])

    @pl.when(least < done)
    def _():
        for index in range(group):
            lax.fori_loop(ready_ref[0, first + index], done, missed, index)


def running_peak(sizes):
    row = lax.broadcasted_iota(jnp.int32, sizes.shape, 0)
    step = 1
    while step < sizes.shape[0]:
        earlier = pltpu.roll(sizes, step, 0)
        sizes = jnp.maximum(sizes, jnp.where(row >= step, earlier, 0.0))
        step *= 2
    return sizes


def local_face(times, ascent, mate, turn, stiffness, record, live, begin):
    extent = ascent.shape[1]
    gather = functools.partial(jnp.take_along_axis, axis=1, mode="promise_in_bounds")
    mate_ascent = gather(mate[:times], jnp.broadcast_to(turn, (times, extent)))
    if begin:
        constants = gather(mate[times:], jnp.broadcast_to(turn, (SUBLANES, extent)))
        stiffness = 0.5 * (stiffness + constants[:1])
        record = jnp.maximum(record, constants[1:2])
    difference = ascent - mate_ascent
    jump = difference / (1.0 + 2.0 * stiffness)
    peak = jnp.maximum(record, running_peak(jnp.abs(jump)))
    damage = jnp.clip((peak - ONSET_JUMP) / (FAILURE_JUMP - ONSET_JUMP), 0.0, 1.0)
    effective = stiffness * (1.0 - damage)
    traction = jnp.where(live, effective * difference / (1.0 + 2.0 * effective), 0.0)
    return traction, traction - ascent, stiffness, record


def local_group(side, begin, partner_ref, turn_ref, own_ref, mate_ref, stiff_ref, record_ref, robin_ref, half_ref, *pair_refs):
    group, times, extent = robin_ref.shape
    first = position(group)[side]
    for index in range(group):
        face = first + index
        partner = partner_ref[0, face]
        constants = lanes_of(face if begin else index, extent)
        traction, motion, stiffness, record = local_face(
            times, own_ref[index, :times], mate_ref[jnp.maximum(partner, 0)], turn_ref[:, lanes_of(face, extent)],
            stiff_ref[:, constants], record_ref[:, constants], partner >= 0, begin,
        )
        robin = traction + motion
        robin_ref[index] = robin
        half_ref[index] = robin.astype(jnp.bfloat16)
        if begin:
            pair_refs[0][:, lanes_of(index, extent)] = stiffness
            pair_refs[1][:, lanes_of(index, extent)] = record


def local_last(partner_ref, turn_ref, own0_ref, own1_ref, mate0_ref, mate1_ref, stiff0_ref, stiff1_ref,
               record0_ref, record1_ref, motion_ref, traction_ref):
    group, times, extent = own0_ref.shape
    starts = position(group)
    for side, (own_ref, mate_ref, stiff_ref, record_ref) in enumerate((
        (own0_ref, mate0_ref, stiff0_ref, record0_ref), (own1_ref, mate1_ref, stiff1_ref, record1_ref),
    )):
        for index in range(group):
            face = starts[side] + index
            lanes, constants = lanes_of(face, extent), lanes_of(index, extent)
            partner = partner_ref[0, face]
            traction, motion, _, _ = local_face(
                times, own_ref[index], mate_ref[jnp.maximum(partner, 0)], turn_ref[:, lanes],
                stiff_ref[:, constants], record_ref[:, constants], partner >= 0, False,
            )
            motion_ref[:, lanes] = motion.astype(jnp.bfloat16)
            traction_ref[:, lanes] = traction.astype(jnp.bfloat16)


def shards(
    compliance,
    block_columns,
    load_response,
    starting_motion,
    start_traction,
    stiffness,
    history,
    face_partner,
    orientation,
):
    _, faces, stored, extent, _ = compliance.shape
    times = starting_motion.shape[1]
    group = faces // 2
    subs = lax.axis_size("sub")
    rows = lax.axis_size("row")
    near_pairs = [(s, s ^ 1) for s in range(subs)]
    far_pairs = []
    for s in range(subs):
        mate = s - 1 if s % 2 == 0 else s + 1
        for r in range(rows):
            there = mate * rows + r if 0 <= mate < subs else s * rows + rows - 1 - r
            far_pairs.append((s * rows + r, there))
    swap = [(r, rows - 1 - r) for r in range(rows)]

    def f32(*shape):
        return jax.ShapeDtypeStruct(shape, jnp.float32)

    def bf16(*shape):
        return jax.ShapeDtypeStruct(shape, jnp.bfloat16)

    def s32(*shape):
        return jax.ShapeDtypeStruct(shape, jnp.int32)

    def call(kernel, in_specs, out_shape, scratch=(), moved=0, out_specs=()):
        outs = out_shape if isinstance(out_shape, tuple) else (out_shape,)
        out_specs = out_specs or (VMEM,) * len(outs)
        return pl.pallas_call(
            kernel,
            out_shape=out_shape,
            in_specs=in_specs,
            out_specs=out_specs if isinstance(out_shape, tuple) else out_specs[0],
            scratch_shapes=scratch,
            compiler_params=pltpu.CompilerParams(vmem_limit_bytes=VMEM_BYTES),
            cost_estimate=pl.CostEstimate(flops=moved, bytes_accessed=moved, transcendentals=0) if moved else None,
        )

    part = (group, times, extent)
    flat = (times, faces * extent)
    block_bytes = faces * stored * extent * extent * 2
    halves = pltpu.VMEM((rows * faces, times, extent), jnp.bfloat16)
    in_hbm = functools.partial(pltpu.with_memory_space_constraint, memory_space=pltpu.HBM)
    own = (start_traction[0].astype(jnp.float32) + starting_motion[0].astype(jnp.float32)).astype(jnp.bfloat16)
    other = lax.ppermute(own, "row", swap)
    blocks, load, motion, stress, stiff, record, turn, partner, *tables = call(
        fetch, [HBM] * 9,
        (pltpu.VMEM((faces, stored, extent, extent), jnp.bfloat16), bf16(*flat), bf16(*flat), bf16(*flat),
         f32(1, faces * extent), f32(1, faces * extent), s32(1, faces * extent), pltpu.SMEM((1, faces), jnp.int32),
         pltpu.SMEM((faces, 1, stored), jnp.int32), pltpu.SMEM((faces, 1, stored), jnp.int32), pltpu.SMEM((1, faces), jnp.int32)),
        [pltpu.SMEM((faces, 1, stored), jnp.int32), pltpu.SemaphoreType.DMA((8 + faces,))],
        block_bytes, (VMEM,) * 7 + (SMEM,) * 4,
    )(
        in_hbm(compliance[0]), in_hbm(load_response[0]), in_hbm(starting_motion[0]), in_hbm(start_traction[0]),
        in_hbm(stiffness), in_hbm(history), in_hbm(orientation.reshape(1, -1)),
        in_hbm(jnp.transpose(block_columns, (1, 0, 2))), in_hbm(face_partner),
    )
    in_smem = functools.partial(pltpu.with_memory_space_constraint, memory_space=pltpu.SMEM)
    partner, tables = in_smem(partner), [in_smem(table) for table in tables]

    robin, half = [None, None], [None, None]
    stiffs, records = [stiff, stiff], [record, record]
    for iteration in range(ITERS):
        begin, last = iteration == 0, iteration == ITERS - 1
        if not begin:
            other = [lax.ppermute(half[side], "row", swap) for side in range(2)]
        ascent, mates, early = [None, None], [None, None], []
        for side in range(0 if begin else 2):
            early.append(call(
                functools.partial(early_products, side), [SMEM] * 3 + [VMEM] * (3 + side) + [ANY] * side, f32(*part),
                [pltpu.VMEM((rows * faces + 1, times, extent), jnp.bfloat16)], block_bytes,
            )(*tables, blocks, *half, *other[:side], *early))
        for side, (axes, pairs) in enumerate((("sub", near_pairs), (("sub", "row"), far_pairs))):
            if begin:
                ascent[side] = call(
                    functools.partial(first_section, side), [SMEM] * 2 + [VMEM] * 8,
                    f32(group + side, times + SUBLANES, extent), [halves], 2 * block_bytes,
                )(*tables[:2], blocks, own, other, motion, stress, load, stiff, record)
            else:
                ascent[side] = call(
                    functools.partial(linear_section, side), [SMEM] * 3 + [VMEM] * 8,
                    f32(group + side, times, extent), [halves], 2 * block_bytes,
                )(*tables, blocks, *half, *other, robin[side], load, early[side])
            mates[side] = lax.ppermute(ascent[side], axes, pairs)
        if last:
            return tuple(out[None] for out in call(
                local_last, [SMEM] + [VMEM] * 9, (bf16(*flat),) * 2,
            )(partner, turn, *ascent, *mates, *stiffs, *records))
        for side in range(2):
            outs = (f32(*part), bf16(*part))
            if begin:
                outs += (f32(1, group * extent),) * 2
            robin[side], half[side], *pair = call(
                functools.partial(local_group, side, begin), [SMEM] + [VMEM] * 5, outs,
            )(partner, turn, ascent[side], mates[side], stiffs[side], records[side])
            if begin:
                stiffs[side], records[side] = pair


def solution(mesh):
    in_specs = (
        P("sub", "row", None, None, None),
        P("sub", "row", None),
        P("sub", None, "row"),
        P("sub", None, "row"),
        P("sub", None, "row"),
        P("sub", "row"),
        P("sub", "row"),
        P("sub", "row"),
        P("sub", "row", None),
    )
    out_specs = (P("sub", None, "row"), P("sub", None, "row"))
    return jax.shard_map(shards, mesh=mesh, in_specs=in_specs, out_specs=out_specs, check_vma=False)
```

```python
import functools

import jax
import jax.numpy as jnp
from jax import lax
from jax.experimental import pallas as pl
from jax.experimental.pallas import tpu as pltpu
from jax.sharding import PartitionSpec as P

ITERS = 3
SUBLANES = 8
LEAST = 2.0**-100
EARLY = (6, 10)
VMEM_BYTES = 24 * 2**20

ONSET_JUMP = 0.15
FAILURE_JUMP = 1.5

VMEM = pl.BlockSpec(memory_space=pltpu.VMEM)
SMEM = pl.BlockSpec(memory_space=pltpu.SMEM)
ANY = pl.BlockSpec(memory_space=pl.ANY)
HBM = pl.BlockSpec(memory_space=pltpu.HBM)


def position(group):
    near = group * (lax.axis_index("sub") % 2)
    return near, group - near, lax.axis_index("row")


def lanes_of(face, extent):
    return pl.ds(pl.multiple_of(face * extent, extent), extent)


def sort_blocks(columns_ref, order_ref, sorted_ref, ready_ref):
    faces, _, stored = columns_ref.shape
    group = faces // 2
    near, far, mine = position(group)
    own = mine * faces
    partner = (1 - mine) * faces + near

    def sort_row(face, _):
        in_far = (face >= far) & (face < far + group)
        width = jnp.where(in_far, group, 0)
        front, back = jnp.int32(0), jnp.int32(stored - 1)
        for j in range(stored):
            column = columns_ref[face, 0, j]
            early = ((column >= own) & (column < own + faces)) | ((column >= partner) & (column < partner + width))
            place = jnp.where(early, front, back)
            order_ref[face, 0, place] = j
            sorted_ref[face, 0, place] = column
            front = jnp.where(early, front + 1, front)
            back = jnp.where(early, back, back - 1)
        ready_ref[0, face] = front
        return 0

    lax.fori_loop(0, faces, sort_row, 0)


def fetch(blocks_hbm, load_hbm, motion_hbm, stress_hbm, stiff_hbm, record_hbm, turn_hbm, columns_hbm, partner_hbm,
          blocks_ref, load_ref, motion_ref, stress_ref, stiff_ref, record_ref, turn_ref, partner_ref,
          order_ref, sorted_ref, ready_ref, columns_ref, sems):
    pairs = [
        (columns_hbm, columns_ref), (load_hbm, load_ref), (motion_hbm, motion_ref), (stress_hbm, stress_ref),
        (stiff_hbm, stiff_ref), (record_hbm, record_ref), (turn_hbm, turn_ref), (partner_hbm, partner_ref),
    ]
    pairs += [(blocks_hbm.at[face], blocks_ref.at[face]) for face in range(blocks_hbm.shape[0])]
    copies = [pltpu.make_async_copy(source, target, sems.at[n]) for n, (source, target) in enumerate(pairs)]
    for copy in copies:
        copy.start()
    copies[0].wait()
    sort_blocks(columns_ref, order_ref, sorted_ref, ready_ref)
    for copy in copies[1:]:
        copy.wait()


def block_products(parts):
    times, extent = parts[0][0][0].shape
    zero = jnp.zeros_like(parts[0][0][1])
    depth = max(len(part) for part in parts)
    parts = [part + [(part[0][0], zero)] * (depth - len(part)) for part in parts]
    values = jnp.concatenate([jnp.concatenate([v for v, _ in part], axis=1) for part in parts], axis=0)
    blocks = jnp.concatenate([jnp.concatenate([c for _, c in part], axis=1) for part in parts], axis=0)
    product = lax.dot_general(values, blocks, (((1,), (1,)), ((), ())), preferred_element_type=jnp.float32)
    return [
        product[p * times : (p + 1) * times, p * extent : (p + 1) * extent] for p in range(len(parts))
    ]


def group_products(first, group, entries, finish):
    for index in range(0, group - 1, 2):
        pair = block_products([entries(first + index + k) for k in range(2)])
        for k in range(2):
            finish(index + k, pair[k])
    if group % 2:
        whole = entries(first + group - 1)
        cut = (len(whole) + 3) // 4 * 2
        finish(group - 1, sum(block_products([whole[:cut], whole[cut:]])))


def early_products(side, order_ref, sorted_ref, ready_ref, compliance_ref, own0_ref, own1_ref, *refs):
    out_ref, half_ref = refs[-2:]
    group, times, _ = out_ref.shape
    faces = compliance_ref.shape[0]
    *starts, mine = position(group)
    none = half_ref.shape[0] - 1
    half_ref[none] = jnp.zeros_like(half_ref[none])
    for start, ref in zip(starts, (own0_ref, own1_ref)):
        half_ref[pl.ds(mine * faces + start, group)] = ref[...]
    for ref in refs[:side]:
        half_ref[pl.ds((1 - mine) * faces + starts[0], group)] = ref[...]

    def entries(face):
        ready = ready_ref[0, face]
        return [
            (half_ref[jnp.where(slot < ready, sorted_ref[face, 0, slot], none)], compliance_ref[face, order_ref[face, 0, slot]])
            for slot in range(EARLY[side])
        ]

    def finish(index, product):
        out_ref[index] = product

    group_products(starts[side], group, entries, finish)


def sorted_entry(half_ref, order_ref, sorted_ref, compliance_ref, face, slot):
    return half_ref[sorted_ref[face, 0, slot]], compliance_ref[face, order_ref[face, 0, slot]]


def first_section(side, order_ref, sorted_ref, compliance_ref, own_ref, other_ref, motion_ref, stress_ref, load_ref,
                  stiff_ref, record_ref, out_ref, half_ref):
    times = motion_ref.shape[0]
    faces, stored, extent, _ = compliance_ref.shape
    group = faces // 2
    *starts, mine = position(group)
    first = starts[side]
    for run, ref in ((mine, own_ref), (1 - mine, other_ref)):
        for face in range(faces):
            half_ref[run * faces + face] = ref[:, face * extent : (face + 1) * extent]
    entry = functools.partial(sorted_entry, half_ref, order_ref, sorted_ref, compliance_ref)

    def finish(index, product):
        lanes = lanes_of(first + index, extent)
        robin = stress_ref[:, lanes].astype(jnp.float32) + motion_ref[:, lanes].astype(jnp.float32)
        response = product + load_ref[:, lanes].astype(jnp.float32)
        out_ref[index] = robin - 2.0 * response
        out_ref[group, index : index + 1] = stiff_ref[:, lanes]
        out_ref[group, group + index : group + index + 1] = record_ref[:, lanes]

    for plane in range(group, out_ref.shape[0]):
        out_ref[plane] = jnp.zeros_like(out_ref[plane])
    group_products(first, group, lambda face: [entry(face, slot) for slot in range(stored)], finish)


def linear_section(side, order_ref, sorted_ref, ready_ref, compliance_ref, own0_ref, own1_ref, other0_ref, other1_ref,
                   robin_ref, load_ref, early_ref, out_ref, sent_ref, half_ref):
    group, times, extent = own0_ref.shape
    faces, stored = compliance_ref.shape[:2]
    *starts, mine = position(group)
    first, done = starts[side], EARLY[side]
    for run, parts in ((mine, (own0_ref, own1_ref)), (1 - mine, (other0_ref, other1_ref))):
        for start, ref in zip(starts, parts):
            half_ref[pl.ds(run * faces + start, group)] = ref[...]
    entry = functools.partial(sorted_entry, half_ref, order_ref, sorted_ref, compliance_ref)

    def finish(index, product):
        response = early_ref[index] + product + load_ref[:, lanes_of(first + index, extent)].astype(jnp.float32)
        out_ref[index] = robin_ref[index] - 2.0 * response

    group_products(first, group, lambda face: [entry(face, slot) for slot in range(done, stored)], finish)

    def missed(slot, index):
        out_ref[index] -= 2.0 * block_products([[entry(first + index, slot)]])[0]
        return index

    least = ready_ref[0, first]
    for index in range(1, group):
        least = jnp.minimum(least, ready_ref[0, first + index])

    @pl.when(least < done)
    def _():
        for index in range(group):
            lax.fori_loop(ready_ref[0, first + index], done, missed, index)

    encode(out_ref, sent_ref)


def encode(values_ref, sent_ref):
    group, times, extent = values_ref.shape
    lane = lax.broadcasted_iota(jnp.int32, (times, extent), 1)
    exponents = jnp.zeros((times, extent), jnp.float32)
    for index in range(group):
        values = values_ref[index]
        largest = jnp.max(jnp.abs(values), axis=1, keepdims=True)
        exponent = jnp.floor(jnp.log2(jnp.maximum(largest, LEAST))) - 14.0
        steps = jnp.clip(jnp.round(values * jnp.exp2(-exponent)), -32767.0, 32767.0)
        sent_ref[index] = steps.astype(jnp.int32).astype(jnp.int16)
        exponents = jnp.where(lane == index, exponent, exponents)
    sent_ref[group] = exponents.astype(jnp.int32).astype(jnp.int16)
    for plane in range(group + 1, sent_ref.shape[0]):
        sent_ref[plane] = jnp.zeros_like(sent_ref[plane])


def decoder(sent_ref, group):
    exponents = sent_ref[group].astype(jnp.int32).astype(jnp.float32)
    lane = lax.broadcasted_iota(jnp.int32, exponents.shape, 1)

    def face_of(index):
        exponent = jnp.sum(jnp.where(lane == index, exponents, 0.0), axis=1, keepdims=True)
        return sent_ref[index].astype(jnp.int32).astype(jnp.float32) * jnp.exp2(exponent)

    return face_of


def running_peak(sizes):
    row = lax.broadcasted_iota(jnp.int32, sizes.shape, 0)
    step = 1
    while step < sizes.shape[0]:
        earlier = pltpu.roll(sizes, step, 0)
        sizes = jnp.maximum(sizes, jnp.where(row >= step, earlier, 0.0))
        step *= 2
    return sizes


def turned(values, turn):
    return jnp.take_along_axis(values, jnp.broadcast_to(turn, values.shape), axis=1, mode="promise_in_bounds")


def local_face(ascent, mate_ascent, stiffness, record, live):
    difference = ascent - mate_ascent
    jump = difference / (1.0 + 2.0 * stiffness)
    peak = jnp.maximum(record, running_peak(jnp.abs(jump)))
    damage = jnp.clip((peak - ONSET_JUMP) / (FAILURE_JUMP - ONSET_JUMP), 0.0, 1.0)
    effective = stiffness * (1.0 - damage)
    traction = jnp.where(live, effective * difference / (1.0 + 2.0 * effective), 0.0)
    return traction, traction - ascent


def local_first(side, partner_ref, turn_ref, own_ref, mate_ref, stiff_ref, record_ref,
                robin_ref, half_ref, pair_stiff_ref, pair_record_ref):
    group, _, extent = robin_ref.shape
    first = position(group)[side]
    for index in range(group):
        face = first + index
        lanes, here = lanes_of(face, extent), lanes_of(index, extent)
        partner = partner_ref[0, face]
        mate = jnp.maximum(partner, 0)
        turn = turn_ref[:, lanes]

        def constant(row):
            return turned(jnp.broadcast_to(mate_ref[group, pl.ds(row, 1), :], (SUBLANES, extent)), turn)[:1]

        stiffness = 0.5 * (stiff_ref[:, lanes] + constant(mate))
        record = jnp.maximum(record_ref[:, lanes], constant(group + mate))
        pair_stiff_ref[:, here] = stiffness
        pair_record_ref[:, here] = record
        traction, motion = local_face(own_ref[index], turned(mate_ref[mate], turn), stiffness, record, partner >= 0)
        robin = traction + motion
        robin_ref[index] = robin
        half_ref[index] = robin.astype(jnp.bfloat16)


def local_faces(side, partner_ref, turn_ref, own_ref, mate_ref, stiff_ref, record_ref):
    group, _, extent = own_ref.shape
    first = position(group)[side]
    mate_face = decoder(mate_ref, group)
    for index in range(group):
        face = first + index
        here = lanes_of(index, extent)
        partner = partner_ref[0, face]
        mate_ascent = turned(mate_face(jnp.maximum(partner, 0)), turn_ref[:, lanes_of(face, extent)])
        yield index, *local_face(own_ref[index], mate_ascent, stiff_ref[:, here], record_ref[:, here], partner >= 0)


def local_group(side, *refs):
    *ins, robin_ref, half_ref = refs
    for index, traction, motion in local_faces(side, *ins):
        robin = traction + motion
        robin_ref[index] = robin
        half_ref[index] = robin.astype(jnp.bfloat16)


def local_last(side, *refs):
    ins, (motion_hbm, traction_hbm, motion_ref, traction_ref, sems) = refs[:6], refs[-5:]
    group, _, extent = ins[2].shape
    for index, traction, motion in local_faces(side, *ins):
        here = lanes_of(index, extent)
        motion_ref[:, here] = motion.astype(jnp.bfloat16)
        traction_ref[:, here] = traction.astype(jnp.bfloat16)
    lanes = pl.ds(pl.multiple_of(position(group)[side] * extent, extent), group * extent)
    copies = [
        pltpu.make_async_copy(motion_ref, motion_hbm.at[:, lanes], sems.at[0]),
        pltpu.make_async_copy(traction_ref, traction_hbm.at[:, lanes], sems.at[1]),
    ]
    for copy in copies:
        copy.start()
    for copy in copies:
        copy.wait()


def shards(
    compliance,
    block_columns,
    load_response,
    starting_motion,
    start_traction,
    stiffness,
    history,
    face_partner,
    orientation,
):
    _, faces, stored, extent, _ = compliance.shape
    times = starting_motion.shape[1]
    group = faces // 2
    subs = lax.axis_size("sub")
    rows = lax.axis_size("row")
    near_pairs = [(s, s ^ 1) for s in range(subs)]
    far_pairs = []
    for s in range(subs):
        mate = s - 1 if s % 2 == 0 else s + 1
        for r in range(rows):
            there = mate * rows + r if 0 <= mate < subs else s * rows + rows - 1 - r
            far_pairs.append((s * rows + r, there))
    swap = [(r, rows - 1 - r) for r in range(rows)]

    def f32(*shape):
        return jax.ShapeDtypeStruct(shape, jnp.float32)

    def bf16(*shape):
        return jax.ShapeDtypeStruct(shape, jnp.bfloat16)

    def s32(*shape):
        return jax.ShapeDtypeStruct(shape, jnp.int32)

    def call(kernel, in_specs, out_shape, scratch=(), moved=0, out_specs=(), aliases={}):
        outs = out_shape if isinstance(out_shape, tuple) else (out_shape,)
        out_specs = out_specs or (VMEM,) * len(outs)
        return pl.pallas_call(
            kernel,
            out_shape=out_shape,
            in_specs=in_specs,
            out_specs=out_specs if isinstance(out_shape, tuple) else out_specs[0],
            scratch_shapes=scratch,
            input_output_aliases=aliases,
            compiler_params=pltpu.CompilerParams(vmem_limit_bytes=VMEM_BYTES),
            cost_estimate=pl.CostEstimate(flops=moved, bytes_accessed=moved, transcendentals=0) if moved else None,
        )

    part = (group, times, extent)
    flat = (times, faces * extent)
    block_bytes = faces * stored * extent * extent * 2
    halves = pltpu.VMEM((rows * faces, times, extent), jnp.bfloat16)
    in_hbm = functools.partial(pltpu.with_memory_space_constraint, memory_space=pltpu.HBM)
    own = (start_traction[0].astype(jnp.float32) + starting_motion[0].astype(jnp.float32)).astype(jnp.bfloat16)
    other = lax.ppermute(own, "row", swap)
    blocks, load, motion, stress, stiff, record, turn, partner, *tables = call(
        fetch, [HBM] * 9,
        (pltpu.VMEM((faces, stored, extent, extent), jnp.bfloat16), bf16(*flat), bf16(*flat), bf16(*flat),
         f32(1, faces * extent), f32(1, faces * extent), s32(1, faces * extent), pltpu.SMEM((1, faces), jnp.int32),
         pltpu.SMEM((faces, 1, stored), jnp.int32), pltpu.SMEM((faces, 1, stored), jnp.int32), pltpu.SMEM((1, faces), jnp.int32)),
        [pltpu.SMEM((faces, 1, stored), jnp.int32), pltpu.SemaphoreType.DMA((8 + faces,))],
        block_bytes, (VMEM,) * 7 + (SMEM,) * 4,
    )(
        in_hbm(compliance[0]), in_hbm(load_response[0]), in_hbm(starting_motion[0]), in_hbm(start_traction[0]),
        in_hbm(stiffness), in_hbm(history), in_hbm(orientation.reshape(1, -1)),
        in_hbm(jnp.transpose(block_columns, (1, 0, 2))), in_hbm(face_partner),
    )
    in_smem = functools.partial(pltpu.with_memory_space_constraint, memory_space=pltpu.SMEM)
    partner, tables = in_smem(partner), [in_smem(table) for table in tables]

    robin, half = [None, None], [None, None]
    stiffs, records = [stiff, stiff], [record, record]
    for iteration in range(ITERS):
        begin, last = iteration == 0, iteration == ITERS - 1
        if not begin:
            other = [lax.ppermute(half[side], "row", swap) for side in range(2)]
        ascent, mates, early = [None, None], [None, None], []
        for side in range(0 if begin else 2):
            early.append(call(
                functools.partial(early_products, side), [SMEM] * 3 + [VMEM] * (3 + side) + [ANY] * side, f32(*part),
                [pltpu.VMEM((rows * faces + 1, times, extent), jnp.bfloat16)], block_bytes,
            )(*tables, blocks, *half, *other[:side], *early))
        for side, (axes, pairs) in enumerate((("sub", near_pairs), (("sub", "row"), far_pairs))):
            if begin:
                ascent[side] = sent = call(
                    functools.partial(first_section, side), [SMEM] * 2 + [VMEM] * 8,
                    f32(group + 1 + side, times, extent), [halves], 2 * block_bytes,
                )(*tables[:2], blocks, own, other, motion, stress, load, stiff, record)
            else:
                ascent[side], sent = call(
                    functools.partial(linear_section, side), [SMEM] * 3 + [VMEM] * 8,
                    (f32(*part), jax.ShapeDtypeStruct((group + 1 + side, times, extent), jnp.int16)),
                    [halves], 2 * block_bytes,
                )(*tables, blocks, *half, *other, robin[side], load, early[side])
            mates[side] = lax.ppermute(sent, axes, pairs)
        outs = ()
        for side in range(2):
            ins = (partner, turn, ascent[side], mates[side], stiffs[side], records[side])
            specs = [SMEM] + [VMEM] * 5
            if begin:
                robin[side], half[side], stiffs[side], records[side] = call(
                    functools.partial(local_first, side), specs,
                    (f32(*part), bf16(*part), f32(1, group * extent), f32(1, group * extent)),
                )(*ins)
            elif not last:
                robin[side], half[side] = call(functools.partial(local_group, side), specs, (f32(*part), bf16(*part)))(*ins)
            else:
                share = pltpu.VMEM((times, group * extent), jnp.bfloat16)
                outs = call(
                    functools.partial(local_last, side), specs + [HBM] * len(outs), (bf16(*flat),) * 2,
                    [share, share, pltpu.SemaphoreType.DMA((2,))], 0, (HBM,) * 2, {6 + n: n for n in range(len(outs))},
                )(*ins, *outs)
    return tuple(out[None] for out in outs)


def solution(mesh):
    in_specs = (
        P("sub", "row", None, None, None),
        P("sub", "row", None),
        P("sub", None, "row"),
        P("sub", None, "row"),
        P("sub", None, "row"),
        P("sub", "row"),
        P("sub", "row"),
        P("sub", "row"),
        P("sub", "row", None),
    )
    out_specs = (P("sub", None, "row"), P("sub", None, "row"))
    return jax.shard_map(shards, mesh=mesh, in_specs=in_specs, out_specs=out_specs, check_vma=False)
```

```python
import functools

import jax
import jax.numpy as jnp
from jax import lax
from jax.experimental import pallas as pl
from jax.experimental.pallas import tpu as pltpu
from jax.sharding import PartitionSpec as P

ITERS = 3
SUBLANES = 8
LEAST = 2.0**-100
EARLY = (6, 10)
VMEM_BYTES = 24 * 2**20

ONSET_JUMP = 0.15
FAILURE_JUMP = 1.5

VMEM = pl.BlockSpec(memory_space=pltpu.VMEM)
SMEM = pl.BlockSpec(memory_space=pltpu.SMEM)
ANY = pl.BlockSpec(memory_space=pl.ANY)
HBM = pl.BlockSpec(memory_space=pltpu.HBM)


def position(group):
    near = group * (lax.axis_index("sub") % 2)
    return near, group - near, lax.axis_index("row")


def lanes_of(face, extent):
    return pl.ds(pl.multiple_of(face * extent, extent), extent)


def sort_blocks(columns_ref, order_ref, sorted_ref, ready_ref):
    faces, _, stored = columns_ref.shape
    group = faces // 2
    near, far, mine = position(group)
    own = mine * faces
    partner = (1 - mine) * faces + near

    def sort_row(face, _):
        in_far = (face >= far) & (face < far + group)
        width = jnp.where(in_far, group, 0)
        front, back = jnp.int32(0), jnp.int32(stored - 1)
        for j in range(stored):
            column = columns_ref[face, 0, j]
            early = ((column >= own) & (column < own + faces)) | ((column >= partner) & (column < partner + width))
            place = jnp.where(early, front, back)
            order_ref[face, 0, place] = j
            sorted_ref[face, 0, place] = column
            front = jnp.where(early, front + 1, front)
            back = jnp.where(early, back, back - 1)
        ready_ref[0, face] = front
        return 0

    lax.fori_loop(0, faces, sort_row, 0)


def fetch(blocks_hbm, load_hbm, motion_hbm, stress_hbm, stiff_hbm, record_hbm, turn_hbm, columns_hbm, partner_hbm,
          blocks_ref, load_ref, motion_ref, stress_ref, stiff_ref, record_ref, turn_ref, partner_ref,
          order_ref, sorted_ref, ready_ref, columns_ref, sems):
    pairs = [
        (columns_hbm, columns_ref), (load_hbm, load_ref), (motion_hbm, motion_ref), (stress_hbm, stress_ref),
        (stiff_hbm, stiff_ref), (record_hbm, record_ref), (turn_hbm, turn_ref), (partner_hbm, partner_ref),
    ]
    pairs += [(blocks_hbm.at[face], blocks_ref.at[face]) for face in range(blocks_hbm.shape[0])]
    copies = [pltpu.make_async_copy(source, target, sems.at[n]) for n, (source, target) in enumerate(pairs)]
    for copy in copies:
        copy.start()
    copies[0].wait()
    sort_blocks(columns_ref, order_ref, sorted_ref, ready_ref)
    for copy in copies[1:]:
        copy.wait()


def block_products(parts):
    times, extent = parts[0][0][0].shape
    zero = jnp.zeros_like(parts[0][0][1])
    depth = max(len(part) for part in parts)
    parts = [part + [(part[0][0], zero)] * (depth - len(part)) for part in parts]
    values = jnp.concatenate([jnp.concatenate([v for v, _ in part], axis=1) for part in parts], axis=0)
    blocks = jnp.concatenate([jnp.concatenate([c for _, c in part], axis=1) for part in parts], axis=0)
    product = lax.dot_general(values, blocks, (((1,), (1,)), ((), ())), preferred_element_type=jnp.float32)
    return [
        product[p * times : (p + 1) * times, p * extent : (p + 1) * extent] for p in range(len(parts))
    ]


def group_products(first, group, entries, finish):
    for index in range(0, group - 1, 2):
        pair = block_products([entries(first + index + k) for k in range(2)])
        for k in range(2):
            finish(index + k, pair[k])
    if group % 2:
        whole = entries(first + group - 1)
        cut = (len(whole) + 3) // 4 * 2
        finish(group - 1, sum(block_products([whole[:cut], whole[cut:]])))


def early_products(side, order_ref, sorted_ref, ready_ref, compliance_ref, own0_ref, own1_ref, *refs):
    out_ref, half_ref = refs[-2:]
    group, times, _ = out_ref.shape
    faces = compliance_ref.shape[0]
    *starts, mine = position(group)
    none = half_ref.shape[0] - 1
    half_ref[none] = jnp.zeros_like(half_ref[none])
    for start, ref in zip(starts, (own0_ref, own1_ref)):
        half_ref[pl.ds(mine * faces + start, group)] = ref[...]
    for ref in refs[:side]:
        half_ref[pl.ds((1 - mine) * faces + starts[0], group)] = ref[...]

    def entries(face):
        ready = ready_ref[0, face]
        return [
            (half_ref[jnp.where(slot < ready, sorted_ref[face, 0, slot], none)], compliance_ref[face, order_ref[face, 0, slot]])
            for slot in range(EARLY[side])
        ]

    def finish(index, product):
        out_ref[index] = product

    group_products(starts[side], group, entries, finish)


def sorted_entry(half_ref, order_ref, sorted_ref, compliance_ref, face, slot):
    return half_ref[sorted_ref[face, 0, slot]], compliance_ref[face, order_ref[face, 0, slot]]


def first_section(side, order_ref, sorted_ref, compliance_ref, own_ref, other_ref, motion_ref, stress_ref, load_ref,
                  stiff_ref, record_ref, out_ref, half_ref):
    times = motion_ref.shape[0]
    faces, stored, extent, _ = compliance_ref.shape
    group = faces // 2
    *starts, mine = position(group)
    first = starts[side]
    for run, ref in ((mine, own_ref), (1 - mine, other_ref)):
        for face in range(faces):
            half_ref[run * faces + face] = ref[:, face * extent : (face + 1) * extent]
    entry = functools.partial(sorted_entry, half_ref, order_ref, sorted_ref, compliance_ref)

    def finish(index, product):
        lanes = lanes_of(first + index, extent)
        robin = stress_ref[:, lanes].astype(jnp.float32) + motion_ref[:, lanes].astype(jnp.float32)
        response = product + load_ref[:, lanes].astype(jnp.float32)
        out_ref[index] = robin - 2.0 * response
        out_ref[group, index : index + 1] = stiff_ref[:, lanes]
        out_ref[group, group + index : group + index + 1] = record_ref[:, lanes]

    for plane in range(group, out_ref.shape[0]):
        out_ref[plane] = jnp.zeros_like(out_ref[plane])
    group_products(first, group, lambda face: [entry(face, slot) for slot in range(stored)], finish)


def linear_section(side, order_ref, sorted_ref, ready_ref, compliance_ref, own0_ref, own1_ref, other0_ref, other1_ref,
                   robin_ref, load_ref, early_ref, out_ref, sent_ref, half_ref):
    group, times, extent = own0_ref.shape
    faces, stored = compliance_ref.shape[:2]
    *starts, mine = position(group)
    first, done = starts[side], EARLY[side]
    for run, parts in ((mine, (own0_ref, own1_ref)), (1 - mine, (other0_ref, other1_ref))):
        for start, ref in zip(starts, parts):
            half_ref[pl.ds(run * faces + start, group)] = ref[...]
    entry = functools.partial(sorted_entry, half_ref, order_ref, sorted_ref, compliance_ref)

    def finish(index, product):
        response = early_ref[index] + product + load_ref[:, lanes_of(first + index, extent)].astype(jnp.float32)
        out_ref[index] = robin_ref[index] - 2.0 * response

    group_products(first, group, lambda face: [entry(face, slot) for slot in range(done, stored)], finish)

    def missed(slot, index):
        out_ref[index] -= 2.0 * block_products([[entry(first + index, slot)]])[0]
        return index

    least = ready_ref[0, first]
    for index in range(1, group):
        least = jnp.minimum(least, ready_ref[0, first + index])

    @pl.when(least < done)
    def _():
        for index in range(group):
            lax.fori_loop(ready_ref[0, first + index], done, missed, index)

    encode(out_ref, sent_ref)


def encode(values_ref, sent_ref):
    group, times, extent = values_ref.shape
    row = lax.broadcasted_iota(jnp.int32, (times, extent), 0)
    exponents = jnp.zeros((times, extent), jnp.float32)
    for index in range(group):
        values = values_ref[index]
        largest = jnp.max(jnp.max(jnp.abs(values), axis=0, keepdims=True), axis=1, keepdims=True)
        exponent = jnp.floor(jnp.log2(jnp.maximum(largest, LEAST))) - 14.0
        steps = jnp.clip(jnp.round(values * jnp.exp2(-exponent)), -32767.0, 32767.0)
        sent_ref[index] = steps.astype(jnp.int32).astype(jnp.int16)
        exponents = jnp.where(row == index, exponent, exponents)
    sent_ref[group] = exponents.astype(jnp.int32).astype(jnp.int16)
    for plane in range(group + 1, sent_ref.shape[0]):
        sent_ref[plane] = jnp.zeros_like(sent_ref[plane])


def decoder(group, sent_ref, steps_ref):
    steps_ref[...] = jnp.exp2(sent_ref[group].astype(jnp.int32).astype(jnp.float32))

    def face_of(index):
        return sent_ref[index].astype(jnp.int32).astype(jnp.float32) * steps_ref[pl.ds(index, 1), :]

    return face_of


def running_peak(sizes):
    row = lax.broadcasted_iota(jnp.int32, sizes.shape, 0)
    step = 1
    while step < sizes.shape[0]:
        earlier = pltpu.roll(sizes, step, 0)
        sizes = jnp.maximum(sizes, jnp.where(row >= step, earlier, 0.0))
        step *= 2
    return sizes


def turned(values, turn):
    return jnp.take_along_axis(values, jnp.broadcast_to(turn, values.shape), axis=1, mode="promise_in_bounds")


def local_face(ascent, mate_ascent, stiffness, record, live):
    difference = ascent - mate_ascent
    jump = difference / (1.0 + 2.0 * stiffness)
    peak = jnp.maximum(record, running_peak(jnp.abs(jump)))
    damage = jnp.clip((peak - ONSET_JUMP) / (FAILURE_JUMP - ONSET_JUMP), 0.0, 1.0)
    effective = stiffness * (1.0 - damage)
    traction = jnp.where(live, effective * difference / (1.0 + 2.0 * effective), 0.0)
    return traction, traction - ascent


def local_first(side, partner_ref, turn_ref, own_ref, mate_ref, stiff_ref, record_ref,
                robin_ref, half_ref, pair_stiff_ref, pair_record_ref):
    group, _, extent = robin_ref.shape
    first = position(group)[side]
    for index in range(group):
        face = first + index
        lanes, here = lanes_of(face, extent), lanes_of(index, extent)
        partner = partner_ref[0, face]
        mate = jnp.maximum(partner, 0)
        turn = turn_ref[:, lanes]

        def constant(row):
            return turned(jnp.broadcast_to(mate_ref[group, pl.ds(row, 1), :], (SUBLANES, extent)), turn)[:1]

        stiffness = 0.5 * (stiff_ref[:, lanes] + constant(mate))
        record = jnp.maximum(record_ref[:, lanes], constant(group + mate))
        pair_stiff_ref[:, here] = stiffness
        pair_record_ref[:, here] = record
        traction, motion = local_face(own_ref[index], turned(mate_ref[mate], turn), stiffness, record, partner >= 0)
        robin = traction + motion
        robin_ref[index] = robin
        half_ref[index] = robin.astype(jnp.bfloat16)


def local_faces(side, partner_ref, turn_ref, own_ref, mate_ref, stiff_ref, record_ref, steps_ref):
    group, _, extent = own_ref.shape
    first = position(group)[side]
    mate_face = decoder(group, mate_ref, steps_ref)
    for index in range(group):
        face = first + index
        here = lanes_of(index, extent)
        partner = partner_ref[0, face]
        mate_ascent = turned(mate_face(jnp.maximum(partner, 0)), turn_ref[:, lanes_of(face, extent)])
        yield index, *local_face(own_ref[index], mate_ascent, stiff_ref[:, here], record_ref[:, here], partner >= 0)


def local_group(side, *refs):
    *ins, robin_ref, half_ref, steps_ref = refs
    for index, traction, motion in local_faces(side, *ins, steps_ref):
        robin = traction + motion
        robin_ref[index] = robin
        half_ref[index] = robin.astype(jnp.bfloat16)


def local_last(side, *refs):
    ins, (motion_hbm, traction_hbm, steps_ref, motion_ref, traction_ref, sems) = refs[:6], refs[-6:]
    group, _, extent = ins[2].shape
    for index, traction, motion in local_faces(side, *ins, steps_ref):
        here = lanes_of(index, extent)
        motion_ref[:, here] = motion.astype(jnp.bfloat16)
        traction_ref[:, here] = traction.astype(jnp.bfloat16)
    lanes = pl.ds(pl.multiple_of(position(group)[side] * extent, extent), group * extent)
    copies = [
        pltpu.make_async_copy(motion_ref, motion_hbm.at[:, lanes], sems.at[0]),
        pltpu.make_async_copy(traction_ref, traction_hbm.at[:, lanes], sems.at[1]),
    ]
    for copy in copies:
        copy.start()
    for copy in copies:
        copy.wait()


def shards(
    compliance,
    block_columns,
    load_response,
    starting_motion,
    start_traction,
    stiffness,
    history,
    face_partner,
    orientation,
):
    _, faces, stored, extent, _ = compliance.shape
    times = starting_motion.shape[1]
    group = faces // 2
    subs = lax.axis_size("sub")
    rows = lax.axis_size("row")
    near_pairs = [(s, s ^ 1) for s in range(subs)]
    far_pairs = []
    for s in range(subs):
        mate = s - 1 if s % 2 == 0 else s + 1
        for r in range(rows):
            there = mate * rows + r if 0 <= mate < subs else s * rows + rows - 1 - r
            far_pairs.append((s * rows + r, there))
    swap = [(r, rows - 1 - r) for r in range(rows)]

    def f32(*shape):
        return jax.ShapeDtypeStruct(shape, jnp.float32)

    def bf16(*shape):
        return jax.ShapeDtypeStruct(shape, jnp.bfloat16)

    def s32(*shape):
        return jax.ShapeDtypeStruct(shape, jnp.int32)

    def call(kernel, in_specs, out_shape, scratch=(), moved=0, out_specs=(), aliases={}):
        outs = out_shape if isinstance(out_shape, tuple) else (out_shape,)
        out_specs = out_specs or (VMEM,) * len(outs)
        return pl.pallas_call(
            kernel,
            out_shape=out_shape,
            in_specs=in_specs,
            out_specs=out_specs if isinstance(out_shape, tuple) else out_specs[0],
            scratch_shapes=scratch,
            input_output_aliases=aliases,
            compiler_params=pltpu.CompilerParams(vmem_limit_bytes=VMEM_BYTES),
            cost_estimate=pl.CostEstimate(flops=moved, bytes_accessed=moved, transcendentals=0) if moved else None,
        )

    part = (group, times, extent)
    flat = (times, faces * extent)
    block_bytes = faces * stored * extent * extent * 2
    steps = pltpu.VMEM((times, extent), jnp.float32)
    halves = pltpu.VMEM((rows * faces, times, extent), jnp.bfloat16)
    in_hbm = functools.partial(pltpu.with_memory_space_constraint, memory_space=pltpu.HBM)
    own = (start_traction[0].astype(jnp.float32) + starting_motion[0].astype(jnp.float32)).astype(jnp.bfloat16)
    other = lax.ppermute(own, "row", swap)
    blocks, load, motion, stress, stiff, record, turn, partner, *tables = call(
        fetch, [HBM] * 9,
        (pltpu.VMEM((faces, stored, extent, extent), jnp.bfloat16), bf16(*flat), bf16(*flat), bf16(*flat),
         f32(1, faces * extent), f32(1, faces * extent), s32(1, faces * extent), pltpu.SMEM((1, faces), jnp.int32),
         pltpu.SMEM((faces, 1, stored), jnp.int32), pltpu.SMEM((faces, 1, stored), jnp.int32), pltpu.SMEM((1, faces), jnp.int32)),
        [pltpu.SMEM((faces, 1, stored), jnp.int32), pltpu.SemaphoreType.DMA((8 + faces,))],
        block_bytes, (VMEM,) * 7 + (SMEM,) * 4,
    )(
        in_hbm(compliance[0]), in_hbm(load_response[0]), in_hbm(starting_motion[0]), in_hbm(start_traction[0]),
        in_hbm(stiffness), in_hbm(history), in_hbm(orientation.reshape(1, -1)),
        in_hbm(jnp.transpose(block_columns, (1, 0, 2))), in_hbm(face_partner),
    )
    in_smem = functools.partial(pltpu.with_memory_space_constraint, memory_space=pltpu.SMEM)
    partner, tables = in_smem(partner), [in_smem(table) for table in tables]

    robin, half = [None, None], [None, None]
    stiffs, records = [stiff, stiff], [record, record]
    for iteration in range(ITERS):
        begin, last = iteration == 0, iteration == ITERS - 1
        if not begin:
            other = [lax.ppermute(half[side], "row", swap) for side in range(2)]
        ascent, mates, early = [None, None], [None, None], []
        for side in range(0 if begin else 2):
            early.append(call(
                functools.partial(early_products, side), [SMEM] * 3 + [VMEM] * (3 + side) + [ANY] * side, f32(*part),
                [pltpu.VMEM((rows * faces + 1, times, extent), jnp.bfloat16)], block_bytes,
            )(*tables, blocks, *half, *other[:side], *early))
        for side, (axes, pairs) in enumerate((("sub", near_pairs), (("sub", "row"), far_pairs))):
            if begin:
                ascent[side] = sent = call(
                    functools.partial(first_section, side), [SMEM] * 2 + [VMEM] * 8,
                    f32(group + 1 + side, times, extent), [halves], 2 * block_bytes,
                )(*tables[:2], blocks, own, other, motion, stress, load, stiff, record)
            else:
                ascent[side], sent = call(
                    functools.partial(linear_section, side), [SMEM] * 3 + [VMEM] * 8,
                    (f32(*part), jax.ShapeDtypeStruct((group + 1 + side, times, extent), jnp.int16)),
                    [halves], 2 * block_bytes,
                )(*tables, blocks, *half, *other, robin[side], load, early[side])
            mates[side] = lax.ppermute(sent, axes, pairs)
        outs = ()
        for side in range(2):
            ins = (partner, turn, ascent[side], mates[side], stiffs[side], records[side])
            specs = [SMEM] + [VMEM] * 5
            if begin:
                robin[side], half[side], stiffs[side], records[side] = call(
                    functools.partial(local_first, side), specs,
                    (f32(*part), bf16(*part), f32(1, group * extent), f32(1, group * extent)),
                )(*ins)
            elif not last:
                robin[side], half[side] = call(
                    functools.partial(local_group, side), specs, (f32(*part), bf16(*part)), [steps],
                )(*ins)
            else:
                share = pltpu.VMEM((times, group * extent), jnp.bfloat16)
                outs = call(
                    functools.partial(local_last, side), specs + [HBM] * len(outs), (bf16(*flat),) * 2,
                    [steps, share, share, pltpu.SemaphoreType.DMA((2,))], 0, (HBM,) * 2, {6 + n: n for n in range(len(outs))},
                )(*ins, *outs)
    return tuple(out[None] for out in outs)


def solution(mesh):
    in_specs = (
        P("sub", "row", None, None, None),
        P("sub", "row", None),
        P("sub", None, "row"),
        P("sub", None, "row"),
        P("sub", None, "row"),
        P("sub", "row"),
        P("sub", "row"),
        P("sub", "row"),
        P("sub", "row", None),
    )
    out_specs = (P("sub", None, "row"), P("sub", None, "row"))
    return jax.shard_map(shards, mesh=mesh, in_specs=in_specs, out_specs=out_specs, check_vma=False)
```

```python
import functools

import jax
import jax.numpy as jnp
from jax import lax
from jax.experimental import pallas as pl
from jax.experimental.pallas import tpu as pltpu
from jax.sharding import PartitionSpec as P

ITERS = 3
SUBLANES = 8
LEAST = 2.0**-100
EARLY = (6, 10)
FIRST = 6
VMEM_BYTES = 24 * 2**20

ONSET_JUMP = 0.15
FAILURE_JUMP = 1.5

VMEM = pl.BlockSpec(memory_space=pltpu.VMEM)
SMEM = pl.BlockSpec(memory_space=pltpu.SMEM)
ANY = pl.BlockSpec(memory_space=pl.ANY)
HBM = pl.BlockSpec(memory_space=pltpu.HBM)


def position(group):
    near = group * (lax.axis_index("sub") % 2)
    return near, group - near, lax.axis_index("row")


def lanes_of(face, extent):
    return pl.ds(pl.multiple_of(face * extent, extent), extent)


def sort_blocks(columns_ref, order_ref, sorted_ref, own_ref, ready_ref):
    faces, _, stored = columns_ref.shape
    group = faces // 2
    near, far, mine = position(group)
    own = mine * faces
    partner = (1 - mine) * faces + near

    def sort_row(face, _):
        in_far = (face >= far) & (face < far + group)
        width = jnp.where(in_far, group, 0)
        columns = [columns_ref[face, 0, j] for j in range(stored)]
        owned = [(column >= own) & (column < own + faces) for column in columns]
        count = sum(jnp.where(here, 1, 0) for here in owned)
        front, middle, back = jnp.int32(0), count, jnp.int32(stored - 1)
        for j in range(stored):
            soon = (columns[j] >= partner) & (columns[j] < partner + width)
            place = jnp.where(owned[j], front, jnp.where(soon, middle, back))
            order_ref[face, 0, place] = j
            sorted_ref[face, 0, place] = columns[j]
            front = jnp.where(owned[j], front + 1, front)
            middle = jnp.where(soon, middle + 1, middle)
            back = jnp.where(owned[j] | soon, back, back - 1)
        own_ref[0, face] = count
        ready_ref[0, face] = middle
        return 0

    lax.fori_loop(0, faces, sort_row, 0)


def block_products(parts):
    times, extent = parts[0][0][0].shape
    zero = jnp.zeros_like(parts[0][0][1])
    depth = max(len(part) for part in parts)
    parts = [part + [(part[0][0], zero)] * (depth - len(part)) for part in parts]
    values = jnp.concatenate([jnp.concatenate([v for v, _ in part], axis=1) for part in parts], axis=0)
    blocks = jnp.concatenate([jnp.concatenate([c for _, c in part], axis=1) for part in parts], axis=0)
    product = lax.dot_general(values, blocks, (((1,), (1,)), ((), ())), preferred_element_type=jnp.float32)
    return [
        product[p * times : (p + 1) * times, p * extent : (p + 1) * extent] for p in range(len(parts))
    ]


def group_products(first, group, entries, finish):
    for index in range(0, group - 1, 2):
        pair = block_products([entries(first + index + k) for k in range(2)])
        for k in range(2):
            finish(index + k, pair[k])
    if group % 2:
        whole = entries(first + group - 1)
        cut = (len(whole) + 3) // 4 * 2
        finish(group - 1, sum(block_products([whole[:cut], whole[cut:]])))


def early_entries(half_ref, order_ref, sorted_ref, ready_ref, compliance_ref, count, face):
    ready, none = ready_ref[0, face], half_ref.shape[0] - 1
    return [
        (half_ref[jnp.where(slot < ready, sorted_ref[face, 0, slot], none)], compliance_ref[face, order_ref[face, 0, slot]])
        for slot in range(count)
    ]


def fetch(blocks_hbm, load_hbm, motion_hbm, stress_hbm, stiff_hbm, record_hbm, turn_hbm, columns_hbm, partner_hbm, half_in_ref,
          blocks_ref, load_ref, motion_ref, stress_ref, stiff_ref, record_ref, turn_ref, partner_ref,
          order_ref, sorted_ref, own_ref, ready_ref, early0_ref, early1_ref, columns_ref, half_ref, sems):
    group, _, extent = early0_ref.shape
    faces = 2 * group
    *starts, mine = position(group)
    columns_copy = pltpu.make_async_copy(columns_hbm, columns_ref, sems.at[0])
    columns_copy.start()
    rows = [[], []]
    for side in (1, 0):
        for index in range(group):
            face = starts[side] + index
            row = pltpu.make_async_copy(blocks_hbm.at[face], blocks_ref.at[face], sems.at[1 + side * group + index])
            row.start()
            rows[side].append(row)
    pairs = (
        (load_hbm, load_ref), (motion_hbm, motion_ref), (stress_hbm, stress_ref), (stiff_hbm, stiff_ref),
        (record_hbm, record_ref), (turn_hbm, turn_ref), (partner_hbm, partner_ref),
    )
    small = [pltpu.make_async_copy(source, target, sems.at[1 + faces + n]) for n, (source, target) in enumerate(pairs)]
    for copy in small:
        copy.start()
    for face in range(faces):
        half_ref[mine * faces + face] = half_in_ref[:, face * extent : (face + 1) * extent]
    none = half_ref.shape[0] - 1
    half_ref[none] = jnp.zeros_like(half_ref[none])
    columns_copy.wait()
    sort_blocks(columns_ref, order_ref, sorted_ref, own_ref, ready_ref)
    entries = functools.partial(early_entries, half_ref, order_ref, sorted_ref, own_ref, blocks_ref, FIRST)
    for side, out_ref in ((1, early1_ref), (0, early0_ref)):
        for index in range(0, group, 2):
            count = min(2, group - index)
            for row in rows[side][index : index + count]:
                row.wait()
            products = block_products([entries(starts[side] + index + k) for k in range(count)])
            for k in range(count):
                out_ref[index + k] = products[k]
    for copy in small:
        copy.wait()


def early_products(side, order_ref, sorted_ref, ready_ref, compliance_ref, own0_ref, own1_ref, *refs):
    out_ref, half_ref = refs[-2:]
    group = out_ref.shape[0]
    faces = compliance_ref.shape[0]
    *starts, mine = position(group)
    none = half_ref.shape[0] - 1
    half_ref[none] = jnp.zeros_like(half_ref[none])
    for start, ref in zip(starts, (own0_ref, own1_ref)):
        half_ref[pl.ds(mine * faces + start, group)] = ref[...]
    for ref in refs[:side]:
        half_ref[pl.ds((1 - mine) * faces + starts[0], group)] = ref[...]
    entries = functools.partial(early_entries, half_ref, order_ref, sorted_ref, ready_ref, compliance_ref, EARLY[side])

    def finish(index, product):
        out_ref[index] = product

    group_products(starts[side], group, entries, finish)


def late_products(first, done, order_ref, sorted_ref, ready_ref, compliance_ref, half_ref, finish, out_ref):
    group, stored = compliance_ref.shape[0] // 2, compliance_ref.shape[1]

    def entry(face, slot):
        return half_ref[sorted_ref[face, 0, slot]], compliance_ref[face, order_ref[face, 0, slot]]

    group_products(first, group, lambda face: [entry(face, slot) for slot in range(done, stored)], finish)

    def missed(slot, index):
        out_ref[index] -= 2.0 * block_products([[entry(first + index, slot)]])[0]
        return index

    least = ready_ref[0, first]
    for index in range(1, group):
        least = jnp.minimum(least, ready_ref[0, first + index])

    @pl.when(least < done)
    def _():
        for index in range(group):
            lax.fori_loop(ready_ref[0, first + index], done, missed, index)


def first_section(side, order_ref, sorted_ref, own_count_ref, compliance_ref, own_ref, other_ref, motion_ref, stress_ref,
                  load_ref, early_ref, stiff_ref, record_ref, out_ref, half_ref):
    faces, _, extent, _ = compliance_ref.shape
    group = faces // 2
    *starts, mine = position(group)
    first = starts[side]
    for run, ref in ((mine, own_ref), (1 - mine, other_ref)):
        for face in range(faces):
            half_ref[run * faces + face] = ref[:, face * extent : (face + 1) * extent]

    def finish(index, product):
        lanes = lanes_of(first + index, extent)
        robin = stress_ref[:, lanes].astype(jnp.float32) + motion_ref[:, lanes].astype(jnp.float32)
        response = early_ref[index] + product + load_ref[:, lanes].astype(jnp.float32)
        out_ref[index] = robin - 2.0 * response
        out_ref[group, index : index + 1] = stiff_ref[:, lanes]
        out_ref[group, group + index : group + index + 1] = record_ref[:, lanes]

    for plane in range(group, out_ref.shape[0]):
        out_ref[plane] = jnp.zeros_like(out_ref[plane])
    late_products(first, FIRST, order_ref, sorted_ref, own_count_ref, compliance_ref, half_ref, finish, out_ref)


def linear_section(side, order_ref, sorted_ref, ready_ref, compliance_ref, own0_ref, own1_ref, other0_ref, other1_ref,
                   robin_ref, load_ref, early_ref, out_ref, sent_ref, half_ref):
    group, _, extent = own0_ref.shape
    faces = compliance_ref.shape[0]
    *starts, mine = position(group)
    first = starts[side]
    for run, parts in ((mine, (own0_ref, own1_ref)), (1 - mine, (other0_ref, other1_ref))):
        for start, ref in zip(starts, parts):
            half_ref[pl.ds(run * faces + start, group)] = ref[...]

    def finish(index, product):
        response = early_ref[index] + product + load_ref[:, lanes_of(first + index, extent)].astype(jnp.float32)
        out_ref[index] = robin_ref[index] - 2.0 * response

    late_products(first, EARLY[side], order_ref, sorted_ref, ready_ref, compliance_ref, half_ref, finish, out_ref)
    encode(out_ref, sent_ref)


def encode(values_ref, sent_ref):
    group, times, extent = values_ref.shape
    row = lax.broadcasted_iota(jnp.int32, (times, extent), 0)
    exponents = jnp.zeros((times, extent), jnp.float32)
    for index in range(group):
        values = values_ref[index]
        largest = jnp.max(jnp.max(jnp.abs(values), axis=0, keepdims=True), axis=1, keepdims=True)
        exponent = jnp.floor(jnp.log2(jnp.maximum(largest, LEAST))) - 14.0
        steps = jnp.clip(jnp.round(values * jnp.exp2(-exponent)), -32767.0, 32767.0)
        sent_ref[index] = steps.astype(jnp.int32).astype(jnp.int16)
        exponents = jnp.where(row == index, exponent, exponents)
    sent_ref[group] = exponents.astype(jnp.int32).astype(jnp.int16)
    for plane in range(group + 1, sent_ref.shape[0]):
        sent_ref[plane] = jnp.zeros_like(sent_ref[plane])


def decoder(group, sent_ref, steps_ref):
    steps_ref[...] = jnp.exp2(sent_ref[group].astype(jnp.int32).astype(jnp.float32))

    def face_of(index):
        return sent_ref[index].astype(jnp.int32).astype(jnp.float32) * steps_ref[pl.ds(index, 1), :]

    return face_of


def running_peak(sizes):
    row = lax.broadcasted_iota(jnp.int32, sizes.shape, 0)
    step = 1
    while step < sizes.shape[0]:
        earlier = pltpu.roll(sizes, step, 0)
        sizes = jnp.maximum(sizes, jnp.where(row >= step, earlier, 0.0))
        step *= 2
    return sizes


def turned(values, turn):
    return jnp.take_along_axis(values, jnp.broadcast_to(turn, values.shape), axis=1, mode="promise_in_bounds")


def local_face(ascent, mate_ascent, stiffness, record, live):
    difference = ascent - mate_ascent
    jump = difference / (1.0 + 2.0 * stiffness)
    peak = jnp.maximum(record, running_peak(jnp.abs(jump)))
    damage = jnp.clip((peak - ONSET_JUMP) / (FAILURE_JUMP - ONSET_JUMP), 0.0, 1.0)
    effective = stiffness * (1.0 - damage)
    traction = jnp.where(live, effective * difference / (1.0 + 2.0 * effective), 0.0)
    return traction, traction - ascent


def local_first(side, partner_ref, turn_ref, own_ref, mate_ref, stiff_ref, record_ref,
                robin_ref, half_ref, pair_stiff_ref, pair_record_ref):
    group, _, extent = robin_ref.shape
    first = position(group)[side]
    for index in range(group):
        face = first + index
        lanes, here = lanes_of(face, extent), lanes_of(index, extent)
        partner = partner_ref[0, face]
        mate = jnp.maximum(partner, 0)
        turn = turn_ref[:, lanes]

        def constant(row):
            return turned(jnp.broadcast_to(mate_ref[group, pl.ds(row, 1), :], (SUBLANES, extent)), turn)[:1]

        stiffness = 0.5 * (stiff_ref[:, lanes] + constant(mate))
        record = jnp.maximum(record_ref[:, lanes], constant(group + mate))
        pair_stiff_ref[:, here] = stiffness
        pair_record_ref[:, here] = record
        traction, motion = local_face(own_ref[index], turned(mate_ref[mate], turn), stiffness, record, partner >= 0)
        robin = traction + motion
        robin_ref[index] = robin
        half_ref[index] = robin.astype(jnp.bfloat16)


def local_faces(side, partner_ref, turn_ref, own_ref, mate_ref, stiff_ref, record_ref, steps_ref):
    group, _, extent = own_ref.shape
    first = position(group)[side]
    mate_face = decoder(group, mate_ref, steps_ref)
    for index in range(group):
        face = first + index
        here = lanes_of(index, extent)
        partner = partner_ref[0, face]
        mate_ascent = turned(mate_face(jnp.maximum(partner, 0)), turn_ref[:, lanes_of(face, extent)])
        yield index, *local_face(own_ref[index], mate_ascent, stiff_ref[:, here], record_ref[:, here], partner >= 0)


def local_group(side, *refs):
    *ins, robin_ref, half_ref, steps_ref = refs
    for index, traction, motion in local_faces(side, *ins, steps_ref):
        robin = traction + motion
        robin_ref[index] = robin
        half_ref[index] = robin.astype(jnp.bfloat16)


def local_last(side, *refs):
    ins, near = refs[:6], refs[6:8]
    if side:
        *outs, steps_ref, motion_ref, traction_ref, sems = refs[8:]
    else:
        motion_ref, traction_ref, steps_ref = refs[6:]
    group, _, extent = ins[2].shape
    starts = position(group)[:2]

    def copies(part, sources):
        lanes = pl.ds(pl.multiple_of(starts[part] * extent, extent), group * extent)
        return [
            pltpu.make_async_copy(source, out.at[:, lanes], sems.at[2 * part + n])
            for n, (source, out) in enumerate(zip(sources, outs))
        ]

    if side:
        for copy in copies(0, near):
            copy.start()
    for index, traction, motion in local_faces(side, *ins, steps_ref):
        here = lanes_of(index, extent)
        motion_ref[:, here] = motion.astype(jnp.bfloat16)
        traction_ref[:, here] = traction.astype(jnp.bfloat16)
    if side:
        for copy in copies(1, (motion_ref, traction_ref)):
            copy.start()
        for copy in copies(0, near) + copies(1, (motion_ref, traction_ref)):
            copy.wait()


def shards(
    compliance,
    block_columns,
    load_response,
    starting_motion,
    start_traction,
    stiffness,
    history,
    face_partner,
    orientation,
):
    _, faces, stored, extent, _ = compliance.shape
    times = starting_motion.shape[1]
    group = faces // 2
    subs = lax.axis_size("sub")
    rows = lax.axis_size("row")
    near_pairs = [(s, s ^ 1) for s in range(subs)]
    far_pairs = []
    for s in range(subs):
        mate = s - 1 if s % 2 == 0 else s + 1
        for r in range(rows):
            there = mate * rows + r if 0 <= mate < subs else s * rows + rows - 1 - r
            far_pairs.append((s * rows + r, there))
    swap = [(r, rows - 1 - r) for r in range(rows)]

    def f32(*shape):
        return jax.ShapeDtypeStruct(shape, jnp.float32)

    def bf16(*shape):
        return jax.ShapeDtypeStruct(shape, jnp.bfloat16)

    def s32(*shape):
        return jax.ShapeDtypeStruct(shape, jnp.int32)

    def call(kernel, in_specs, out_shape, scratch=(), moved=0, out_specs=()):
        outs = out_shape if isinstance(out_shape, tuple) else (out_shape,)
        out_specs = out_specs or (VMEM,) * len(outs)
        return pl.pallas_call(
            kernel,
            out_shape=out_shape,
            in_specs=in_specs,
            out_specs=out_specs if isinstance(out_shape, tuple) else out_specs[0],
            scratch_shapes=scratch,
            compiler_params=pltpu.CompilerParams(vmem_limit_bytes=VMEM_BYTES),
            cost_estimate=pl.CostEstimate(flops=moved, bytes_accessed=moved, transcendentals=0) if moved else None,
        )

    part = (group, times, extent)
    flat = (times, faces * extent)
    block_bytes = faces * stored * extent * extent * 2
    steps = pltpu.VMEM((times, extent), jnp.float32)
    halves = pltpu.VMEM((rows * faces, times, extent), jnp.bfloat16)
    in_hbm = functools.partial(pltpu.with_memory_space_constraint, memory_space=pltpu.HBM)
    own = (start_traction[0].astype(jnp.float32) + starting_motion[0].astype(jnp.float32)).astype(jnp.bfloat16)
    other = lax.ppermute(own, "row", swap)
    table, counts = pltpu.SMEM((faces, 1, stored), jnp.int32), pltpu.SMEM((1, faces), jnp.int32)
    blocks, load, motion, stress, stiff, record, turn, *tables, first0, first1 = call(
        fetch, [HBM] * 9 + [VMEM],
        (pltpu.VMEM((faces, stored, extent, extent), jnp.bfloat16), bf16(*flat), bf16(*flat), bf16(*flat),
         f32(1, faces * extent), f32(1, faces * extent), s32(1, faces * extent),
         counts, table, table, counts, counts, f32(*part), f32(*part)),
        [table, pltpu.VMEM((rows * faces + 1, times, extent), jnp.bfloat16), pltpu.SemaphoreType.DMA((8 + faces,))],
        block_bytes, (VMEM,) * 7 + (SMEM,) * 5 + (VMEM,) * 2,
    )(
        in_hbm(compliance[0]), in_hbm(load_response[0]), in_hbm(starting_motion[0]), in_hbm(start_traction[0]),
        in_hbm(stiffness), in_hbm(history), in_hbm(orientation.reshape(1, -1)),
        in_hbm(jnp.transpose(block_columns, (1, 0, 2))), in_hbm(face_partner), own,
    )
    partner, order, columns, owned, ready = (pltpu.with_memory_space_constraint(value, pltpu.SMEM) for value in tables)

    robin, half = [None, None], [None, None]
    stiffs, records = [stiff, stiff], [record, record]
    for iteration in range(ITERS):
        begin, last = iteration == 0, iteration == ITERS - 1
        if not begin:
            other = [lax.ppermute(half[side], "row", swap) for side in range(2)]
        ascent, mates, early = [None, None], [None, None], []
        for side in range(0 if begin else 2):
            early.append(call(
                functools.partial(early_products, side), [SMEM] * 3 + [VMEM] * (3 + side) + [ANY] * side, f32(*part),
                [pltpu.VMEM((rows * faces + 1, times, extent), jnp.bfloat16)], block_bytes,
            )(order, columns, ready, blocks, *half, *other[:side], *early))
        for side, (axes, pairs) in enumerate((("sub", near_pairs), (("sub", "row"), far_pairs))):
            if begin:
                ascent[side] = sent = call(
                    functools.partial(first_section, side), [SMEM] * 3 + [VMEM] * 9,
                    f32(group + 1 + side, times, extent), [halves], 2 * block_bytes,
                )(order, columns, owned, blocks, own, other, motion, stress, load, (first0, first1)[side], stiff, record)
            else:
                ascent[side], sent = call(
                    functools.partial(linear_section, side), [SMEM] * 3 + [VMEM] * 8,
                    (f32(*part), jax.ShapeDtypeStruct((group + 1 + side, times, extent), jnp.int16)),
                    [halves], 2 * block_bytes,
                )(order, columns, ready, blocks, *half, *other, robin[side], load, early[side])
            mates[side] = lax.ppermute(sent, axes, pairs)
        outs = ()
        for side in range(2):
            ins = (partner, turn, ascent[side], mates[side], stiffs[side], records[side])
            specs = [SMEM] + [VMEM] * 5
            if begin:
                robin[side], half[side], stiffs[side], records[side] = call(
                    functools.partial(local_first, side), specs,
                    (f32(*part), bf16(*part), f32(1, group * extent), f32(1, group * extent)),
                )(*ins)
            elif not last:
                robin[side], half[side] = call(
                    functools.partial(local_group, side), specs, (f32(*part), bf16(*part)), [steps],
                )(*ins)
            else:
                share = (times, group * extent)
                if side:
                    outs = call(
                        functools.partial(local_last, side), specs + [VMEM] * 2, (bf16(*flat),) * 2,
                        [steps, pltpu.VMEM(share, jnp.bfloat16), pltpu.VMEM(share, jnp.bfloat16), pltpu.SemaphoreType.DMA((4,))],
                        0, (HBM,) * 2,
                    )(*ins, *outs)
                else:
                    outs = call(functools.partial(local_last, side), specs, (bf16(*share),) * 2, [steps])(*ins)
    return tuple(out[None] for out in outs)


def solution(mesh):
    in_specs = (
        P("sub", "row", None, None, None),
        P("sub", "row", None),
        P("sub", None, "row"),
        P("sub", None, "row"),
        P("sub", None, "row"),
        P("sub", "row"),
        P("sub", "row"),
        P("sub", "row"),
        P("sub", "row", None),
    )
    out_specs = (P("sub", None, "row"), P("sub", None, "row"))
    return jax.shard_map(shards, mesh=mesh, in_specs=in_specs, out_specs=out_specs, check_vma=False)
```

```python
import functools

import jax
import jax.numpy as jnp
from jax import lax
from jax.experimental import pallas as pl
from jax.experimental.pallas import tpu as pltpu
from jax.sharding import PartitionSpec as P

ITERS = 3
SUBLANES = 8
LEAST = 2.0**-100
EARLY = (6, 10)
FIRST = 6
VMEM_BYTES = 24 * 2**20

ONSET_JUMP = 0.15
FAILURE_JUMP = 1.5

VMEM = pl.BlockSpec(memory_space=pltpu.VMEM)
SMEM = pl.BlockSpec(memory_space=pltpu.SMEM)
ANY = pl.BlockSpec(memory_space=pl.ANY)
HBM = pl.BlockSpec(memory_space=pltpu.HBM)


def position(group):
    near = group * (lax.axis_index("sub") % 2)
    return near, group - near, lax.axis_index("row")


def lanes_of(face, extent):
    return pl.ds(pl.multiple_of(face * extent, extent), extent)


def sort_blocks(columns_ref, order_ref, sorted_ref, own_ref, ready_ref):
    faces, _, stored = columns_ref.shape
    group = faces // 2
    near, far, mine = position(group)
    columns = jnp.concatenate([columns_ref[face] for face in range(faces)], axis=0).astype(jnp.float32)
    row = lax.broadcasted_iota(jnp.int32, columns.shape, 0)
    lane = lax.broadcasted_iota(jnp.int32, columns.shape, 1).astype(jnp.float32)
    own = (mine * faces).astype(jnp.float32)
    partner = ((1 - mine) * faces + near).astype(jnp.float32)
    width = jnp.where((row >= far) & (row < far + group), group, 0).astype(jnp.float32)
    count = jnp.sum(jnp.where((columns >= own) & (columns < own + faces), 1.0, 0.0), axis=1, keepdims=True)
    front = jnp.zeros_like(columns)
    middle = count + front
    back = front + (stored - 1.0)
    order, placed = front, front
    for j in range(stored):
        column = jnp.broadcast_to(columns[:, j : j + 1], columns.shape)
        owned = (column >= own) & (column < own + faces)
        soon = (column >= partner) & (column < partner + width)
        there = lane == jnp.where(owned, front, jnp.where(soon, middle, back))
        order = jnp.where(there, float(j), order)
        placed = jnp.where(there, column, placed)
        front = front + jnp.where(owned, 1.0, 0.0)
        middle = middle + jnp.where(soon, 1.0, 0.0)
        back = back - jnp.where(owned | soon, 0.0, 1.0)
    for ref, values in ((order_ref, order), (sorted_ref, placed), (own_ref, front[:, :1]), (ready_ref, middle[:, :1])):
        for face in range(faces):
            ref[face] = values[face : face + 1].astype(jnp.int32)


def block_products(parts):
    times, extent = parts[0][0][0].shape
    zero = jnp.zeros_like(parts[0][0][1])
    depth = max(len(part) for part in parts)
    parts = [part + [(part[0][0], zero)] * (depth - len(part)) for part in parts]
    values = jnp.concatenate([jnp.concatenate([v for v, _ in part], axis=1) for part in parts], axis=0)
    blocks = jnp.concatenate([jnp.concatenate([c for _, c in part], axis=1) for part in parts], axis=0)
    product = lax.dot_general(values, blocks, (((1,), (1,)), ((), ())), preferred_element_type=jnp.float32)
    return [
        product[p * times : (p + 1) * times, p * extent : (p + 1) * extent] for p in range(len(parts))
    ]


def group_products(first, group, entries, finish):
    for index in range(0, group - 1, 2):
        pair = block_products([entries(first + index + k) for k in range(2)])
        for k in range(2):
            finish(index + k, pair[k])
    if group % 2:
        whole = entries(first + group - 1)
        cut = (len(whole) + 3) // 4 * 2
        finish(group - 1, sum(block_products([whole[:cut], whole[cut:]])))


def early_entries(half_ref, order_ref, sorted_ref, ready_ref, compliance_ref, count, face):
    ready, none = ready_ref[face, 0, 0], half_ref.shape[0] - 1
    return [
        (half_ref[jnp.where(slot < ready, sorted_ref[face, 0, slot], none)], compliance_ref[face, order_ref[face, 0, slot]])
        for slot in range(count)
    ]


def fetch(blocks_hbm, load_hbm, motion_hbm, stress_hbm, stiff_hbm, record_hbm, turn_hbm, columns_hbm, partner_hbm, half_in_ref,
          blocks_ref, load_ref, motion_ref, stress_ref, stiff_ref, record_ref, turn_ref, partner_ref,
          order_ref, sorted_ref, own_ref, ready_ref, early0_ref, early1_ref,
          columns_ref, order_vmem, sorted_vmem, own_vmem, ready_vmem, half_ref, sems):
    group, _, extent = early0_ref.shape
    faces = 2 * group
    *starts, mine = position(group)
    columns_copy = pltpu.make_async_copy(columns_hbm, columns_ref, sems.at[0])
    columns_copy.start()
    rows = [[], []]
    for side in (1, 0):
        for index in range(group):
            face = starts[side] + index
            row = pltpu.make_async_copy(blocks_hbm.at[face], blocks_ref.at[face], sems.at[1 + side * group + index])
            row.start()
            rows[side].append(row)
    pairs = (
        (load_hbm, load_ref), (motion_hbm, motion_ref), (stress_hbm, stress_ref), (stiff_hbm, stiff_ref),
        (record_hbm, record_ref), (turn_hbm, turn_ref), (partner_hbm, partner_ref),
    )
    small = [pltpu.make_async_copy(source, target, sems.at[1 + faces + n]) for n, (source, target) in enumerate(pairs)]
    for copy in small:
        copy.start()
    for face in range(faces):
        half_ref[mine * faces + face] = half_in_ref[:, face * extent : (face + 1) * extent]
    none = half_ref.shape[0] - 1
    half_ref[none] = jnp.zeros_like(half_ref[none])
    columns_copy.wait()
    tables = ((order_vmem, order_ref), (sorted_vmem, sorted_ref), (own_vmem, own_ref), (ready_vmem, ready_ref))
    sort_blocks(columns_ref, *(source for source, _ in tables))
    tables = [
        pltpu.make_async_copy(source, target, sems.at[1 + faces + len(pairs) + n]) for n, (source, target) in enumerate(tables)
    ]
    for copy in tables:
        copy.start()
    for copy in tables:
        copy.wait()
    entries = functools.partial(early_entries, half_ref, order_ref, sorted_ref, own_ref, blocks_ref, FIRST)
    for side, out_ref in ((1, early1_ref), (0, early0_ref)):
        for index in range(0, group, 2):
            count = min(2, group - index)
            for row in rows[side][index : index + count]:
                row.wait()
            products = block_products([entries(starts[side] + index + k) for k in range(count)])
            for k in range(count):
                out_ref[index + k] = products[k]
    for copy in small:
        copy.wait()


def early_products(side, order_ref, sorted_ref, ready_ref, compliance_ref, own0_ref, own1_ref, *refs):
    out_ref, half_ref = refs[-2:]
    group = out_ref.shape[0]
    faces = compliance_ref.shape[0]
    *starts, mine = position(group)
    none = half_ref.shape[0] - 1
    half_ref[none] = jnp.zeros_like(half_ref[none])
    for start, ref in zip(starts, (own0_ref, own1_ref)):
        half_ref[pl.ds(mine * faces + start, group)] = ref[...]
    for ref in refs[:side]:
        half_ref[pl.ds((1 - mine) * faces + starts[0], group)] = ref[...]
    entries = functools.partial(early_entries, half_ref, order_ref, sorted_ref, ready_ref, compliance_ref, EARLY[side])

    def finish(index, product):
        out_ref[index] = product

    group_products(starts[side], group, entries, finish)


def late_products(first, done, order_ref, sorted_ref, ready_ref, compliance_ref, half_ref, finish, out_ref):
    group, stored = compliance_ref.shape[0] // 2, compliance_ref.shape[1]

    def entry(face, slot):
        return half_ref[sorted_ref[face, 0, slot]], compliance_ref[face, order_ref[face, 0, slot]]

    group_products(first, group, lambda face: [entry(face, slot) for slot in range(done, stored)], finish)

    def missed(slot, index):
        out_ref[index] -= 2.0 * block_products([[entry(first + index, slot)]])[0]
        return index

    least = ready_ref[first, 0, 0]
    for index in range(1, group):
        least = jnp.minimum(least, ready_ref[first + index, 0, 0])

    @pl.when(least < done)
    def _():
        for index in range(group):
            lax.fori_loop(ready_ref[first + index, 0, 0], done, missed, index)


def first_section(side, order_ref, sorted_ref, own_count_ref, compliance_ref, own_ref, other_ref, motion_ref, stress_ref,
                  load_ref, early_ref, stiff_ref, record_ref, out_ref, half_ref):
    faces, _, extent, _ = compliance_ref.shape
    group = faces // 2
    *starts, mine = position(group)
    first = starts[side]
    for run, ref in ((mine, own_ref), (1 - mine, other_ref)):
        for face in range(faces):
            half_ref[run * faces + face] = ref[:, face * extent : (face + 1) * extent]

    def finish(index, product):
        lanes = lanes_of(first + index, extent)
        robin = stress_ref[:, lanes].astype(jnp.float32) + motion_ref[:, lanes].astype(jnp.float32)
        response = early_ref[index] + product + load_ref[:, lanes].astype(jnp.float32)
        out_ref[index] = robin - 2.0 * response
        out_ref[group, index : index + 1] = stiff_ref[:, lanes]
        out_ref[group, group + index : group + index + 1] = record_ref[:, lanes]

    for plane in range(group, out_ref.shape[0]):
        out_ref[plane] = jnp.zeros_like(out_ref[plane])
    late_products(first, FIRST, order_ref, sorted_ref, own_count_ref, compliance_ref, half_ref, finish, out_ref)


def linear_section(side, order_ref, sorted_ref, ready_ref, compliance_ref, own0_ref, own1_ref, other0_ref, other1_ref,
                   robin_ref, load_ref, early_ref, out_ref, sent_ref, half_ref):
    group, _, extent = own0_ref.shape
    faces = compliance_ref.shape[0]
    *starts, mine = position(group)
    first = starts[side]
    for run, parts in ((mine, (own0_ref, own1_ref)), (1 - mine, (other0_ref, other1_ref))):
        for start, ref in zip(starts, parts):
            half_ref[pl.ds(run * faces + start, group)] = ref[...]

    def finish(index, product):
        response = early_ref[index] + product + load_ref[:, lanes_of(first + index, extent)].astype(jnp.float32)
        out_ref[index] = robin_ref[index] - 2.0 * response

    late_products(first, EARLY[side], order_ref, sorted_ref, ready_ref, compliance_ref, half_ref, finish, out_ref)
    encode(out_ref, sent_ref)


def encode(values_ref, sent_ref):
    group, times, extent = values_ref.shape
    row = lax.broadcasted_iota(jnp.int32, (times, extent), 0)
    exponents = jnp.zeros((times, extent), jnp.float32)
    for index in range(group):
        values = values_ref[index]
        largest = jnp.max(jnp.max(jnp.abs(values), axis=0, keepdims=True), axis=1, keepdims=True)
        exponent = jnp.floor(jnp.log2(jnp.maximum(largest, LEAST))) - 14.0
        steps = jnp.clip(jnp.round(values * jnp.exp2(-exponent)), -32767.0, 32767.0)
        sent_ref[index] = steps.astype(jnp.int32).astype(jnp.int16)
        exponents = jnp.where(row == index, exponent, exponents)
    sent_ref[group] = exponents.astype(jnp.int32).astype(jnp.int16)
    for plane in range(group + 1, sent_ref.shape[0]):
        sent_ref[plane] = jnp.zeros_like(sent_ref[plane])


def decoder(group, sent_ref, steps_ref):
    steps_ref[...] = jnp.exp2(sent_ref[group].astype(jnp.int32).astype(jnp.float32))

    def face_of(index):
        return sent_ref[index].astype(jnp.int32).astype(jnp.float32) * steps_ref[pl.ds(index, 1), :]

    return face_of


def running_peak(sizes):
    row = lax.broadcasted_iota(jnp.int32, sizes.shape, 0)
    step = 1
    while step < sizes.shape[0]:
        earlier = pltpu.roll(sizes, step, 0)
        sizes = jnp.maximum(sizes, jnp.where(row >= step, earlier, 0.0))
        step *= 2
    return sizes


def turned(values, turn):
    return jnp.take_along_axis(values, jnp.broadcast_to(turn, values.shape), axis=1, mode="promise_in_bounds")


def local_face(ascent, mate_ascent, stiffness, record, live):
    difference = ascent - mate_ascent
    jump = difference / (1.0 + 2.0 * stiffness)
    peak = jnp.maximum(record, running_peak(jnp.abs(jump)))
    damage = jnp.clip((peak - ONSET_JUMP) / (FAILURE_JUMP - ONSET_JUMP), 0.0, 1.0)
    effective = stiffness * (1.0 - damage)
    traction = jnp.where(live, effective * difference / (1.0 + 2.0 * effective), 0.0)
    return traction, traction - ascent


def local_first(side, partner_ref, turn_ref, own_ref, mate_ref, stiff_ref, record_ref,
                robin_ref, half_ref, pair_stiff_ref, pair_record_ref):
    group, _, extent = robin_ref.shape
    first = position(group)[side]
    for index in range(group):
        face = first + index
        lanes, here = lanes_of(face, extent), lanes_of(index, extent)
        partner = partner_ref[0, face]
        mate = jnp.maximum(partner, 0)
        turn = turn_ref[:, lanes]

        def constant(row):
            return turned(jnp.broadcast_to(mate_ref[group, pl.ds(row, 1), :], (SUBLANES, extent)), turn)[:1]

        stiffness = 0.5 * (stiff_ref[:, lanes] + constant(mate))
        record = jnp.maximum(record_ref[:, lanes], constant(group + mate))
        pair_stiff_ref[:, here] = stiffness
        pair_record_ref[:, here] = record
        traction, motion = local_face(own_ref[index], turned(mate_ref[mate], turn), stiffness, record, partner >= 0)
        robin = traction + motion
        robin_ref[index] = robin
        half_ref[index] = robin.astype(jnp.bfloat16)


def local_faces(side, partner_ref, turn_ref, own_ref, mate_ref, stiff_ref, record_ref, steps_ref):
    group, _, extent = own_ref.shape
    first = position(group)[side]
    mate_face = decoder(group, mate_ref, steps_ref)
    for index in range(group):
        face = first + index
        here = lanes_of(index, extent)
        partner = partner_ref[0, face]
        mate_ascent = turned(mate_face(jnp.maximum(partner, 0)), turn_ref[:, lanes_of(face, extent)])
        yield index, *local_face(own_ref[index], mate_ascent, stiff_ref[:, here], record_ref[:, here], partner >= 0)


def local_group(side, *refs):
    *ins, robin_ref, half_ref, steps_ref = refs
    for index, traction, motion in local_faces(side, *ins, steps_ref):
        robin = traction + motion
        robin_ref[index] = robin
        half_ref[index] = robin.astype(jnp.bfloat16)


def local_last(side, *refs):
    ins, near = refs[:6], refs[6:8]
    if side:
        *outs, steps_ref, motion_ref, traction_ref, sems = refs[8:]
    else:
        motion_ref, traction_ref, steps_ref = refs[6:]
    group, _, extent = ins[2].shape
    starts = position(group)[:2]

    def copies(part, sources):
        lanes = pl.ds(pl.multiple_of(starts[part] * extent, extent), group * extent)
        return [
            pltpu.make_async_copy(source, out.at[:, lanes], sems.at[2 * part + n])
            for n, (source, out) in enumerate(zip(sources, outs))
        ]

    if side:
        for copy in copies(0, near):
            copy.start()
    for index, traction, motion in local_faces(side, *ins, steps_ref):
        here = lanes_of(index, extent)
        motion_ref[:, here] = motion.astype(jnp.bfloat16)
        traction_ref[:, here] = traction.astype(jnp.bfloat16)
    if side:
        for copy in copies(1, (motion_ref, traction_ref)):
            copy.start()
        for copy in copies(0, near) + copies(1, (motion_ref, traction_ref)):
            copy.wait()


def shards(
    compliance,
    block_columns,
    load_response,
    starting_motion,
    start_traction,
    stiffness,
    history,
    face_partner,
    orientation,
):
    _, faces, stored, extent, _ = compliance.shape
    times = starting_motion.shape[1]
    group = faces // 2
    subs = lax.axis_size("sub")
    rows = lax.axis_size("row")
    near_pairs = [(s, s ^ 1) for s in range(subs)]
    far_pairs = []
    for s in range(subs):
        mate = s - 1 if s % 2 == 0 else s + 1
        for r in range(rows):
            there = mate * rows + r if 0 <= mate < subs else s * rows + rows - 1 - r
            far_pairs.append((s * rows + r, there))
    swap = [(r, rows - 1 - r) for r in range(rows)]

    def f32(*shape):
        return jax.ShapeDtypeStruct(shape, jnp.float32)

    def bf16(*shape):
        return jax.ShapeDtypeStruct(shape, jnp.bfloat16)

    def s32(*shape):
        return jax.ShapeDtypeStruct(shape, jnp.int32)

    def call(kernel, in_specs, out_shape, scratch=(), moved=0, out_specs=()):
        outs = out_shape if isinstance(out_shape, tuple) else (out_shape,)
        out_specs = out_specs or (VMEM,) * len(outs)
        return pl.pallas_call(
            kernel,
            out_shape=out_shape,
            in_specs=in_specs,
            out_specs=out_specs if isinstance(out_shape, tuple) else out_specs[0],
            scratch_shapes=scratch,
            compiler_params=pltpu.CompilerParams(vmem_limit_bytes=VMEM_BYTES),
            cost_estimate=pl.CostEstimate(flops=moved, bytes_accessed=moved, transcendentals=0) if moved else None,
        )

    part = (group, times, extent)
    flat = (times, faces * extent)
    block_bytes = faces * stored * extent * extent * 2
    steps = pltpu.VMEM((times, extent), jnp.float32)
    halves = pltpu.VMEM((rows * faces, times, extent), jnp.bfloat16)
    in_hbm = functools.partial(pltpu.with_memory_space_constraint, memory_space=pltpu.HBM)
    own = (start_traction[0].astype(jnp.float32) + starting_motion[0].astype(jnp.float32)).astype(jnp.bfloat16)
    other = lax.ppermute(own, "row", swap)
    table, counts = pltpu.SMEM((faces, 1, stored), jnp.int32), pltpu.SMEM((faces, 1, 1), jnp.int32)
    tables = [pltpu.VMEM((faces, 1, width), jnp.int32) for width in (stored, stored, stored, 1, 1)]
    blocks, load, motion, stress, stiff, record, turn, *tables, first0, first1 = call(
        fetch, [HBM] * 9 + [VMEM],
        (pltpu.VMEM((faces, stored, extent, extent), jnp.bfloat16), bf16(*flat), bf16(*flat), bf16(*flat),
         f32(1, faces * extent), f32(1, faces * extent), s32(1, faces * extent),
         pltpu.SMEM((1, faces), jnp.int32), table, table, counts, counts, f32(*part), f32(*part)),
        tables + [pltpu.VMEM((rows * faces + 1, times, extent), jnp.bfloat16), pltpu.SemaphoreType.DMA((12 + faces,))],
        block_bytes, (VMEM,) * 7 + (SMEM,) * 5 + (VMEM,) * 2,
    )(
        in_hbm(compliance[0]), in_hbm(load_response[0]), in_hbm(starting_motion[0]), in_hbm(start_traction[0]),
        in_hbm(stiffness), in_hbm(history), in_hbm(orientation.reshape(1, -1)),
        in_hbm(jnp.transpose(block_columns, (1, 0, 2))), in_hbm(face_partner), own,
    )
    partner, order, columns, owned, ready = (pltpu.with_memory_space_constraint(value, pltpu.SMEM) for value in tables)

    robin, half = [None, None], [None, None]
    stiffs, records = [stiff, stiff], [record, record]
    for iteration in range(ITERS):
        begin, last = iteration == 0, iteration == ITERS - 1
        if not begin:
            other = [lax.ppermute(half[side], "row", swap) for side in range(2)]
        ascent, mates, early = [None, None], [None, None], []
        for side in range(0 if begin else 2):
            early.append(call(
                functools.partial(early_products, side), [SMEM] * 3 + [VMEM] * (3 + side) + [ANY] * side, f32(*part),
                [pltpu.VMEM((rows * faces + 1, times, extent), jnp.bfloat16)], block_bytes,
            )(order, columns, ready, blocks, *half, *other[:side], *early))
        for side, (axes, pairs) in enumerate((("sub", near_pairs), (("sub", "row"), far_pairs))):
            if begin:
                ascent[side] = sent = call(
                    functools.partial(first_section, side), [SMEM] * 3 + [VMEM] * 9,
                    f32(group + 1 + side, times, extent), [halves], 2 * block_bytes,
                )(order, columns, owned, blocks, own, other, motion, stress, load, (first0, first1)[side], stiff, record)
            else:
                ascent[side], sent = call(
                    functools.partial(linear_section, side), [SMEM] * 3 + [VMEM] * 8,
                    (f32(*part), jax.ShapeDtypeStruct((group + 1 + side, times, extent), jnp.int16)),
                    [halves], 2 * block_bytes,
                )(order, columns, ready, blocks, *half, *other, robin[side], load, early[side])
            mates[side] = lax.ppermute(sent, axes, pairs)
        outs = ()
        for side in range(2):
            ins = (partner, turn, ascent[side], mates[side], stiffs[side], records[side])
            specs = [SMEM] + [VMEM] * 5
            if begin:
                robin[side], half[side], stiffs[side], records[side] = call(
                    functools.partial(local_first, side), specs,
                    (f32(*part), bf16(*part), f32(1, group * extent), f32(1, group * extent)),
                )(*ins)
            elif not last:
                robin[side], half[side] = call(
                    functools.partial(local_group, side), specs, (f32(*part), bf16(*part)), [steps],
                )(*ins)
            else:
                share = (times, group * extent)
                if side:
                    outs = call(
                        functools.partial(local_last, side), specs + [VMEM] * 2, (bf16(*flat),) * 2,
                        [steps, pltpu.VMEM(share, jnp.bfloat16), pltpu.VMEM(share, jnp.bfloat16), pltpu.SemaphoreType.DMA((4,))],
                        0, (HBM,) * 2,
                    )(*ins, *outs)
                else:
                    outs = call(functools.partial(local_last, side), specs, (bf16(*share),) * 2, [steps])(*ins)
    return tuple(out[None] for out in outs)


def solution(mesh):
    in_specs = (
        P("sub", "row", None, None, None),
        P("sub", "row", None),
        P("sub", None, "row"),
        P("sub", None, "row"),
        P("sub", None, "row"),
        P("sub", "row"),
        P("sub", "row"),
        P("sub", "row"),
        P("sub", "row", None),
    )
    out_specs = (P("sub", None, "row"), P("sub", None, "row"))
    return jax.shard_map(shards, mesh=mesh, in_specs=in_specs, out_specs=out_specs, check_vma=False)
```

```python
import functools

import jax
import jax.numpy as jnp
from jax import lax
from jax.experimental import pallas as pl
from jax.experimental.pallas import tpu as pltpu
from jax.sharding import PartitionSpec as P

ITERS = 3
SUBLANES = 8
LEAST = 2.0**-100
EARLY = (6, 10)
VMEM_BYTES = 24 * 2**20

ONSET_JUMP = 0.15
FAILURE_JUMP = 1.5

VMEM = pl.BlockSpec(memory_space=pltpu.VMEM)
SMEM = pl.BlockSpec(memory_space=pltpu.SMEM)
ANY = pl.BlockSpec(memory_space=pl.ANY)
HBM = pl.BlockSpec(memory_space=pltpu.HBM)


def position(group):
    near = group * (lax.axis_index("sub") % 2)
    return near, group - near, lax.axis_index("row")


def lanes_of(face, extent):
    return pl.ds(pl.multiple_of(face * extent, extent), extent)


def sort_blocks(columns_ref, order_ref, sorted_ref, ready_ref):
    faces, _, stored = columns_ref.shape
    group = faces // 2
    near, far, mine = position(group)
    columns = jnp.concatenate([columns_ref[face] for face in range(faces)], axis=0).astype(jnp.float32)
    row = lax.broadcasted_iota(jnp.int32, columns.shape, 0)
    lane = lax.broadcasted_iota(jnp.int32, columns.shape, 1).astype(jnp.float32)
    own = (mine * faces).astype(jnp.float32)
    partner = ((1 - mine) * faces + near).astype(jnp.float32)
    width = jnp.where((row >= far) & (row < far + group), group, 0).astype(jnp.float32)
    front = jnp.zeros_like(columns)
    back = front + (stored - 1.0)
    order, placed = front, front
    for j in range(stored):
        column = jnp.broadcast_to(columns[:, j : j + 1], columns.shape)
        early = ((column >= own) & (column < own + faces)) | ((column >= partner) & (column < partner + width))
        there = lane == jnp.where(early, front, back)
        order = jnp.where(there, float(j), order)
        placed = jnp.where(there, column, placed)
        front = front + jnp.where(early, 1.0, 0.0)
        back = back - jnp.where(early, 0.0, 1.0)
    for ref, values in ((order_ref, order), (sorted_ref, placed), (ready_ref, front[:, :1])):
        for face in range(faces):
            ref[face] = values[face : face + 1].astype(jnp.int32)


def fetch(blocks_hbm, load_hbm, motion_hbm, stress_hbm, stiff_hbm, record_hbm, turn_hbm, columns_hbm, partner_hbm,
          blocks_ref, load_ref, motion_ref, stress_ref, stiff_ref, record_ref, turn_ref, partner_ref,
          order_ref, sorted_ref, ready_ref, columns_ref, order_vmem, sorted_vmem, ready_vmem, sems):
    pairs = [
        (columns_hbm, columns_ref), (load_hbm, load_ref), (motion_hbm, motion_ref), (stress_hbm, stress_ref),
        (stiff_hbm, stiff_ref), (record_hbm, record_ref), (turn_hbm, turn_ref), (partner_hbm, partner_ref),
    ]
    pairs += [(blocks_hbm.at[face], blocks_ref.at[face]) for face in range(blocks_hbm.shape[0])]
    pairs += [(order_vmem, order_ref), (sorted_vmem, sorted_ref), (ready_vmem, ready_ref)]
    copies = [pltpu.make_async_copy(source, target, sems.at[n]) for n, (source, target) in enumerate(pairs)]
    for copy in copies[:-3]:
        copy.start()
    copies[0].wait()
    sort_blocks(columns_ref, order_vmem, sorted_vmem, ready_vmem)
    for copy in copies[-3:]:
        copy.start()
    for copy in copies[1:]:
        copy.wait()


def block_products(parts):
    times, extent = parts[0][0][0].shape
    zero = jnp.zeros_like(parts[0][0][1])
    depth = max(len(part) for part in parts)
    parts = [part + [(part[0][0], zero)] * (depth - len(part)) for part in parts]
    values = jnp.concatenate([jnp.concatenate([v for v, _ in part], axis=1) for part in parts], axis=0)
    blocks = jnp.concatenate([jnp.concatenate([c for _, c in part], axis=1) for part in parts], axis=0)
    product = lax.dot_general(values, blocks, (((1,), (1,)), ((), ())), preferred_element_type=jnp.float32)
    return [
        product[p * times : (p + 1) * times, p * extent : (p + 1) * extent] for p in range(len(parts))
    ]


def group_products(first, group, entries, finish):
    for index in range(0, group - 1, 2):
        pair = block_products([entries(first + index + k) for k in range(2)])
        for k in range(2):
            finish(index + k, pair[k])
    if group % 2:
        whole = entries(first + group - 1)
        cut = (len(whole) + 3) // 4 * 2
        finish(group - 1, sum(block_products([whole[:cut], whole[cut:]])))


def early_products(side, order_ref, sorted_ref, ready_ref, compliance_ref, own0_ref, own1_ref, *refs):
    out_ref, half_ref = refs[-2:]
    group = out_ref.shape[0]
    faces = compliance_ref.shape[0]
    *starts, mine = position(group)
    none = half_ref.shape[0] - 1
    half_ref[none] = jnp.zeros_like(half_ref[none])
    for start, ref in zip(starts, (own0_ref, own1_ref)):
        half_ref[pl.ds(mine * faces + start, group)] = ref[...]
    for ref in refs[:side]:
        half_ref[pl.ds((1 - mine) * faces + starts[0], group)] = ref[...]

    def entries(face):
        ready = ready_ref[face, 0, 0]
        return [
            (half_ref[jnp.where(slot < ready, sorted_ref[face, 0, slot], none)], compliance_ref[face, order_ref[face, 0, slot]])
            for slot in range(EARLY[side])
        ]

    def finish(index, product):
        out_ref[index] = product

    group_products(starts[side], group, entries, finish)


def late_products(first, done, order_ref, sorted_ref, ready_ref, compliance_ref, half_ref, finish, out_ref):
    group, stored = compliance_ref.shape[0] // 2, compliance_ref.shape[1]

    def entry(face, slot):
        return half_ref[sorted_ref[face, 0, slot]], compliance_ref[face, order_ref[face, 0, slot]]

    group_products(first, group, lambda face: [entry(face, slot) for slot in range(done, stored)], finish)

    if not done:
        return

    def missed(slot, index):
        out_ref[index] -= 2.0 * block_products([[entry(first + index, slot)]])[0]
        return index

    least = ready_ref[first, 0, 0]
    for index in range(1, group):
        least = jnp.minimum(least, ready_ref[first + index, 0, 0])

    @pl.when(least < done)
    def _():
        for index in range(group):
            lax.fori_loop(ready_ref[first + index, 0, 0], done, missed, index)


def first_section(side, order_ref, sorted_ref, ready_ref, compliance_ref, own_ref, other_ref, motion_ref, stress_ref,
                  load_ref, stiff_ref, record_ref, out_ref, half_ref):
    faces, _, extent, _ = compliance_ref.shape
    group = faces // 2
    *starts, mine = position(group)
    first = starts[side]
    for run, ref in ((mine, own_ref), (1 - mine, other_ref)):
        for face in range(faces):
            half_ref[run * faces + face] = ref[:, face * extent : (face + 1) * extent]

    def finish(index, product):
        lanes = lanes_of(first + index, extent)
        robin = stress_ref[:, lanes].astype(jnp.float32) + motion_ref[:, lanes].astype(jnp.float32)
        response = product + load_ref[:, lanes].astype(jnp.float32)
        out_ref[index] = robin - 2.0 * response
        out_ref[group, index : index + 1] = stiff_ref[:, lanes]
        out_ref[group, group + index : group + index + 1] = record_ref[:, lanes]

    for plane in range(group, out_ref.shape[0]):
        out_ref[plane] = jnp.zeros_like(out_ref[plane])
    late_products(first, 0, order_ref, sorted_ref, ready_ref, compliance_ref, half_ref, finish, out_ref)


def linear_section(side, order_ref, sorted_ref, ready_ref, compliance_ref, own0_ref, own1_ref, other0_ref, other1_ref,
                   robin_ref, load_ref, early_ref, out_ref, sent_ref, half_ref):
    group, _, extent = own0_ref.shape
    faces = compliance_ref.shape[0]
    *starts, mine = position(group)
    first = starts[side]
    for run, parts in ((mine, (own0_ref, own1_ref)), (1 - mine, (other0_ref, other1_ref))):
        for start, ref in zip(starts, parts):
            half_ref[pl.ds(run * faces + start, group)] = ref[...]

    def finish(index, product):
        response = early_ref[index] + product + load_ref[:, lanes_of(first + index, extent)].astype(jnp.float32)
        out_ref[index] = robin_ref[index] - 2.0 * response

    late_products(first, EARLY[side], order_ref, sorted_ref, ready_ref, compliance_ref, half_ref, finish, out_ref)
    encode(out_ref, sent_ref)


def encode(values_ref, sent_ref):
    group, times, extent = values_ref.shape
    row = lax.broadcasted_iota(jnp.int32, (times, extent), 0)
    exponents = jnp.zeros((times, extent), jnp.float32)
    for index in range(group):
        values = values_ref[index]
        largest = jnp.max(jnp.max(jnp.abs(values), axis=0, keepdims=True), axis=1, keepdims=True)
        exponent = jnp.floor(jnp.log2(jnp.maximum(largest, LEAST))) - 14.0
        steps = jnp.clip(jnp.round(values * jnp.exp2(-exponent)), -32767.0, 32767.0)
        sent_ref[index] = steps.astype(jnp.int32).astype(jnp.int16)
        exponents = jnp.where(row == index, exponent, exponents)
    sent_ref[group] = exponents.astype(jnp.int32).astype(jnp.int16)
    for plane in range(group + 1, sent_ref.shape[0]):
        sent_ref[plane] = jnp.zeros_like(sent_ref[plane])


def decoder(group, sent_ref, steps_ref):
    steps_ref[...] = jnp.exp2(sent_ref[group].astype(jnp.int32).astype(jnp.float32))

    def face_of(index):
        return sent_ref[index].astype(jnp.int32).astype(jnp.float32) * steps_ref[pl.ds(index, 1), :]

    return face_of


def running_peak(sizes):
    row = lax.broadcasted_iota(jnp.int32, sizes.shape, 0)
    step = 1
    while step < sizes.shape[0]:
        earlier = pltpu.roll(sizes, step, 0)
        sizes = jnp.maximum(sizes, jnp.where(row >= step, earlier, 0.0))
        step *= 2
    return sizes


def turned(values, turn):
    return jnp.take_along_axis(values, jnp.broadcast_to(turn, values.shape), axis=1, mode="promise_in_bounds")


def local_face(ascent, mate_ascent, stiffness, record, live):
    difference = ascent - mate_ascent
    jump = difference / (1.0 + 2.0 * stiffness)
    peak = jnp.maximum(record, running_peak(jnp.abs(jump)))
    damage = jnp.clip((peak - ONSET_JUMP) / (FAILURE_JUMP - ONSET_JUMP), 0.0, 1.0)
    effective = stiffness * (1.0 - damage)
    traction = jnp.where(live, effective * difference / (1.0 + 2.0 * effective), 0.0)
    return traction, traction - ascent


def local_first(side, partner_ref, turn_ref, own_ref, mate_ref, stiff_ref, record_ref,
                robin_ref, half_ref, pair_stiff_ref, pair_record_ref):
    group, _, extent = robin_ref.shape
    first = position(group)[side]
    for index in range(group):
        face = first + index
        lanes, here = lanes_of(face, extent), lanes_of(index, extent)
        partner = partner_ref[0, face]
        mate = jnp.maximum(partner, 0)
        turn = turn_ref[:, lanes]

        def constant(row):
            return turned(jnp.broadcast_to(mate_ref[group, pl.ds(row, 1), :], (SUBLANES, extent)), turn)[:1]

        stiffness = 0.5 * (stiff_ref[:, lanes] + constant(mate))
        record = jnp.maximum(record_ref[:, lanes], constant(group + mate))
        pair_stiff_ref[:, here] = stiffness
        pair_record_ref[:, here] = record
        traction, motion = local_face(own_ref[index], turned(mate_ref[mate], turn), stiffness, record, partner >= 0)
        robin = traction + motion
        robin_ref[index] = robin
        half_ref[index] = robin.astype(jnp.bfloat16)


def local_faces(side, partner_ref, turn_ref, own_ref, mate_ref, stiff_ref, record_ref, steps_ref):
    group, _, extent = own_ref.shape
    first = position(group)[side]
    mate_face = decoder(group, mate_ref, steps_ref)
    for index in range(group):
        face = first + index
        here = lanes_of(index, extent)
        partner = partner_ref[0, face]
        mate_ascent = turned(mate_face(jnp.maximum(partner, 0)), turn_ref[:, lanes_of(face, extent)])
        yield index, *local_face(own_ref[index], mate_ascent, stiff_ref[:, here], record_ref[:, here], partner >= 0)


def local_group(side, *refs):
    *ins, robin_ref, half_ref, steps_ref = refs
    for index, traction, motion in local_faces(side, *ins, steps_ref):
        robin = traction + motion
        robin_ref[index] = robin
        half_ref[index] = robin.astype(jnp.bfloat16)


def local_last(side, *refs):
    ins, near = refs[:6], refs[6:8]
    if side:
        *outs, steps_ref, motion_ref, traction_ref, sems = refs[8:]
    else:
        motion_ref, traction_ref, steps_ref = refs[6:]
    group, _, extent = ins[2].shape
    starts = position(group)[:2]

    def copies(part, sources):
        lanes = pl.ds(pl.multiple_of(starts[part] * extent, extent), group * extent)
        return [
            pltpu.make_async_copy(source, out.at[:, lanes], sems.at[2 * part + n])
            for n, (source, out) in enumerate(zip(sources, outs))
        ]

    if side:
        for copy in copies(0, near):
            copy.start()
    for index, traction, motion in local_faces(side, *ins, steps_ref):
        here = lanes_of(index, extent)
        motion_ref[:, here] = motion.astype(jnp.bfloat16)
        traction_ref[:, here] = traction.astype(jnp.bfloat16)
    if side:
        for copy in copies(1, (motion_ref, traction_ref)):
            copy.start()
        for copy in copies(0, near) + copies(1, (motion_ref, traction_ref)):
            copy.wait()


def shards(
    compliance,
    block_columns,
    load_response,
    starting_motion,
    start_traction,
    stiffness,
    history,
    face_partner,
    orientation,
):
    _, faces, stored, extent, _ = compliance.shape
    times = starting_motion.shape[1]
    group = faces // 2
    subs = lax.axis_size("sub")
    rows = lax.axis_size("row")
    near_pairs = [(s, s ^ 1) for s in range(subs)]
    far_pairs = []
    for s in range(subs):
        mate = s - 1 if s % 2 == 0 else s + 1
        for r in range(rows):
            there = mate * rows + r if 0 <= mate < subs else s * rows + rows - 1 - r
            far_pairs.append((s * rows + r, there))
    swap = [(r, rows - 1 - r) for r in range(rows)]

    def f32(*shape):
        return jax.ShapeDtypeStruct(shape, jnp.float32)

    def bf16(*shape):
        return jax.ShapeDtypeStruct(shape, jnp.bfloat16)

    def s32(*shape):
        return jax.ShapeDtypeStruct(shape, jnp.int32)

    def call(kernel, in_specs, out_shape, scratch=(), moved=0, out_specs=()):
        outs = out_shape if isinstance(out_shape, tuple) else (out_shape,)
        out_specs = out_specs or (VMEM,) * len(outs)
        return pl.pallas_call(
            kernel,
            out_shape=out_shape,
            in_specs=in_specs,
            out_specs=out_specs if isinstance(out_shape, tuple) else out_specs[0],
            scratch_shapes=scratch,
            compiler_params=pltpu.CompilerParams(vmem_limit_bytes=VMEM_BYTES),
            cost_estimate=pl.CostEstimate(flops=moved, bytes_accessed=moved, transcendentals=0) if moved else None,
        )

    part = (group, times, extent)
    flat = (times, faces * extent)
    block_bytes = faces * stored * extent * extent * 2
    steps = pltpu.VMEM((times, extent), jnp.float32)
    halves = pltpu.VMEM((rows * faces, times, extent), jnp.bfloat16)
    in_hbm = functools.partial(pltpu.with_memory_space_constraint, memory_space=pltpu.HBM)
    own = (start_traction[0].astype(jnp.float32) + starting_motion[0].astype(jnp.float32)).astype(jnp.bfloat16)
    other = lax.ppermute(own, "row", swap)
    in_smem = [pltpu.SMEM((faces, 1, width), jnp.int32) for width in (stored, stored, 1)]
    in_vmem = [pltpu.VMEM((faces, 1, width), jnp.int32) for width in (stored, stored, stored, 1)]
    blocks, load, motion, stress, stiff, record, turn, *tables = call(
        fetch, [HBM] * 9,
        (pltpu.VMEM((faces, stored, extent, extent), jnp.bfloat16), bf16(*flat), bf16(*flat), bf16(*flat),
         f32(1, faces * extent), f32(1, faces * extent), s32(1, faces * extent), pltpu.SMEM((1, faces), jnp.int32), *in_smem),
        in_vmem + [pltpu.SemaphoreType.DMA((11 + faces,))],
        block_bytes, (VMEM,) * 7 + (SMEM,) * 4,
    )(
        in_hbm(compliance[0]), in_hbm(load_response[0]), in_hbm(starting_motion[0]), in_hbm(start_traction[0]),
        in_hbm(stiffness), in_hbm(history), in_hbm(orientation.reshape(1, -1)),
        in_hbm(jnp.transpose(block_columns, (1, 0, 2))), in_hbm(face_partner),
    )
    partner, order, columns, ready = (pltpu.with_memory_space_constraint(value, pltpu.SMEM) for value in tables)

    robin, half = [None, None], [None, None]
    stiffs, records = [stiff, stiff], [record, record]
    for iteration in range(ITERS):
        begin, last = iteration == 0, iteration == ITERS - 1
        if not begin:
            other = [lax.ppermute(half[side], "row", swap) for side in range(2)]
        ascent, mates, early = [None, None], [None, None], []
        for side in range(0 if begin else 2):
            early.append(call(
                functools.partial(early_products, side), [SMEM] * 3 + [VMEM] * (3 + side) + [ANY] * side, f32(*part),
                [pltpu.VMEM((rows * faces + 1, times, extent), jnp.bfloat16)], block_bytes,
            )(order, columns, ready, blocks, *half, *other[:side], *early))
        for side, (axes, pairs) in enumerate((("sub", near_pairs), (("sub", "row"), far_pairs))):
            if begin:
                ascent[side] = sent = call(
                    functools.partial(first_section, side), [SMEM] * 3 + [VMEM] * 8,
                    f32(group + 1 + side, times, extent), [halves], 2 * block_bytes,
                )(order, columns, ready, blocks, own, other, motion, stress, load, stiff, record)
            else:
                ascent[side], sent = call(
                    functools.partial(linear_section, side), [SMEM] * 3 + [VMEM] * 8,
                    (f32(*part), jax.ShapeDtypeStruct((group + 1 + side, times, extent), jnp.int16)),
                    [halves], 2 * block_bytes,
                )(order, columns, ready, blocks, *half, *other, robin[side], load, early[side])
            mates[side] = lax.ppermute(sent, axes, pairs)
        outs = ()
        for side in range(2):
            ins = (partner, turn, ascent[side], mates[side], stiffs[side], records[side])
            specs = [SMEM] + [VMEM] * 5
            if begin:
                robin[side], half[side], stiffs[side], records[side] = call(
                    functools.partial(local_first, side), specs,
                    (f32(*part), bf16(*part), f32(1, group * extent), f32(1, group * extent)),
                )(*ins)
            elif not last:
                robin[side], half[side] = call(
                    functools.partial(local_group, side), specs, (f32(*part), bf16(*part)), [steps],
                )(*ins)
            else:
                share = (times, group * extent)
                if side:
                    outs = call(
                        functools.partial(local_last, side), specs + [VMEM] * 2, (bf16(*flat),) * 2,
                        [steps, pltpu.VMEM(share, jnp.bfloat16), pltpu.VMEM(share, jnp.bfloat16), pltpu.SemaphoreType.DMA((4,))],
                        0, (HBM,) * 2,
                    )(*ins, *outs)
                else:
                    outs = call(functools.partial(local_last, side), specs, (bf16(*share),) * 2, [steps])(*ins)
    return tuple(out[None] for out in outs)


def solution(mesh):
    in_specs = (
        P("sub", "row", None, None, None),
        P("sub", "row", None),
        P("sub", None, "row"),
        P("sub", None, "row"),
        P("sub", None, "row"),
        P("sub", "row"),
        P("sub", "row"),
        P("sub", "row"),
        P("sub", "row", None),
    )
    out_specs = (P("sub", None, "row"), P("sub", None, "row"))
    return jax.shard_map(shards, mesh=mesh, in_specs=in_specs, out_specs=out_specs, check_vma=False)
```

```python
import functools

import jax
import jax.numpy as jnp
from jax import lax
from jax.experimental import pallas as pl
from jax.experimental.pallas import tpu as pltpu
from jax.sharding import PartitionSpec as P

ITERS = 3
SUBLANES = 8
LEAST = 2.0**-100
EARLY = (0, 6, 10)
VMEM_BYTES = 24 * 2**20

ONSET_JUMP = 0.15
FAILURE_JUMP = 1.5

VMEM = pl.BlockSpec(memory_space=pltpu.VMEM)
SMEM = pl.BlockSpec(memory_space=pltpu.SMEM)
ANY = pl.BlockSpec(memory_space=pl.ANY)
HBM = pl.BlockSpec(memory_space=pltpu.HBM)


def position(group):
    near = group * (lax.axis_index("sub") % 2)
    return near, group - near, lax.axis_index("row")


def lanes_of(face, extent):
    return pl.ds(pl.multiple_of(face * extent, extent), extent)


def sort_blocks(columns_ref, order_ref, sorted_ref, own_ref, ready_ref):
    faces, _, stored = columns_ref.shape
    group = faces // 2
    near, _, mine = position(group)
    columns = jnp.concatenate([columns_ref[face] for face in range(faces)], axis=0).astype(jnp.float32)
    lane = lax.broadcasted_iota(jnp.int32, columns.shape, 1).astype(jnp.float32)
    own = (mine * faces).astype(jnp.float32)
    partner = ((1 - mine) * faces + near).astype(jnp.float32)
    front = jnp.zeros_like(columns)
    middle = front + jnp.sum(jnp.where((columns >= own) & (columns < own + faces), 1.0, 0.0), axis=1, keepdims=True)
    back = front + (stored - 1.0)
    order, placed = front, front
    for j in range(stored):
        column = jnp.broadcast_to(columns[:, j : j + 1], columns.shape)
        owned = (column >= own) & (column < own + faces)
        soon = (column >= partner) & (column < partner + group)
        there = lane == jnp.where(owned, front, jnp.where(soon, middle, back))
        order = jnp.where(there, float(j), order)
        placed = jnp.where(there, column, placed)
        front = front + jnp.where(owned, 1.0, 0.0)
        middle = middle + jnp.where(soon, 1.0, 0.0)
        back = back - jnp.where(owned | soon, 0.0, 1.0)
    for ref, values in ((order_ref, order), (sorted_ref, placed), (own_ref, front[:, :1]), (ready_ref, middle[:, :1])):
        for face in range(faces):
            ref[face] = values[face : face + 1].astype(jnp.int32)


def fetch(blocks_hbm, load_hbm, motion_hbm, stress_hbm, stiff_hbm, record_hbm, turn_hbm, columns_hbm, partner_hbm,
          blocks_ref, load_ref, motion_ref, stress_ref, stiff_ref, record_ref, turn_ref, partner_ref,
          order_ref, sorted_ref, own_ref, ready_ref, columns_ref, order_vmem, sorted_vmem, own_vmem, ready_vmem, sems):
    pairs = [
        (columns_hbm, columns_ref), (load_hbm, load_ref), (motion_hbm, motion_ref), (stress_hbm, stress_ref),
        (stiff_hbm, stiff_ref), (record_hbm, record_ref), (turn_hbm, turn_ref), (partner_hbm, partner_ref),
    ]
    pairs += [(blocks_hbm.at[face], blocks_ref.at[face]) for face in range(blocks_hbm.shape[0])]
    pairs += [(order_vmem, order_ref), (sorted_vmem, sorted_ref), (own_vmem, own_ref), (ready_vmem, ready_ref)]
    copies = [pltpu.make_async_copy(source, target, sems.at[n]) for n, (source, target) in enumerate(pairs)]
    for copy in copies[:-4]:
        copy.start()
    copies[0].wait()
    sort_blocks(columns_ref, order_vmem, sorted_vmem, own_vmem, ready_vmem)
    for copy in copies[-4:]:
        copy.start()
    for copy in copies[1:]:
        copy.wait()


def block_products(parts):
    times, extent = parts[0][0][0].shape
    zero = jnp.zeros_like(parts[0][0][1])
    depth = max(len(part) for part in parts)
    parts = [part + [(part[0][0], zero)] * (depth - len(part)) for part in parts]
    values = jnp.concatenate([jnp.concatenate([v for v, _ in part], axis=1) for part in parts], axis=0)
    blocks = jnp.concatenate([jnp.concatenate([c for _, c in part], axis=1) for part in parts], axis=0)
    product = lax.dot_general(values, blocks, (((1,), (1,)), ((), ())), preferred_element_type=jnp.float32)
    return [
        product[p * times : (p + 1) * times, p * extent : (p + 1) * extent] for p in range(len(parts))
    ]


def group_products(first, group, entries, finish):
    for index in range(0, group - 1, 2):
        pair = block_products([entries(first + index + k) for k in range(2)])
        for k in range(2):
            finish(index + k, pair[k])
    if group % 2:
        whole = entries(first + group - 1)
        cut = (len(whole) + 3) // 4 * 2
        finish(group - 1, sum(block_products([whole[:cut], whole[cut:]])))


def early_products(stage, order_ref, sorted_ref, count_ref, compliance_ref, own0_ref, own1_ref, *refs):
    out_ref, half_ref = refs[-2:]
    faces = compliance_ref.shape[0]
    group = faces // 2
    *starts, mine = position(group)
    none = half_ref.shape[0] - 1
    half_ref[none] = jnp.zeros_like(half_ref[none])
    for start, ref in zip(starts, (own0_ref, own1_ref)):
        half_ref[pl.ds(mine * faces + start, group)] = ref[...]
    if stage:
        half_ref[pl.ds((1 - mine) * faces + starts[0], group)] = refs[0][...]

    def entries(face):
        count = count_ref[face, 0, 0]
        return [
            (half_ref[jnp.where(slot < count, sorted_ref[face, 0, slot], none)], compliance_ref[face, order_ref[face, 0, slot]])
            for slot in range(EARLY[stage], EARLY[stage + 1])
        ]

    for side in range(2):
        def finish(index, product):
            place = side * group + index
            out_ref[place] = refs[1][place] + product if stage else product

        group_products(starts[side], group, entries, finish)


def late_products(first, done, order_ref, sorted_ref, compliance_ref, half_ref, finish):
    group, stored = compliance_ref.shape[0] // 2, compliance_ref.shape[1]

    def entries(face):
        return [
            (half_ref[sorted_ref[face, 0, slot]], compliance_ref[face, order_ref[face, 0, slot]]) for slot in range(done, stored)
        ]

    group_products(first, group, entries, finish)


def missed_products(first, order_ref, sorted_ref, own_ref, ready_ref, compliance_ref, half_ref, out_ref):
    group = out_ref.shape[0]

    def missed(slot, index):
        face = first + index
        entry = (half_ref[sorted_ref[face, 0, slot]], compliance_ref[face, order_ref[face, 0, slot]])
        out_ref[index] -= 2.0 * block_products([[entry]])[0]
        return index

    spare = jnp.int32(0)
    for index in range(group):
        spare = jnp.minimum(spare, own_ref[first + index, 0, 0] - EARLY[1])
        spare = jnp.minimum(spare, ready_ref[first + index, 0, 0] - EARLY[2])

    @pl.when(spare < 0)
    def _():
        for index in range(group):
            lax.fori_loop(own_ref[first + index, 0, 0], EARLY[1], missed, index)
            lax.fori_loop(jnp.maximum(ready_ref[first + index, 0, 0], EARLY[1]), EARLY[2], missed, index)


def first_section(side, order_ref, sorted_ref, compliance_ref, own_ref, other_ref, motion_ref, stress_ref,
                  load_ref, stiff_ref, record_ref, out_ref, half_ref):
    faces, _, extent, _ = compliance_ref.shape
    group = faces // 2
    *starts, mine = position(group)
    first = starts[side]
    for run, ref in ((mine, own_ref), (1 - mine, other_ref)):
        for face in range(faces):
            half_ref[run * faces + face] = ref[:, face * extent : (face + 1) * extent]

    def finish(index, product):
        lanes = lanes_of(first + index, extent)
        robin = stress_ref[:, lanes].astype(jnp.float32) + motion_ref[:, lanes].astype(jnp.float32)
        response = product + load_ref[:, lanes].astype(jnp.float32)
        out_ref[index] = robin - 2.0 * response
        out_ref[group, index : index + 1] = stiff_ref[:, lanes]
        out_ref[group, group + index : group + index + 1] = record_ref[:, lanes]

    for plane in range(group, out_ref.shape[0]):
        out_ref[plane] = jnp.zeros_like(out_ref[plane])
    late_products(first, 0, order_ref, sorted_ref, compliance_ref, half_ref, finish)


def linear_section(side, order_ref, sorted_ref, count_ref, ready_ref, compliance_ref, own0_ref, own1_ref, other0_ref, other1_ref,
                   robin_ref, load_ref, early_ref, out_ref, sent_ref, half_ref):
    group, _, extent = own0_ref.shape
    faces = compliance_ref.shape[0]
    *starts, mine = position(group)
    first = starts[side]
    for run, parts in ((mine, (own0_ref, own1_ref)), (1 - mine, (other0_ref, other1_ref))):
        for start, ref in zip(starts, parts):
            half_ref[pl.ds(run * faces + start, group)] = ref[...]

    def finish(index, product):
        response = early_ref[side * group + index] + product + load_ref[:, lanes_of(first + index, extent)].astype(jnp.float32)
        out_ref[index] = robin_ref[index] - 2.0 * response

    late_products(first, EARLY[2], order_ref, sorted_ref, compliance_ref, half_ref, finish)
    missed_products(first, order_ref, sorted_ref, count_ref, ready_ref, compliance_ref, half_ref, out_ref)
    encode(out_ref, sent_ref)


def encode(values_ref, sent_ref):
    group, times, extent = values_ref.shape
    row = lax.broadcasted_iota(jnp.int32, (times, extent), 0)
    exponents = jnp.zeros((times, extent), jnp.float32)
    for index in range(group):
        values = values_ref[index]
        largest = jnp.max(jnp.max(jnp.abs(values), axis=0, keepdims=True), axis=1, keepdims=True)
        exponent = jnp.floor(jnp.log2(jnp.maximum(largest, LEAST))) - 14.0
        steps = jnp.clip(jnp.round(values * jnp.exp2(-exponent)), -32767.0, 32767.0)
        sent_ref[index] = steps.astype(jnp.int32).astype(jnp.int16)
        exponents = jnp.where(row == index, exponent, exponents)
    sent_ref[group] = exponents.astype(jnp.int32).astype(jnp.int16)
    for plane in range(group + 1, sent_ref.shape[0]):
        sent_ref[plane] = jnp.zeros_like(sent_ref[plane])


def decoder(group, sent_ref, steps_ref):
    steps_ref[...] = jnp.exp2(sent_ref[group].astype(jnp.int32).astype(jnp.float32))

    def face_of(index):
        return sent_ref[index].astype(jnp.int32).astype(jnp.float32) * steps_ref[pl.ds(index, 1), :]

    return face_of


def running_peak(sizes):
    row = lax.broadcasted_iota(jnp.int32, sizes.shape, 0)
    step = 1
    while step < sizes.shape[0]:
        earlier = pltpu.roll(sizes, step, 0)
        sizes = jnp.maximum(sizes, jnp.where(row >= step, earlier, 0.0))
        step *= 2
    return sizes


def turned(values, turn):
    return jnp.take_along_axis(values, jnp.broadcast_to(turn, values.shape), axis=1, mode="promise_in_bounds")


def local_face(ascent, mate_ascent, stiffness, record, live):
    difference = ascent - mate_ascent
    jump = difference / (1.0 + 2.0 * stiffness)
    peak = jnp.maximum(record, running_peak(jnp.abs(jump)))
    damage = jnp.clip((peak - ONSET_JUMP) / (FAILURE_JUMP - ONSET_JUMP), 0.0, 1.0)
    effective = stiffness * (1.0 - damage)
    traction = jnp.where(live, effective * difference / (1.0 + 2.0 * effective), 0.0)
    return traction, traction - ascent


def local_first(side, partner_ref, turn_ref, own_ref, mate_ref, stiff_ref, record_ref,
                robin_ref, half_ref, pair_stiff_ref, pair_record_ref):
    group, _, extent = robin_ref.shape
    first = position(group)[side]
    for index in range(group):
        face = first + index
        lanes, here = lanes_of(face, extent), lanes_of(index, extent)
        partner = partner_ref[0, face]
        mate = jnp.maximum(partner, 0)
        turn = turn_ref[:, lanes]

        def constant(row):
            return turned(jnp.broadcast_to(mate_ref[group, pl.ds(row, 1), :], (SUBLANES, extent)), turn)[:1]

        stiffness = 0.5 * (stiff_ref[:, lanes] + constant(mate))
        record = jnp.maximum(record_ref[:, lanes], constant(group + mate))
        pair_stiff_ref[:, here] = stiffness
        pair_record_ref[:, here] = record
        traction, motion = local_face(own_ref[index], turned(mate_ref[mate], turn), stiffness, record, partner >= 0)
        robin = traction + motion
        robin_ref[index] = robin
        half_ref[index] = robin.astype(jnp.bfloat16)


def local_faces(side, partner_ref, turn_ref, own_ref, mate_ref, stiff_ref, record_ref, steps_ref):
    group, _, extent = own_ref.shape
    first = position(group)[side]
    mate_face = decoder(group, mate_ref, steps_ref)
    for index in range(group):
        face = first + index
        here = lanes_of(index, extent)
        partner = partner_ref[0, face]
        mate_ascent = turned(mate_face(jnp.maximum(partner, 0)), turn_ref[:, lanes_of(face, extent)])
        yield index, *local_face(own_ref[index], mate_ascent, stiff_ref[:, here], record_ref[:, here], partner >= 0)


def local_group(side, *refs):
    *ins, robin_ref, half_ref, steps_ref = refs
    for index, traction, motion in local_faces(side, *ins, steps_ref):
        robin = traction + motion
        robin_ref[index] = robin
        half_ref[index] = robin.astype(jnp.bfloat16)


def local_last(side, *refs):
    ins, near = refs[:6], refs[6:8]
    if side:
        *outs, steps_ref, motion_ref, traction_ref, sems = refs[8:]
    else:
        motion_ref, traction_ref, steps_ref = refs[6:]
    group, _, extent = ins[2].shape
    starts = position(group)[:2]

    def copies(part, sources):
        lanes = pl.ds(pl.multiple_of(starts[part] * extent, extent), group * extent)
        return [
            pltpu.make_async_copy(source, out.at[:, lanes], sems.at[2 * part + n])
            for n, (source, out) in enumerate(zip(sources, outs))
        ]

    if side:
        for copy in copies(0, near):
            copy.start()
    for index, traction, motion in local_faces(side, *ins, steps_ref):
        here = lanes_of(index, extent)
        motion_ref[:, here] = motion.astype(jnp.bfloat16)
        traction_ref[:, here] = traction.astype(jnp.bfloat16)
    if side:
        for copy in copies(1, (motion_ref, traction_ref)):
            copy.start()
        for copy in copies(0, near) + copies(1, (motion_ref, traction_ref)):
            copy.wait()


def shards(
    compliance,
    block_columns,
    load_response,
    starting_motion,
    start_traction,
    stiffness,
    history,
    face_partner,
    orientation,
):
    _, faces, stored, extent, _ = compliance.shape
    times = starting_motion.shape[1]
    group = faces // 2
    subs = lax.axis_size("sub")
    rows = lax.axis_size("row")
    near_pairs = [(s, s ^ 1) for s in range(subs)]
    far_pairs = []
    for s in range(subs):
        mate = s - 1 if s % 2 == 0 else s + 1
        for r in range(rows):
            there = mate * rows + r if 0 <= mate < subs else s * rows + rows - 1 - r
            far_pairs.append((s * rows + r, there))
    swap = [(r, rows - 1 - r) for r in range(rows)]

    def f32(*shape):
        return jax.ShapeDtypeStruct(shape, jnp.float32)

    def bf16(*shape):
        return jax.ShapeDtypeStruct(shape, jnp.bfloat16)

    def s32(*shape):
        return jax.ShapeDtypeStruct(shape, jnp.int32)

    def call(kernel, in_specs, out_shape, scratch=(), moved=0, out_specs=()):
        outs = out_shape if isinstance(out_shape, tuple) else (out_shape,)
        out_specs = out_specs or (VMEM,) * len(outs)
        return pl.pallas_call(
            kernel,
            out_shape=out_shape,
            in_specs=in_specs,
            out_specs=out_specs if isinstance(out_shape, tuple) else out_specs[0],
            scratch_shapes=scratch,
            compiler_params=pltpu.CompilerParams(vmem_limit_bytes=VMEM_BYTES),
            cost_estimate=pl.CostEstimate(flops=moved, bytes_accessed=moved, transcendentals=0) if moved else None,
        )

    part = (group, times, extent)
    flat = (times, faces * extent)
    block_bytes = faces * stored * extent * extent * 2
    steps = pltpu.VMEM((times, extent), jnp.float32)
    halves = pltpu.VMEM((rows * faces, times, extent), jnp.bfloat16)
    in_hbm = functools.partial(pltpu.with_memory_space_constraint, memory_space=pltpu.HBM)
    own = (start_traction[0].astype(jnp.float32) + starting_motion[0].astype(jnp.float32)).astype(jnp.bfloat16)
    other = lax.ppermute(own, "row", swap)
    in_smem = [pltpu.SMEM((faces, 1, width), jnp.int32) for width in (stored, stored, 1, 1)]
    in_vmem = [pltpu.VMEM((faces, 1, width), jnp.int32) for width in (stored, stored, stored, 1, 1)]
    blocks, load, motion, stress, stiff, record, turn, *tables = call(
        fetch, [HBM] * 9,
        (pltpu.VMEM((faces, stored, extent, extent), jnp.bfloat16), bf16(*flat), bf16(*flat), bf16(*flat),
         f32(1, faces * extent), f32(1, faces * extent), s32(1, faces * extent), pltpu.SMEM((1, faces), jnp.int32), *in_smem),
        in_vmem + [pltpu.SemaphoreType.DMA((12 + faces,))],
        block_bytes, (VMEM,) * 7 + (SMEM,) * 5,
    )(
        in_hbm(compliance[0]), in_hbm(load_response[0]), in_hbm(starting_motion[0]), in_hbm(start_traction[0]),
        in_hbm(stiffness), in_hbm(history), in_hbm(orientation.reshape(1, -1)),
        in_hbm(jnp.transpose(block_columns, (1, 0, 2))), in_hbm(face_partner),
    )
    partner, order, columns, owned, ready = (pltpu.with_memory_space_constraint(value, pltpu.SMEM) for value in tables)

    robin, half = [None, None], [None, None]
    stiffs, records = [stiff, stiff], [record, record]
    for iteration in range(ITERS):
        begin, last = iteration == 0, iteration == ITERS - 1
        if not begin:
            other = [lax.ppermute(half[side], "row", swap) for side in range(2)]
        ascent, mates = [None, None], [None, None]
        early = ()
        for stage in range(0 if begin else 2):
            late = (other[0], early) if stage else ()
            early = call(
                functools.partial(early_products, stage), [SMEM] * 3 + [VMEM] * (3 + len(late)), f32(faces, times, extent),
                [pltpu.VMEM((rows * faces + 1, times, extent), jnp.bfloat16)], block_bytes,
            )(order, columns, (owned, ready)[stage], blocks, *half, *late)
        for side, (axes, pairs) in enumerate((("sub", near_pairs), (("sub", "row"), far_pairs))):
            if begin:
                ascent[side] = sent = call(
                    functools.partial(first_section, side), [SMEM] * 2 + [VMEM] * 8,
                    f32(group + 1 + side, times, extent), [halves], 2 * block_bytes,
                )(order, columns, blocks, own, other, motion, stress, load, stiff, record)
            else:
                ascent[side], sent = call(
                    functools.partial(linear_section, side), [SMEM] * 4 + [VMEM] * 8,
                    (f32(*part), jax.ShapeDtypeStruct((group + 1 + side, times, extent), jnp.int16)),
                    [halves], 2 * block_bytes,
                )(order, columns, owned, ready, blocks, *half, *other, robin[side], load, early)
            mates[side] = lax.ppermute(sent, axes, pairs)
        outs = ()
        for side in range(2):
            ins = (partner, turn, ascent[side], mates[side], stiffs[side], records[side])
            specs = [SMEM] + [VMEM] * 5
            if begin:
                robin[side], half[side], stiffs[side], records[side] = call(
                    functools.partial(local_first, side), specs,
                    (f32(*part), bf16(*part), f32(1, group * extent), f32(1, group * extent)),
                )(*ins)
            elif not last:
                robin[side], half[side] = call(
                    functools.partial(local_group, side), specs, (f32(*part), bf16(*part)), [steps],
                )(*ins)
            else:
                share = (times, group * extent)
                if side:
                    outs = call(
                        functools.partial(local_last, side), specs + [VMEM] * 2, (bf16(*flat),) * 2,
                        [steps, pltpu.VMEM(share, jnp.bfloat16), pltpu.VMEM(share, jnp.bfloat16), pltpu.SemaphoreType.DMA((4,))],
                        0, (HBM,) * 2,
                    )(*ins, *outs)
                else:
                    outs = call(functools.partial(local_last, side), specs, (bf16(*share),) * 2, [steps])(*ins)
    return tuple(out[None] for out in outs)


def solution(mesh):
    in_specs = (
        P("sub", "row", None, None, None),
        P("sub", "row", None),
        P("sub", None, "row"),
        P("sub", None, "row"),
        P("sub", None, "row"),
        P("sub", "row"),
        P("sub", "row"),
        P("sub", "row"),
        P("sub", "row", None),
    )
    out_specs = (P("sub", None, "row"), P("sub", None, "row"))
    return jax.shard_map(shards, mesh=mesh, in_specs=in_specs, out_specs=out_specs, check_vma=False)
```
